256 devices in a mesh: tiles: 64 (over x, z, core), chan: 4 (over y).
Axes of the slice: x: 4, y: 4, z: 8, core: 2. Of those that a mesh axis runs over, the one named last changes fastest.
Arguments:
- ocean_state: bfloat16 [64, 200, 32, 128], P('tiles', 'chan'), may hold values from -6 to 6
- first_weight: bfloat16 [9, 200, 200], P(None, None, 'chan'), may hold values from -0.125 to 0.125
- first_bias: float32 [200], P('chan'), may hold values from -3 to 3
- second_weight: bfloat16 [9, 200, 200], P(None, None, 'chan'), may hold values from -0.125 to 0.125
- second_bias: float32 [200], P('chan'), may hold values from -3 to 3
- wet_mask: int32 [64, 32, 128], P('tiles'), may hold values from 0 to 1
- neighbours: int32 [64, 8], P('tiles'), may hold values from -1 to 63, as said below
- fold_flags: int32 [64, 8], P('tiles'), may hold values from 0 to 1, as said below
Outputs:
- updated_state: bfloat16 [64, 200, 32, 128], P('tiles', 'chan')
The draws below stay inside these ranges and needn't reach their ends.
Inputs may be any that keep to these rules, and one draw needn't show every extreme that they name: `neighbours`: entries are patch indices or -1. A patch's N and S entries differ, its E and W entries differ and its four diagonal entries differ, where not -1. The relation is mutual: if q is the direction-k neighbour of p, p is q's neighbour in the opposite direction, or in the same direction where the entry crosses the fold. `fold_flags`: only N, NE and NW entries of patches in the northernmost row of patches may be 1, and only where the neighbour is not -1.
All inputs are finite; a program needn't handle non-finite values.
Results may differ from the reference program's by a relative error of at most 0.0033.
Values may be sent and summed in bfloat16 or wider, within the bound.
A program may use at most 128 MiB of HBM per device.

```python
import jax
import jax.numpy as jnp
import numpy as np
from jax import lax

C = 200
PROWS = 32
PCOLS = 128
BLOCK_ROWS = 3
BLOCK_COLS = 32
NPATCH = 64


def curve_position(curve_side, column, height):
    distance = 0
    step_size = curve_side // 2
    while step_size > 0:
        right_bit = 1 if column & step_size > 0 else 0
        upper_bit = 1 if height & step_size > 0 else 0
        distance += step_size * step_size * (3 * right_bit ^ upper_bit)
        if upper_bit == 0:
            if right_bit == 1:
                column = curve_side - 1 - column
                height = curve_side - 1 - height
            column, height = (height, column)
        step_size //= 2
    return distance


def patch_layout(key):
    block_count = BLOCK_COLS * BLOCK_ROWS
    curve_side = 1
    while curve_side < max(BLOCK_COLS, BLOCK_ROWS):
        curve_side *= 2
    curve_table = np.array([curve_position(curve_side, block % BLOCK_COLS, block // BLOCK_COLS) for block in range(block_count)], np.int32)
    shuffled = jax.random.permutation(jax.random.fold_in(key, 11), block_count).astype(jnp.int32)
    ocean_flags = jnp.zeros((block_count,), jnp.int32).at[shuffled[:NPATCH]].set(1)
    filler = curve_side * curve_side + jnp.arange(block_count, dtype=jnp.int32)
    scores = jnp.where(ocean_flags == 1, jnp.asarray(curve_table), filler)
    curve_order = jnp.argsort(scores, stable=True).astype(jnp.int32)
    patch_blocks = curve_order[:NPATCH]
    position = jnp.full((block_count,), -1, jnp.int32).at[patch_blocks].set(jnp.arange(NPATCH, dtype=jnp.int32))
    block_col = patch_blocks % BLOCK_COLS
    block_row = patch_blocks // BLOCK_COLS
    at_top = block_row == BLOCK_ROWS - 1
    always = block_row >= 0
    below_ok = block_row > 0

    def locate(target_col, target_row, usable):
        flat_index = jnp.clip(target_row, 0, BLOCK_ROWS - 1) * BLOCK_COLS + target_col % BLOCK_COLS
        return jnp.where(usable, position[flat_index], -1)
    north_id = jnp.where(at_top, locate(BLOCK_COLS - 1 - block_col, block_row, always), locate(block_col, block_row + 1, always))
    south_id = locate(block_col, block_row - 1, below_ok)
    east_id = locate(block_col + 1, block_row, always)
    west_id = locate(block_col - 1, block_row, always)
    north_east = jnp.where(at_top, locate(BLOCK_COLS - 2 - block_col, block_row, always), locate(block_col + 1, block_row + 1, always))
    north_west = jnp.where(at_top, locate(BLOCK_COLS - block_col, block_row, always), locate(block_col - 1, block_row + 1, always))
    south_east = locate(block_col + 1, block_row - 1, below_ok)
    south_west = locate(block_col - 1, block_row - 1, below_ok)
    neighbour_ids = jnp.stack([north_id, south_id, east_id, west_id, north_east, north_west, south_east, south_west], axis=1).astype(jnp.int32)
    nothing = jnp.zeros_like(at_top)
    fold_bits = jnp.stack([at_top & (north_id >= 0), nothing, nothing, nothing, at_top & (north_east >= 0), at_top & (north_west >= 0), nothing, nothing], axis=1).astype(jnp.int32)
    return (neighbour_ids, fold_bits)


def draw_neighbours(key, part):
    return patch_layout(key)[0]


def draw_fold_flags(key, part):
    return patch_layout(key)[1]


def draw_wet_mask(key, part):
    levels = jax.random.randint(jax.random.fold_in(key, 29), (NPATCH, PROWS, PCOLS), 0, 7)
    return (levels > 0).astype(jnp.int32)


def block_levels(key, shape, shards, smallest, largest):
    def one(dim, parts):
        draws = jax.random.uniform(jax.random.fold_in(jax.random.fold_in(key, 6), dim), (parts,), jnp.float32, smallest / len(shards), largest / len(shards))
        return jnp.repeat(jnp.exp(draws), shape[dim] // parts).reshape((-1,) + (1,) * (len(shape) - dim - 1))

    gain = one(*shards[0])
    for cut in shards[1:]:
        gain = gain * one(*cut)
    return gain


def normal_values(stream_key, shape, spread, bound, split=(), kind=jnp.bfloat16):
    values = spread * jax.random.normal(stream_key, shape, jnp.float32)
    if split:
        values = values * block_levels(stream_key, shape, split, -0.22, 0.18)
    return jnp.clip(values, -bound, bound).astype(kind)


def setup_inputs(seed: int = 0) -> dict:
    streams_of = jax.random.split(jax.random.key(seed), 9)
    return {
        "ocean_state": normal_values(streams_of[0], (NPATCH, C, PROWS, PCOLS), 1.0, 6.0, ((0, 64), (1, 4))),
        "first_weight": normal_values(streams_of[1], (9, C, C), (9 * C) ** -0.5, 0.125, ((2, 4),)),
        "first_bias": normal_values(streams_of[2], (C,), 0.5, 3.0, ((0, 4),), jnp.float32),
        "second_weight": normal_values(streams_of[3], (9, C, C), (9 * C) ** -0.5, 0.125, ((2, 4),)),
        "second_bias": normal_values(streams_of[4], (C,), 0.5, 3.0, ((0, 4),), jnp.float32),
        "wet_mask": draw_wet_mask(jax.random.fold_in(streams_of[8], 71), 0),
        "neighbours": draw_neighbours(jax.random.fold_in(streams_of[8], 71), 0),
        "fold_flags": draw_fold_flags(jax.random.fold_in(streams_of[8], 71), 0),
    }


def conv_patch(padded, weight):
    channels = padded.shape[0]
    row_count = padded.shape[1] - 2
    col_count = padded.shape[2] - 2
    running = jnp.zeros((weight.shape[2], row_count * col_count), jnp.float32)
    for tap_index in range(9):
        row_shift = tap_index // 3
        col_shift = tap_index % 3
        window = padded[:, row_shift:row_shift + row_count, col_shift:col_shift + col_count]
        window = window.reshape(channels, row_count * col_count)
        running = running + jnp.dot(weight[tap_index].T, window, preferred_element_type=jnp.float32)
    return running


def pad_patch(patches, patch_index, neighbours, fold_flags):
    row_count = patches.shape[2]
    col_count = patches.shape[3]

    def source_of(direction):
        found = neighbours[patch_index, direction]
        other = patches[jnp.maximum(found, 0)]
        usable = (found >= 0).astype(patches.dtype)
        folded = fold_flags[patch_index, direction] == 1
        return other, usable, folded

    other, usable, folded = source_of(0)
    north_strip = jnp.where(folded, other[:, row_count - 1, ::-1], other[:, 0, :]) * usable
    other, usable, folded = source_of(1)
    south_strip = other[:, row_count - 1, :] * usable
    other, usable, folded = source_of(2)
    east_strip = other[:, :, 0] * usable
    other, usable, folded = source_of(3)
    west_strip = other[:, :, col_count - 1] * usable
    other, usable, folded = source_of(4)
    north_east = jnp.where(folded, other[:, row_count - 1, col_count - 1], other[:, 0, 0]) * usable
    other, usable, folded = source_of(5)
    north_west = jnp.where(folded, other[:, row_count - 1, 0], other[:, 0, col_count - 1]) * usable
    other, usable, folded = source_of(6)
    south_east = other[:, row_count - 1, 0] * usable
    other, usable, folded = source_of(7)
    south_west = other[:, row_count - 1, col_count - 1] * usable
    middle = jnp.concatenate([west_strip[:, :, None], patches[patch_index], east_strip[:, :, None]], axis=2)
    south_row = jnp.concatenate([south_west[:, None], south_strip, south_east[:, None]], axis=1)
    north_row = jnp.concatenate([north_west[:, None], north_strip, north_east[:, None]], axis=1)
    return jnp.concatenate([south_row[:, None], middle, north_row[:, None]], axis=1)


def reference(ocean_state, first_weight, first_bias, second_weight, second_bias, wet_mask, neighbours, fold_flags):
    mask_values = wet_mask.astype(jnp.bfloat16)
    masked = ocean_state * mask_values[:, None]
    patch_ids = jnp.arange(NPATCH, dtype=jnp.int32)

    def first_layer(patch_index):
        padded = pad_patch(masked, patch_index, neighbours, fold_flags)
        before = conv_patch(padded, first_weight) + first_bias[:, None]
        mask_flat = wet_mask[patch_index].reshape(1, -1).astype(jnp.float32)
        return (mask_flat * jax.nn.gelu(before)).astype(jnp.bfloat16).reshape(C, PROWS, PCOLS)

    hidden = lax.map(first_layer, patch_ids)

    def second_layer(patch_index):
        padded = pad_patch(hidden, patch_index, neighbours, fold_flags)
        residual = ocean_state[patch_index].reshape(C, -1).astype(jnp.float32)
        mask_flat = wet_mask[patch_index].reshape(1, -1).astype(jnp.float32)
        after = mask_flat * (residual + conv_patch(padded, second_weight) + second_bias[:, None])
        return after.astype(jnp.bfloat16).reshape(C, PROWS, PCOLS)

    return lax.map(second_layer, patch_ids)
```

```python
import functools
import math

import jax
import jax.numpy as jnp
from jax import lax
from jax.experimental import pallas as pl
from jax.experimental.pallas import tpu as pltpu
from jax.sharding import PartitionSpec as P

MESH = pl.DeviceIdType.MESH
LANES = 128
SLOT = 64
PEERS = 4
X_SIZE = 4
Z_SIZE = 8


def body_kernel(
    geo,
    state,
    w1,
    b1,
    w2,
    b2,
    wet,
    nb,
    fold,
    out,
    flat,
    share,
    packed,
    packed_halo,
    taps_f,
    taps,
    rows_z,
    sums,
    ring,
    ring_z0,
    ring_z1,
    slots,
    slots_x0,
    slots_x1,
    halo,
    table_own,
    table,
    table_s,
    y_send,
    y_recv,
    h_send,
    h_recv,
    z_send,
    z_recv,
    u_send,
    u_recv,
    t_send,
    t_recv,
    local_sem,
):
    xs, zs, ch, chp, nr = geo
    us = 2 * xs
    ring_z, slots_x = (ring_z0, ring_z1), (slots_x0, slots_x1)
    pairs = nr // 2
    half = pairs // 2
    f32, bf16 = jnp.float32, jnp.bfloat16

    t = lax.axis_index("tiles")
    c = lax.axis_index("chan")
    k = lax.rem(t, 2)
    z = lax.rem(t // 2, zs)
    x = t // (2 * zs)
    u = x * 2 + k
    up = lax.rem(c + 1, PEERS)
    down = lax.rem(c + PEERS - 1, PEERS)

    def z_peer(o):
        return (x * zs + lax.rem(z + o, zs)) * 2 + k

    def u_peer(o):
        v = lax.rem(u + o, us)
        return ((v // 2) * zs + z) * 2 + lax.rem(v, 2)

    lane = lax.broadcasted_iota(jnp.int32, (chp, LANES), 1)

    barrier = pltpu.get_barrier_semaphore()
    for o in range(1, PEERS):
        pl.semaphore_signal(barrier, inc=1, device_id=(t, lax.rem(c + o, PEERS)), device_id_type=MESH)
    for o in range(1, zs):
        pl.semaphore_signal(barrier, inc=1, device_id=(z_peer(o), c), device_id_type=MESH)
    for o in range(1, us):
        pl.semaphore_signal(barrier, inc=1, device_id=(u_peer(o), c), device_id_type=MESH)

    flat[0 : ch * nr] = state[0].astype(f32).reshape(ch * nr, LANES)
    flat[ch * nr : chp * nr] = jnp.zeros(((chp - ch) * nr, LANES), f32)

    def put_row(layer, i, h, row, sides):
        r = 2 * i + h
        row16 = row.astype(bf16)
        share[layer, 0, i, :, h * LANES : (h + 1) * LANES] = row16
        sides = jnp.where(lane == 1 + r, pltpu.roll(row, r + 2, 1), sides)
        return jnp.where(lane == 65 + r, pltpu.roll(row, r + 65, 1), sides)

    def mask_row(r):
        return wet[0, pl.ds(r, 1), :].astype(f32)

    def load_pair(i, sides):
        for h in range(2):
            r = 2 * i + h
            row = flat[pl.ds(r, chp, stride=nr), :] * mask_row(r)
            sides = put_row(0, i, h, row, sides)
        return sides

    def put_ring(layer, sides):
        ring[layer, :, 0:LANES] = share[layer, 0, 0, :, 0:LANES]
        ring[layer, :, LANES : 2 * LANES] = share[layer, 0, pairs - 1, :, LANES : 2 * LANES]
        ring[layer, :, 2 * LANES : 3 * LANES] = sides.astype(bf16)

    put_ring(0, lax.fori_loop(0, pairs, load_pair, jnp.zeros((chp, LANES), f32)))
    table_own[...] = jnp.zeros((8, LANES), jnp.int32)
    table_own[0:1, 0:8] = nb[...] * 2 + fold[...]

    pl.semaphore_wait(barrier, (PEERS - 1) + (zs - 1) + (us - 1))

    def remote(src, dst, send, recv, tile, chan):
        return pltpu.make_async_remote_copy(
            src_ref=src, dst_ref=dst, send_sem=send, recv_sem=recv, device_id=(tile, chan), device_id_type=MESH
        )

    first, second = pl.ds(0, half), pl.ds(half, half)

    def y_copy(layer, n):
        src, dst, part, chan = (
            (0, 3, first, up),
            (0, 3, second, up),
            (0, 1, second, down),
            (0, 1, first, down),
            (3, 2, first, up),
            (1, 2, second, down),
        )[n]
        return remote(
            share.at[layer, src, part], share.at[layer, dst, part], y_send.at[layer, n], y_recv.at[layer, n], t, chan
        )

    def z_copy(layer, o):
        return remote(ring.at[layer], ring_z[layer].at[z], z_send.at[layer, o], z_recv.at[layer, o], z_peer(o), c)

    def u_copy(layer, o):
        return remote(
            slots.at[layer, lax.rem(u + o, us)],
            slots_x[layer].at[u],
            u_send.at[layer, o],
            u_recv.at[layer, o],
            u_peer(o),
            c,
        )

    def t_copy(o):
        return remote(table_own, table.at[u], t_send.at[o], t_recv.at[o], u_peer(o), c)

    def h_copy(layer, o):
        return remote(
            halo.at[layer, 0],
            halo.at[layer, PEERS - o],
            h_send.at[layer, o],
            h_recv.at[layer, o],
            t,
            lax.rem(c + o, PEERS),
        )

    def start_layer(layer):
        for o in range(1, zs):
            z_copy(layer, o).start()
        for n in (0, 2, 1, 3):
            y_copy(layer, n).start()

    start_layer(0)
    for o in range(1, us):
        t_copy(o).start()

    k_in = lax.broadcasted_iota(jnp.int32, (PEERS * ch, PEERS * SLOT), 0)
    k_at = lax.broadcasted_iota(jnp.int32, (PEERS * ch, PEERS * SLOT), 1)
    place = jnp.zeros((PEERS * ch, PEERS * SLOT), jnp.bool_)
    for j in range(PEERS):
        owner = lax.rem(c + j, PEERS)
        place = place | (
            (k_at - SLOT * j == k_in - ch * owner) & (k_at >= SLOT * j) & (k_at < SLOT * j + ch)
        )
    place = jnp.where(place, 1.0, 0.0).astype(bf16)
    taps_f[...] = jnp.zeros(taps_f.shape, f32)
    for layer, w in enumerate((w1, w2)):
        for tap in range(9):
            taps_f[tap * chp : tap * chp + ch, :] = lax.dot_general(
                w[tap], place, (((0,), (0,)), ((), ())), preferred_element_type=f32
            )
        taps[layer] = taps_f[...].astype(bf16)
    packed[...] = jnp.zeros(packed.shape, bf16)
    packed_halo[...] = jnp.zeros(packed_halo.shape, bf16)

    eye = lax.broadcasted_iota(jnp.int32, (chp, ch), 0) == lax.broadcasted_iota(jnp.int32, (chp, ch), 1)

    def bias_column(b):
        spread = jnp.broadcast_to(b[...], (chp, ch))
        return jnp.sum(jnp.where(eye, spread, 0.0), axis=1, keepdims=True)

    flip = jnp.where(
        lax.broadcasted_iota(jnp.int32, (LANES, LANES), 0) + lax.broadcasted_iota(jnp.int32, (LANES, LANES), 1)
        == LANES - 1,
        1.0,
        0.0,
    ).astype(bf16)

    table[u] = table_own[...]
    for o in range(1, us):
        t_copy(o).wait_recv()
    move = pltpu.make_async_copy(table, table_s, local_sem)
    move.start()
    move.wait()

    east, west = (lane >= 65) & (lane < 65 + nr), (lane >= 1) & (lane < 1 + nr)
    sides_at = slice(2 * LANES, 3 * LANES)

    def read_table(v):
        codes = [table_s[v, 0, n] for n in range(8)]
        return [code >> 1 for code in codes], [code & 1 for code in codes]

    def build_slot(layer, v):
        ids, folds = read_table(v)
        at = [lax.rem(jnp.maximum(q, 0) // 2, zs) for q in ids]
        slots[layer, v, :, 0:LANES] = ring_z[layer][at[1], :, LANES : 2 * LANES]
        plain = ring_z[layer][at[0], :, 0:LANES]
        folded = ring_z[layer][at[0], :, LANES : 2 * LANES]
        slots[layer, v, :, LANES : 2 * LANES] = jnp.where(folds[0] == 1, folded, plain)

        def sides(n):
            return ring_z[layer][at[n], :, sides_at].astype(f32)

        result = jnp.where(east, sides(2), sides(3))
        result = jnp.where(lane == 65 + nr, corner_top(sides(4), folds[4]), result)
        result = jnp.where(lane == 1 + nr, corner_top(sides(5), folds[5]), result)
        result = jnp.where(lane == 64, pltpu.roll(sides(6), LANES - nr, 1), result)
        result = jnp.where(lane == 0, pltpu.roll(sides(7), LANES - nr, 1), result)
        slots[layer, v, :, sides_at] = result.astype(bf16)

    def corner_top(v, is_fold):
        return jnp.where(is_fold == 1, pltpu.roll(v, 65, 1), pltpu.roll(v, nr, 1))

    def merge(layer):
        ids, folds = read_table(u)
        at = [(jnp.maximum(q, 0) // (2 * zs)) * 2 + lax.rem(jnp.maximum(q, 0), 2) for q in ids]

        def usable(n, value):
            return jnp.where(ids[n] >= 0, value, jnp.zeros_like(value))

        halo[layer, 0, :, 0:LANES] = usable(1, slots_x[layer][at[1], :, 0:LANES])
        north = slots_x[layer][at[0], :, LANES : 2 * LANES]
        turned = jnp.dot(north, flip, preferred_element_type=f32).astype(bf16)
        halo[layer, 0, :, LANES : 2 * LANES] = usable(0, jnp.where(folds[0] == 1, turned, north))

        def sides(n):
            return usable(n, slots_x[layer][at[n], :, sides_at].astype(f32))

        result = jnp.where(east, sides(2), 0.0)
        result = jnp.where(west, sides(3), result)
        result = jnp.where(lane == 65 + nr, sides(4), result)
        result = jnp.where(lane == 1 + nr, sides(5), result)
        result = jnp.where(lane == 64, sides(6), result)
        result = jnp.where(lane == 0, sides(7), result)
        halo[layer, 0, :, sides_at] = result.astype(bf16)

    def exchange(layer):
        y_copy(layer, 0).wait_recv()
        y_copy(layer, 4).start()
        y_copy(layer, 2).wait_recv()
        y_copy(layer, 5).start()
        ring_z[layer][z] = ring[layer]
        for o in range(1, zs):
            z_copy(layer, o).wait_recv()

        def one_slot(v, carry):
            build_slot(layer, v)
            return carry

        lax.fori_loop(0, us, one_slot, 0)
        for o in range(1, us):
            u_copy(layer, o).start()
        slots_x[layer][u] = slots[layer, u]
        for o in range(1, us):
            u_copy(layer, o).wait_recv()
        merge(layer)
        for o in range(1, PEERS):
            h_copy(layer, o).start()

    def tap_rows(tap):
        return slice(tap * chp, (tap + 1) * chp)

    def row_sum(r):
        total = []
        for b in range(3):
            total.append(
                rows_z[r, tap_rows(b), :] + rows_z[r + 1, tap_rows(3 + b), :] + rows_z[r + 2, tap_rows(6 + b), :]
            )
        left = jnp.where(lane == 0, 0.0, pltpu.roll(total[0], 1, 1))
        right = jnp.where(lane == LANES - 1, 0.0, pltpu.roll(total[2], LANES - 1, 1))
        return total[1] + left + right

    def conv(layer):
        for n in (1, 3, 4, 5):
            y_copy(layer, n).wait_recv()

        def one_pair(i, carry):
            for j in range(PEERS):
                packed[i, j * SLOT : j * SLOT + chp, :] = share[layer, j, i]
            both = jnp.dot(taps[layer], packed[i], preferred_element_type=f32)
            rows_z[2 * i + 1] = both[:, 0:LANES]
            rows_z[2 * i + 2] = both[:, LANES : 2 * LANES]
            return carry

        lax.fori_loop(0, pairs, one_pair, 0)

        def inner_row(r, carry):
            sums[r] = row_sum(r)
            return carry

        lax.fori_loop(1, nr - 1, inner_row, 0)
        for o in range(1, PEERS):
            h_copy(layer, o).wait_recv()
        for j in range(PEERS):
            packed_halo[j * SLOT : j * SLOT + chp, :] = halo[layer, j]
        frame = jnp.dot(taps[layer], packed_halo[...], preferred_element_type=f32)
        rows_z[0] = frame[:, 0:LANES]
        rows_z[nr + 1] = frame[:, LANES : 2 * LANES]
        sums[0] = row_sum(0)
        sums[nr - 1] = row_sum(nr - 1)
        side = frame[:, sides_at]
        to_west = pltpu.roll(side[tap_rows(0)], 1, 1) + side[tap_rows(3)] + pltpu.roll(side[tap_rows(6)], LANES - 1, 1)
        to_east = pltpu.roll(side[tap_rows(2)], 1, 1) + side[tap_rows(5)] + pltpu.roll(side[tap_rows(8)], LANES - 1, 1)
        return to_west, to_east

    def full_row(r, to_west, to_east):
        edge = jnp.where(lane == 0, pltpu.roll(to_west, LANES - 1 - r, 1), 0.0)
        edge = jnp.where(lane == LANES - 1, pltpu.roll(to_east, 62 - r, 1), edge)
        return sums[r] + edge

    exchange(0)
    to_west, to_east = conv(0)
    bias = bias_column(b1)

    def hidden_pair(i, sides):
        for h in range(2):
            r = 2 * i + h
            v = full_row(r, to_west, to_east) + bias
            v = 0.5 * v * (1.0 + jnp.tanh(math.sqrt(2.0 / math.pi) * (v + 0.044715 * (v * v * v))))
            sides = put_row(1, i, h, v * mask_row(r), sides)
        return sides

    put_ring(1, lax.fori_loop(0, pairs, hidden_pair, jnp.zeros((chp, LANES), f32)))
    start_layer(1)

    exchange(1)
    to_west, to_east = conv(1)
    bias = bias_column(b2)

    def final_pair(i, carry):
        for h in range(2):
            r = 2 * i + h
            own = share[0, 0, i, :, h * LANES : (h + 1) * LANES].astype(f32)
            v = own + full_row(r, to_west, to_east) + bias
            flat[pl.ds(r, chp, stride=nr), :] = v * mask_row(r)
        return carry

    lax.fori_loop(0, pairs, final_pair, 0)
    out[0] = flat[0 : ch * nr].reshape(ch, nr, LANES).astype(bf16)

    for o in range(1, us):
        t_copy(o).wait_send()
    for layer in range(2):
        for n in range(6):
            y_copy(layer, n).wait_send()
        for o in range(1, zs):
            z_copy(layer, o).wait_send()
        for o in range(1, us):
            u_copy(layer, o).wait_send()
        for o in range(1, PEERS):
            h_copy(layer, o).wait_send()


def build(mesh, xs, zs):
    us = 2 * xs

    def body(state, w1, b1, w2, b2, wet, nb, fold):
        ch, nr = state.shape[1], state.shape[2]
        chp = -(-ch // 8) * 8
        pairs = nr // 2
        f32, bf16 = jnp.float32, jnp.bfloat16
        vmem, dma = pltpu.VMEM, pltpu.SemaphoreType.DMA
        inside = pl.BlockSpec(memory_space=pltpu.VMEM)
        return pl.pallas_call(
            functools.partial(body_kernel, (xs, zs, ch, chp, nr)),
            out_shape=jax.ShapeDtypeStruct(state.shape, bf16),
            in_specs=[inside] * 8,
            out_specs=inside,
            scratch_shapes=[
                vmem((chp * nr, LANES), f32),
                vmem((2, PEERS, pairs, chp, 2 * LANES), bf16),
                vmem((pairs, PEERS * SLOT, 2 * LANES), bf16),
                vmem((PEERS * SLOT, 3 * LANES), bf16),
                vmem((9 * chp, PEERS * SLOT), f32),
                vmem((2, 9 * chp, PEERS * SLOT), bf16),
                vmem((nr + 2, 9 * chp, LANES), f32),
                vmem((nr, chp, LANES), f32),
                vmem((2, chp, 3 * LANES), bf16),
                vmem((zs, chp, 3 * LANES), bf16),
                vmem((zs, chp, 3 * LANES), bf16),
                vmem((2, us, chp, 3 * LANES), bf16),
                vmem((us, chp, 3 * LANES), bf16),
                vmem((us, chp, 3 * LANES), bf16),
                vmem((2, PEERS, chp, 3 * LANES), bf16),
                vmem((8, LANES), jnp.int32),
                vmem((us, 8, LANES), jnp.int32),
                pltpu.SMEM((us, 8, LANES), jnp.int32),
                dma((2, 6)),
                dma((2, 6)),
                dma((2, PEERS)),
                dma((2, PEERS)),
                dma((2, zs)),
                dma((2, zs)),
                dma((2, us)),
                dma((2, us)),
                dma((us,)),
                dma((us,)),
                dma,
            ],
            compiler_params=pltpu.CompilerParams(
                collective_id=0, has_side_effects=True, vmem_limit_bytes=48 * 1024 * 1024
            ),
        )(state, w1, b1.reshape(1, -1), w2, b2.reshape(1, -1), wet, nb, fold)

    return jax.shard_map(
        body,
        mesh=mesh,
        in_specs=(
            P("tiles", "chan", None, None),
            P(None, None, "chan"),
            P("chan"),
            P(None, None, "chan"),
            P("chan"),
            P("tiles", None, None),
            P("tiles", None),
            P("tiles", None),
        ),
        out_specs=P("tiles", "chan", None, None),
        check_vma=False,
    )


def solution(mesh):
    return build(mesh, X_SIZE, Z_SIZE)
```

```python
import functools
import math

import jax
import jax.numpy as jnp
from jax import lax
from jax.experimental import pallas as pl
from jax.experimental.pallas import tpu as pltpu
from jax.sharding import PartitionSpec as P

MESH = pl.DeviceIdType.MESH
LANES = 128
SLOT = 64
PEERS = 4
X_SIZE = 4
Z_SIZE = 8
CHUNKS = 4


def body_kernel(
    geo,
    state,
    w1,
    b1,
    w2,
    b2,
    wet,
    nb,
    fold,
    out,
    flat,
    share,
    grid,
    sides_k,
    taps_f,
    taps,
    sums,
    ring,
    ring_z0,
    ring_z1,
    slots,
    slots_x0,
    slots_x1,
    halo,
    table_own,
    table,
    table_s,
    y_send,
    y_recv,
    h_send,
    h_recv,
    z_send,
    z_recv,
    u_send,
    u_recv,
    t_send,
    t_recv,
    local_sem,
):
    xs, zs, ch, chp, nr = geo
    us = 2 * xs
    ring_z, slots_x = (ring_z0, ring_z1), (slots_x0, slots_x1)
    pairs = nr // 2
    part = pairs // CHUNKS
    rows_of = 2 * part
    depth = PEERS * SLOT
    f32, bf16 = jnp.float32, jnp.bfloat16

    t = lax.axis_index("tiles")
    c = lax.axis_index("chan")
    k = lax.rem(t, 2)
    z = lax.rem(t // 2, zs)
    x = t // (2 * zs)
    u = x * 2 + k
    up = lax.rem(c + 1, PEERS)
    down = lax.rem(c + PEERS - 1, PEERS)

    def z_peer(o):
        return (x * zs + lax.rem(z + o, zs)) * 2 + k

    def u_peer(o):
        v = lax.rem(u + o, us)
        return ((v // 2) * zs + z) * 2 + lax.rem(v, 2)

    lane = lax.broadcasted_iota(jnp.int32, (chp, LANES), 1)

    barrier = pltpu.get_barrier_semaphore()
    for o in range(1, PEERS):
        pl.semaphore_signal(barrier, inc=1, device_id=(t, lax.rem(c + o, PEERS)), device_id_type=MESH)
    for o in range(1, zs):
        pl.semaphore_signal(barrier, inc=1, device_id=(z_peer(o), c), device_id_type=MESH)
    for o in range(1, us):
        pl.semaphore_signal(barrier, inc=1, device_id=(u_peer(o), c), device_id_type=MESH)

    def remote(src, dst, send, recv, tile, chan):
        return pltpu.make_async_remote_copy(
            src_ref=src, dst_ref=dst, send_sem=send, recv_sem=recv, device_id=(tile, chan), device_id_type=MESH
        )

    def y_copy(layer, n, q):
        src, dst, chan = ((0, 3, up), (0, 1, down), (3, 2, up), (1, 2, down))[n]
        at = (pl.ds(q * part, part),) + (() if n < 2 else (n - 2,))
        return remote(
            share.at[(layer, src) + at],
            share.at[(layer, dst) + at],
            y_send.at[layer, n, q],
            y_recv.at[layer, n, q],
            t,
            chan,
        )

    def z_copy(layer, o):
        return remote(ring.at[layer], ring_z[layer].at[z], z_send.at[layer, o], z_recv.at[layer, o], z_peer(o), c)

    def u_copy(layer, o):
        return remote(
            slots.at[layer, lax.rem(u + o, us)],
            slots_x[layer].at[u],
            u_send.at[layer, o],
            u_recv.at[layer, o],
            u_peer(o),
            c,
        )

    def t_copy(o):
        return remote(table_own, table.at[u], t_send.at[o], t_recv.at[o], u_peer(o), c)

    def h_copy(layer, o):
        return remote(
            halo.at[layer, 0],
            halo.at[layer, PEERS - o],
            h_send.at[layer, o],
            h_recv.at[layer, o],
            t,
            lax.rem(c + o, PEERS),
        )

    flat[0 : ch * nr] = state[0].astype(f32).reshape(ch * nr, LANES)
    flat[ch * nr : chp * nr] = jnp.zeros(((chp - ch) * nr, LANES), f32)
    grid[...] = jnp.zeros(grid.shape, bf16)
    sides_k[...] = jnp.zeros(sides_k.shape, f32)

    def put_row(layer, i, h, row, sides):
        r = 2 * i + h
        row16 = row.astype(bf16)
        share[layer, 0, i, h] = row16
        grid[r + 1, 0:chp, :] = row16
        sides = jnp.where(lane == 1 + r, pltpu.roll(row, r + 2, 1), sides)
        return jnp.where(lane == 65 + r, pltpu.roll(row, r + 65, 1), sides)

    def mask_row(r):
        return wet[0, pl.ds(r, 1), :].astype(f32)

    def load_chunk(q, sides):
        for i in range(part):
            for h in range(2):
                r = 2 * (q * part + i) + h
                row = flat[pl.ds(r, chp, stride=nr), :] * mask_row(r)
                sides = put_row(0, q * part + i, h, row, sides)
        return sides

    def put_ring(layer, sides):
        ring[layer, :, 0:LANES] = share[layer, 0, 0, 0]
        ring[layer, :, LANES : 2 * LANES] = share[layer, 0, pairs - 1, 1]
        ring[layer, :, 2 * LANES : 3 * LANES] = sides.astype(bf16)

    def send_own(layer, q):
        for n in range(2):
            y_copy(layer, n, q).start()

    def send_ring(layer):
        for o in range(1, zs):
            z_copy(layer, o).start()

    put_ring(0, lax.fori_loop(0, CHUNKS, load_chunk, jnp.zeros((chp, LANES), f32)))
    table_own[...] = jnp.zeros((8, LANES), jnp.int32)
    table_own[0:1, 0:8] = nb[...] * 2 + fold[...]

    pl.semaphore_wait(barrier, (PEERS - 1) + (zs - 1) + (us - 1))
    send_ring(0)
    for q in range(2):
        send_own(0, q)
    for o in range(1, us):
        t_copy(o).start()

    k_in = lax.broadcasted_iota(jnp.int32, (PEERS * ch, depth), 0)
    k_at = lax.broadcasted_iota(jnp.int32, (PEERS * ch, depth), 1)
    place = jnp.zeros((PEERS * ch, depth), jnp.bool_)
    for j in range(PEERS):
        owner = lax.rem(c + j, PEERS)
        place = place | ((k_at - SLOT * j == k_in - ch * owner) & (k_at >= SLOT * j) & (k_at < SLOT * j + ch))
    place = jnp.where(place, 1.0, 0.0).astype(bf16)
    taps_f[...] = jnp.zeros(taps_f.shape, f32)
    for layer, w in enumerate((w1, w2)):
        for a in range(3):
            for b in range(3):
                taps_f[b * chp : b * chp + ch, a * depth : (a + 1) * depth] = jnp.dot(
                    w[3 * a + b], place, preferred_element_type=f32
                )
        taps[layer] = taps_f[...].astype(bf16)

    eye = lax.broadcasted_iota(jnp.int32, (chp, ch), 0) == lax.broadcasted_iota(jnp.int32, (chp, ch), 1)

    def bias_column(b):
        spread = jnp.broadcast_to(b[...], (chp, ch))
        return jnp.sum(jnp.where(eye, spread, 0.0), axis=1, keepdims=True)

    biases = bias_column(b1), bias_column(b2)
    flip = jnp.where(
        lax.broadcasted_iota(jnp.int32, (LANES, LANES), 0) + lax.broadcasted_iota(jnp.int32, (LANES, LANES), 1)
        == LANES - 1,
        1.0,
        0.0,
    ).astype(bf16)

    table[u] = table_own[...]
    for o in range(1, us):
        t_copy(o).wait_recv()
    move = pltpu.make_async_copy(table, table_s, local_sem)
    move.start()
    move.wait()

    east, west = (lane >= 65) & (lane < 65 + nr), (lane >= 1) & (lane < 1 + nr)
    sides_at = slice(2 * LANES, 3 * LANES)

    def read_table(v):
        codes = [table_s[v, 0, n] for n in range(8)]
        return [code >> 1 for code in codes], [code & 1 for code in codes]

    def build_slot(layer, v):
        ids, folds = read_table(v)
        at = [lax.rem(jnp.maximum(q, 0) // 2, zs) for q in ids]
        slots[layer, v, :, 0:LANES] = ring_z[layer][at[1], :, LANES : 2 * LANES]
        plain = ring_z[layer][at[0], :, 0:LANES]
        folded = ring_z[layer][at[0], :, LANES : 2 * LANES]
        slots[layer, v, :, LANES : 2 * LANES] = jnp.where(folds[0] == 1, folded, plain)

        def sides(n):
            return ring_z[layer][at[n], :, sides_at].astype(f32)

        def corner_top(n):
            v = sides(n)
            return jnp.where(folds[n] == 1, pltpu.roll(v, 65, 1), pltpu.roll(v, nr, 1))

        result = jnp.where(east, sides(2), sides(3))
        result = jnp.where(lane == 65 + nr, corner_top(4), result)
        result = jnp.where(lane == 1 + nr, corner_top(5), result)
        result = jnp.where(lane == 64, pltpu.roll(sides(6), LANES - nr, 1), result)
        result = jnp.where(lane == 0, pltpu.roll(sides(7), LANES - nr, 1), result)
        slots[layer, v, :, sides_at] = result.astype(bf16)

    def merge(layer):
        ids, folds = read_table(u)
        at = [(jnp.maximum(q, 0) // (2 * zs)) * 2 + lax.rem(jnp.maximum(q, 0), 2) for q in ids]

        def usable(n, value):
            return jnp.where(ids[n] >= 0, value, jnp.zeros_like(value))

        halo[layer, 0, :, 0:LANES] = usable(1, slots_x[layer][at[1], :, 0:LANES])
        north = slots_x[layer][at[0], :, LANES : 2 * LANES]
        turned = jnp.dot(north, flip, preferred_element_type=f32).astype(bf16)
        halo[layer, 0, :, LANES : 2 * LANES] = usable(0, jnp.where(folds[0] == 1, turned, north))

        def sides(n):
            return usable(n, slots_x[layer][at[n], :, sides_at].astype(f32))

        result = jnp.where(east, sides(2), 0.0)
        result = jnp.where(west, sides(3), result)
        result = jnp.where(lane == 65 + nr, sides(4), result)
        result = jnp.where(lane == 1 + nr, sides(5), result)
        result = jnp.where(lane == 64, sides(6), result)
        result = jnp.where(lane == 0, sides(7), result)
        halo[layer, 0, :, sides_at] = result.astype(bf16)

    def gather(layer, q):
        for n in range(2):
            y_copy(layer, n, q).wait_recv()
            y_copy(layer, n + 2, q).start()
        if q + 2 < CHUNKS:
            send_own(layer, q + 2)

    def conv_rows(layer, columns):
        stacked = jnp.concatenate(
            [jnp.concatenate([column[a] for column in columns], axis=1) for a in range(3)], axis=0
        )
        return jnp.dot(taps[layer], stacked, preferred_element_type=f32)

    def add_columns(total):
        left = jnp.where(lane == 0, 0.0, pltpu.roll(total[0:chp], 1, 1))
        right = jnp.where(lane == LANES - 1, 0.0, pltpu.roll(total[2 * chp : 3 * chp], LANES - 1, 1))
        return total[chp : 2 * chp] + left + right

    def conv_chunk(layer, q, low, count):
        for n in range(2, 4):
            y_copy(layer, n, q).wait_recv()

        def pack(i, carry):
            for h in range(2):
                for j in range(1, PEERS):
                    grid[1 + 2 * i + h, j * SLOT : j * SLOT + chp, :] = share[layer, j, i, h]
            return carry

        lax.fori_loop(q * part, (q + 1) * part, pack, 0)
        total = conv_rows(layer, [[grid[low + n + a] for a in range(3)] for n in range(count)])
        for n in range(count):
            sums[low + n] = add_columns(total[:, n * LANES : (n + 1) * LANES])

    def layer_sums(layer):
        gather(layer, 0)
        gather(layer, 1)
        ring_z[layer][z] = ring[layer]
        for o in range(1, zs):
            z_copy(layer, o).wait_recv()

        def one_slot(v, carry):
            build_slot(layer, v)
            return carry

        lax.fori_loop(0, us, one_slot, 0)
        for o in range(1, us):
            u_copy(layer, o).start()
        slots_x[layer][u] = slots[layer, u]
        gather(layer, 2)
        conv_chunk(layer, 0, 1, rows_of - 2)
        gather(layer, 3)
        for o in range(1, us):
            u_copy(layer, o).wait_recv()
        merge(layer)
        for o in range(1, PEERS):
            h_copy(layer, o).start()
        for q in range(1, CHUNKS):
            conv_chunk(layer, q, q * rows_of - 1, rows_of)
        for o in range(1, PEERS):
            h_copy(layer, o).wait_recv()
        for j in range(PEERS):
            block = slice(j * SLOT, j * SLOT + chp)
            grid[0, block, :] = halo[layer, j, :, 0:LANES]
            grid[nr + 1, block, :] = halo[layer, j, :, LANES : 2 * LANES]
            sides_k[block, :] = halo[layer, j, :, sides_at].astype(f32)
        column = [pltpu.roll(sides_k[...], shift, 1).astype(bf16) if shift else sides_k[...].astype(bf16) for shift in (1, 0, LANES - 1)]
        total = conv_rows(layer, [[grid[r + a] for a in range(3)] for r in (0, nr - 1)] + [column])
        sums[0] = add_columns(total[:, 0:LANES])
        sums[nr - 1] = add_columns(total[:, LANES : 2 * LANES])
        return total[0:chp, sides_at], total[2 * chp : 3 * chp, sides_at]

    def full_row(r, to_west, to_east):
        edge = jnp.where(lane == 0, pltpu.roll(to_west, LANES - 1 - r, 1), 0.0)
        edge = jnp.where(lane == LANES - 1, pltpu.roll(to_east, 62 - r, 1), edge)
        return sums[r] + edge

    to_west, to_east = layer_sums(0)

    def hidden_chunk(q, sides):
        for i in range(part):
            for h in range(2):
                r = 2 * (q * part + i) + h
                v = full_row(r, to_west, to_east) + biases[0]
                v = 0.5 * v * (1.0 + jnp.tanh(math.sqrt(2.0 / math.pi) * (v + 0.044715 * (v * v * v))))
                sides = put_row(1, q * part + i, h, v * mask_row(r), sides)
        return sides

    def hidden_and_send(q, sides):
        sides = hidden_chunk(q, sides)
        send_own(1, q)
        return sides

    sides = lax.fori_loop(0, 2, hidden_and_send, jnp.zeros((chp, LANES), f32))
    put_ring(1, lax.fori_loop(2, CHUNKS, hidden_chunk, sides))
    send_ring(1)

    to_west, to_east = layer_sums(1)

    def final_chunk(q, carry):
        for i in range(part):
            for h in range(2):
                r = 2 * (q * part + i) + h
                own = share[0, 0, q * part + i, h].astype(f32)
                v = own + full_row(r, to_west, to_east) + biases[1]
                flat[pl.ds(r, chp, stride=nr), :] = v * mask_row(r)
        return carry

    lax.fori_loop(0, CHUNKS, final_chunk, 0)
    out[0] = flat[0 : ch * nr].reshape(ch, nr, LANES).astype(bf16)

    for o in range(1, us):
        t_copy(o).wait_send()
    for layer in range(2):
        for n in range(4):
            for q in range(CHUNKS):
                y_copy(layer, n, q).wait_send()
        for o in range(1, zs):
            z_copy(layer, o).wait_send()
        for o in range(1, us):
            u_copy(layer, o).wait_send()
        for o in range(1, PEERS):
            h_copy(layer, o).wait_send()


def build(mesh, xs, zs):
    us = 2 * xs

    def body(state, w1, b1, w2, b2, wet, nb, fold):
        ch, nr = state.shape[1], state.shape[2]
        chp = -(-ch // 8) * 8
        pairs = nr // 2
        f32, bf16 = jnp.float32, jnp.bfloat16
        vmem, dma = pltpu.VMEM, pltpu.SemaphoreType.DMA
        inside = pl.BlockSpec(memory_space=pltpu.VMEM)
        return pl.pallas_call(
            functools.partial(body_kernel, (xs, zs, ch, chp, nr)),
            out_shape=jax.ShapeDtypeStruct(state.shape, bf16),
            in_specs=[inside] * 8,
            out_specs=inside,
            scratch_shapes=[
                vmem((chp * nr, LANES), f32),
                vmem((2, PEERS, pairs, 2, chp, LANES), bf16),
                vmem((nr + 2, PEERS * SLOT, LANES), bf16),
                vmem((PEERS * SLOT, LANES), f32),
                vmem((3 * chp, 3 * PEERS * SLOT), f32),
                vmem((2, 3 * chp, 3 * PEERS * SLOT), bf16),
                vmem((nr, chp, LANES), f32),
                vmem((2, chp, 3 * LANES), bf16),
                vmem((zs, chp, 3 * LANES), bf16),
                vmem((zs, chp, 3 * LANES), bf16),
                vmem((2, us, chp, 3 * LANES), bf16),
                vmem((us, chp, 3 * LANES), bf16),
                vmem((us, chp, 3 * LANES), bf16),
                vmem((2, PEERS, chp, 3 * LANES), bf16),
                vmem((8, LANES), jnp.int32),
                vmem((us, 8, LANES), jnp.int32),
                pltpu.SMEM((us, 8, LANES), jnp.int32),
                dma((2, 4, CHUNKS)),
                dma((2, 4, CHUNKS)),
                dma((2, PEERS)),
                dma((2, PEERS)),
                dma((2, zs)),
                dma((2, zs)),
                dma((2, us)),
                dma((2, us)),
                dma((us,)),
                dma((us,)),
                dma,
            ],
            compiler_params=pltpu.CompilerParams(
                collective_id=0, has_side_effects=True, vmem_limit_bytes=48 * 1024 * 1024
            ),
        )(
            state,
            jnp.swapaxes(w1, 1, 2),
            b1.reshape(1, -1),
            jnp.swapaxes(w2, 1, 2),
            b2.reshape(1, -1),
            wet,
            nb,
            fold,
        )

    return jax.shard_map(
        body,
        mesh=mesh,
        in_specs=(
            P("tiles", "chan", None, None),
            P(None, None, "chan"),
            P("chan"),
            P(None, None, "chan"),
            P("chan"),
            P("tiles", None, None),
            P("tiles", None),
            P("tiles", None),
        ),
        out_specs=P("tiles", "chan", None, None),
        check_vma=False,
    )


def solution(mesh):
    return build(mesh, X_SIZE, Z_SIZE)
```

```python
import functools
import math

import jax
import jax.numpy as jnp
from jax import lax
from jax.experimental import pallas as pl
from jax.experimental.pallas import tpu as pltpu
from jax.sharding import PartitionSpec as P

MESH = pl.DeviceIdType.MESH
LANES = 128
SLOT = 64
PEERS = 4
X_SIZE = 4
Z_SIZE = 8
CHUNKS = 4


def body_kernel(
    geo,
    state_at,
    w1_at,
    b1_at,
    w2_at,
    b2_at,
    wet_at,
    nb_at,
    fold_at,
    out,
    state,
    w1,
    b1,
    w2,
    b2,
    wet,
    nb,
    fold,
    flat,
    share,
    grid,
    sides_k,
    taps_f,
    taps,
    sums,
    ring_z0,
    ring_z1,
    slots,
    slots_x0,
    slots_x1,
    halo,
    table_own,
    table,
    table_s,
    y_send,
    y_recv,
    h_send,
    h_recv,
    z_send,
    z_recv,
    s_send,
    s_recv,
    u_send,
    u_recv,
    t_send,
    t_recv,
    local_sem,
):
    xs, zs, ch, chp, nr = geo
    ring_z, slots_x = (ring_z0, ring_z1), (slots_x0, slots_x1)
    pairs = nr // 2
    part = pairs // CHUNKS
    rows_of = 2 * part
    depth = PEERS * SLOT
    f32, bf16 = jnp.float32, jnp.bfloat16

    t = lax.axis_index("tiles")
    c = lax.axis_index("chan")
    k = lax.rem(t, 2)
    z = lax.rem(t // 2, zs)
    x = t // (2 * zs)
    me = z * 2 + k
    up = lax.rem(c + 1, PEERS)
    down = lax.rem(c + PEERS - 1, PEERS)

    def along_z(o):
        return lax.rem(z + o + zs, zs) * 2 + k

    def z_peer(o):
        return x * zs * 2 + along_z(o)

    def x_peer(o):
        return lax.rem(x + o, xs) * zs * 2 + me

    sibling = t + 1 - 2 * k
    copies = [
        pltpu.make_async_copy(src, dst, local_sem.at[n])
        for n, (src, dst) in enumerate(
            (
                (state_at, state),
                (wet_at, wet),
                (nb_at, nb),
                (fold_at, fold),
                (w1_at, w1),
                (w2_at, w2),
                (b1_at, b1),
                (b2_at, b2),
            )
        )
    ]
    for copy in copies:
        copy.start()
    lane = lax.broadcasted_iota(jnp.int32, (chp, LANES), 1)

    barrier = pltpu.get_barrier_semaphore()
    for o in range(1, PEERS):
        pl.semaphore_signal(barrier, inc=1, device_id=(t, lax.rem(c + o, PEERS)), device_id_type=MESH)
    tiles = [z_peer(o) for o in (2, -2, 1, -1)] + [x_peer(o) for o in range(1, xs)] + [sibling]
    for tile in tiles:
        pl.semaphore_signal(barrier, inc=1, device_id=(tile, c), device_id_type=MESH)

    def remote(src, dst, send, recv, tile, chan):
        return pltpu.make_async_remote_copy(
            src_ref=src, dst_ref=dst, send_sem=send, recv_sem=recv, device_id=(tile, chan), device_id_type=MESH
        )

    def y_copy(layer, n, q):
        src, dst, chan = ((0, 3, up), (0, 1, down), (3, 2, up), (1, 2, down))[n]
        at = (pl.ds(q * part, part),) + (() if n < 2 else (n - 2,))
        return remote(
            share.at[(layer, src) + at],
            share.at[(layer, dst) + at],
            y_send.at[layer, n, q],
            y_recv.at[layer, n, q],
            t,
            chan,
        )

    def z_copy(layer, n):
        origin, target, tiles_of = (
            (0, 2, None),
            (0, -2, None),
            (0, 1, None),
            (0, -1, None),
            (-2, 1, None),
            (2, -1, None),
            (-2, 2, pl.ds(0, 2)),
            (2, -2, pl.ds(2, 1)),
        )[n]
        at = (along_z(origin),) + (() if tiles_of is None else (tiles_of,))
        return remote(
            ring_z[layer].at[at], ring_z[layer].at[at], z_send.at[layer, n], z_recv.at[layer, n], z_peer(target), c
        )

    def s_copy(layer, o, mine=True):
        at = along_z(o) if mine else along_z(o) + 1 - 2 * k
        return remote(ring_z[layer].at[at], ring_z[layer].at[at], s_send.at[layer, o], s_recv.at[layer, o], sibling, c)

    def u_copy(layer, o):
        return remote(
            slots.at[layer, lax.rem(x + o, xs)],
            slots_x[layer].at[x],
            u_send.at[layer, o],
            u_recv.at[layer, o],
            x_peer(o),
            c,
        )

    def t_copy(o):
        return remote(table_own, table.at[x], t_send.at[o], t_recv.at[o], x_peer(o), c)

    def h_copy(layer, o):
        return remote(
            halo.at[layer, 0],
            halo.at[layer, PEERS - o],
            h_send.at[layer, o],
            h_recv.at[layer, o],
            t,
            lax.rem(c + o, PEERS),
        )

    grid[...] = jnp.zeros(grid.shape, bf16)
    sides_k[...] = jnp.zeros(sides_k.shape, f32)
    table_own[...] = jnp.zeros((8, LANES), jnp.int32)
    for n in range(4):
        copies[n].wait()
    table_own[0:1, 0:8] = nb[...] * 2 + fold[...]
    flat[0 : ch * nr] = state[0].astype(f32).reshape(ch * nr, LANES)
    flat[ch * nr : chp * nr] = jnp.zeros(((chp - ch) * nr, LANES), f32)

    def put_row(layer, i, h, row, sides):
        r = 2 * i + h
        row16 = row[0:ch].astype(bf16)
        share[layer, 0, i, h] = row16
        grid[r + 1, 0:ch, :] = row16
        sides = jnp.where(lane == 1 + r, pltpu.roll(row, r + 2, 1), sides)
        return jnp.where(lane == 65 + r, pltpu.roll(row, r + 65, 1), sides)

    def mask_row(r):
        return wet[0, pl.ds(r, 1), :].astype(f32)

    def load_chunk(q, sides):
        for i in range(part):
            for h in range(2):
                r = 2 * (q * part + i) + h
                row = flat[pl.ds(r, chp, stride=nr), :] * mask_row(r)
                sides = put_row(0, q * part + i, h, row, sides)
        return sides

    def put_ring(layer, sides):
        ring_z[layer][me, 0] = share[layer, 0, 0, 0]
        ring_z[layer][me, 1] = share[layer, 0, pairs - 1, 1]
        ring_z[layer][me, 2] = sides[0:ch].astype(bf16)

    def send_own(layer, q):
        for n in range(2):
            y_copy(layer, n, q).start()

    def send_ring(layer):
        for n in range(4):
            z_copy(layer, n).start()
        s_copy(layer, 0).start()

    put_ring(0, lax.fori_loop(0, CHUNKS, load_chunk, jnp.zeros((chp, LANES), f32)))
    pl.semaphore_wait(barrier, PEERS - 1 + len(tiles))
    send_ring(0)
    for q in range(2):
        send_own(0, q)
    for o in range(1, xs):
        t_copy(o).start()

    k_in = lax.broadcasted_iota(jnp.int32, (PEERS * ch, depth), 0)
    k_at = lax.broadcasted_iota(jnp.int32, (PEERS * ch, depth), 1)
    place = jnp.zeros((PEERS * ch, depth), jnp.bool_)
    for j in range(PEERS):
        owner = lax.rem(c + j, PEERS)
        place = place | ((k_at - SLOT * j == k_in - ch * owner) & (k_at >= SLOT * j) & (k_at < SLOT * j + ch))
    place = jnp.where(place, 1.0, 0.0).astype(bf16)
    taps_f[...] = jnp.zeros(taps_f.shape, f32)
    for n in range(4, 8):
        copies[n].wait()
    for layer, w in enumerate((w1, w2)):
        for a in range(3):
            for b in range(3):
                taps_f[b * chp : b * chp + ch, a * depth : (a + 1) * depth] = jnp.dot(
                    w[3 * a + b], place, preferred_element_type=f32
                )
        taps[layer] = taps_f[...].astype(bf16)

    eye = lax.broadcasted_iota(jnp.int32, (chp, ch), 0) == lax.broadcasted_iota(jnp.int32, (chp, ch), 1)

    def bias_column(b):
        spread = jnp.broadcast_to(b[...], (chp, ch))
        return jnp.sum(jnp.where(eye, spread, 0.0), axis=1, keepdims=True)

    biases = bias_column(b1), bias_column(b2)
    flip = jnp.where(
        lax.broadcasted_iota(jnp.int32, (LANES, LANES), 0) + lax.broadcasted_iota(jnp.int32, (LANES, LANES), 1)
        == LANES - 1,
        1.0,
        0.0,
    ).astype(bf16)

    table[x] = table_own[...]
    for o in range(1, xs):
        t_copy(o).wait_recv()
    move = pltpu.make_async_copy(table, table_s, local_sem.at[8])
    move.start()
    move.wait()

    lane_ch = lax.broadcasted_iota(jnp.int32, (ch, LANES), 1)
    east = (lane_ch >= 65) & (lane_ch < 65 + nr)
    west = (lane_ch >= 1) & (lane_ch < 1 + nr)

    def read_table(v):
        codes = [table_s[v, 0, n] for n in range(8)]
        return [code >> 1 for code in codes], [code & 1 for code in codes]

    def build_slot(layer, v):
        ids, folds = read_table(v)
        at = [lax.rem(jnp.maximum(q, 0), 2 * zs) for q in ids]
        slots[layer, v, 0] = ring_z[layer][at[1], 1]
        slots[layer, v, 1] = jnp.where(folds[0] == 1, ring_z[layer][at[0], 1], ring_z[layer][at[0], 0])

        def sides(n):
            return ring_z[layer][at[n], 2].astype(f32)

        def corner_top(n):
            v = sides(n)
            return jnp.where(folds[n] == 1, pltpu.roll(v, 65, 1), pltpu.roll(v, nr, 1))

        result = jnp.where(east, sides(2), sides(3))
        result = jnp.where(lane_ch == 65 + nr, corner_top(4), result)
        result = jnp.where(lane_ch == 1 + nr, corner_top(5), result)
        result = jnp.where(lane_ch == 64, pltpu.roll(sides(6), LANES - nr, 1), result)
        result = jnp.where(lane_ch == 0, pltpu.roll(sides(7), LANES - nr, 1), result)
        slots[layer, v, 2] = result.astype(bf16)

    def merge(layer):
        ids, folds = read_table(x)
        at = [jnp.maximum(q, 0) // (2 * zs) for q in ids]

        def usable(n, value):
            return jnp.where(ids[n] >= 0, value, jnp.zeros_like(value))

        halo[layer, 0, 0] = usable(1, slots_x[layer][at[1], 0])
        north = slots_x[layer][at[0], 1]
        turned = jnp.dot(north, flip, preferred_element_type=f32).astype(bf16)
        halo[layer, 0, 1] = usable(0, jnp.where(folds[0] == 1, turned, north))

        def sides(n):
            return usable(n, slots_x[layer][at[n], 2].astype(f32))

        result = jnp.where(east, sides(2), 0.0)
        result = jnp.where(west, sides(3), result)
        result = jnp.where(lane_ch == 65 + nr, sides(4), result)
        result = jnp.where(lane_ch == 1 + nr, sides(5), result)
        result = jnp.where(lane_ch == 64, sides(6), result)
        result = jnp.where(lane_ch == 0, sides(7), result)
        halo[layer, 0, 2] = result.astype(bf16)

    def gather(layer, q):
        for n in range(2):
            y_copy(layer, n, q).wait_recv()
            y_copy(layer, n + 2, q).start()
        if q + 2 < CHUNKS:
            send_own(layer, q + 2)

    def conv_rows(layer, columns):
        stacked = jnp.concatenate(
            [jnp.concatenate([column[a] for column in columns], axis=1) for a in range(3)], axis=0
        )
        return jnp.dot(taps[layer], stacked, preferred_element_type=f32)

    def add_columns(total):
        left = jnp.where(lane == 0, 0.0, pltpu.roll(total[0:chp], 1, 1))
        right = jnp.where(lane == LANES - 1, 0.0, pltpu.roll(total[2 * chp : 3 * chp], LANES - 1, 1))
        return total[chp : 2 * chp] + left + right

    def conv_chunk(layer, q, low, count):
        for n in range(2, 4):
            y_copy(layer, n, q).wait_recv()

        def pack(i, carry):
            for h in range(2):
                for j in range(1, PEERS):
                    grid[1 + 2 * i + h, j * SLOT : j * SLOT + ch, :] = share[layer, j, i, h]
            return carry

        lax.fori_loop(q * part, (q + 1) * part, pack, 0)
        total = conv_rows(layer, [[grid[low + n + a] for a in range(3)] for n in range(count)])
        for n in range(count):
            sums[low + n] = add_columns(total[:, n * LANES : (n + 1) * LANES])

    def layer_sums(layer):
        z_copy(layer, 0).wait_recv()
        z_copy(layer, 4).start()
        z_copy(layer, 6).start()
        z_copy(layer, 1).wait_recv()
        z_copy(layer, 5).start()
        z_copy(layer, 7).start()
        s_copy(layer, zs - 2).start()
        s_copy(layer, 2).start()
        for n, o in ((2, zs - 1), (3, 1)):
            z_copy(layer, n).wait_recv()
            s_copy(layer, o).start()
        gather(layer, 0)
        for n, o in ((4, zs - 3), (5, 3)):
            z_copy(layer, n).wait_recv()
            s_copy(layer, o).start()
        z_copy(layer, 6).wait_recv()
        z_copy(layer, 7).wait_recv()
        s_copy(layer, 4).start()
        gather(layer, 1)
        for o in range(zs):
            s_copy(layer, o, False).wait_recv()

        def one_slot(v, carry):
            build_slot(layer, v)
            return carry

        lax.fori_loop(0, xs, one_slot, 0)
        for o in range(1, xs):
            u_copy(layer, o).start()
        slots_x[layer][x] = slots[layer, x]
        gather(layer, 2)
        conv_chunk(layer, 0, 1, rows_of - 2)
        for o in range(1, xs):
            u_copy(layer, o).wait_recv()
        merge(layer)
        for o in range(1, PEERS):
            h_copy(layer, o).start()
        gather(layer, 3)
        for q in range(1, CHUNKS):
            conv_chunk(layer, q, q * rows_of - 1, rows_of)
        for o in range(1, PEERS):
            h_copy(layer, o).wait_recv()
        for j in range(PEERS):
            block = slice(j * SLOT, j * SLOT + ch)
            grid[0, block, :] = halo[layer, j, 0]
            grid[nr + 1, block, :] = halo[layer, j, 1]
            sides_k[block, :] = halo[layer, j, 2].astype(f32)
        column = [pltpu.roll(sides_k[...], shift, 1).astype(bf16) if shift else sides_k[...].astype(bf16) for shift in (1, 0, LANES - 1)]
        total = conv_rows(layer, [[grid[r + a] for a in range(3)] for r in (0, nr - 1)] + [column])
        sums[0] = add_columns(total[:, 0:LANES])
        sums[nr - 1] = add_columns(total[:, LANES : 2 * LANES])
        return total[0:chp, 2 * LANES :], total[2 * chp : 3 * chp, 2 * LANES :]

    def full_row(r, to_west, to_east):
        edge = jnp.where(lane == 0, pltpu.roll(to_west, LANES - 1 - r, 1), 0.0)
        edge = jnp.where(lane == LANES - 1, pltpu.roll(to_east, 62 - r, 1), edge)
        return sums[r] + edge

    to_west, to_east = layer_sums(0)

    def hidden_chunk(q, sides):
        for i in range(part):
            for h in range(2):
                r = 2 * (q * part + i) + h
                v = full_row(r, to_west, to_east) + biases[0]
                v = 0.5 * v * (1.0 + jnp.tanh(math.sqrt(2.0 / math.pi) * (v + 0.044715 * (v * v * v))))
                sides = put_row(1, q * part + i, h, v * mask_row(r), sides)
        return sides

    def hidden_and_send(q, sides):
        sides = hidden_chunk(q, sides)
        send_own(1, q)
        return sides

    sides = lax.fori_loop(0, 2, hidden_and_send, jnp.zeros((chp, LANES), f32))
    put_ring(1, lax.fori_loop(2, CHUNKS, hidden_chunk, sides))
    send_ring(1)

    to_west, to_east = layer_sums(1)

    def final_chunk(q, carry):
        for i in range(part):
            for h in range(2):
                r = 2 * (q * part + i) + h
                own = share[0, 0, q * part + i, h].astype(f32)
                v = own + (full_row(r, to_west, to_east) + biases[1])[0:ch]
                flat[pl.ds(r, ch, stride=nr), :] = v * mask_row(r)
        return carry

    lax.fori_loop(0, CHUNKS, final_chunk, 0)
    out[0] = flat[0 : ch * nr].reshape(ch, nr, LANES).astype(bf16)

    for o in range(1, xs):
        t_copy(o).wait_send()
    for layer in range(2):
        for n in range(4):
            for q in range(CHUNKS):
                y_copy(layer, n, q).wait_send()
        for n in range(8):
            z_copy(layer, n).wait_send()
        for o in range(zs):
            s_copy(layer, o).wait_send()
        for o in range(1, xs):
            u_copy(layer, o).wait_send()
        for o in range(1, PEERS):
            h_copy(layer, o).wait_send()


def build(mesh, xs, zs):
    def body(state, w1, b1, w2, b2, wet, nb, fold):
        ch, nr = state.shape[1], state.shape[2]
        chp = -(-ch // 8) * 8
        pairs = nr // 2
        f32, bf16 = jnp.float32, jnp.bfloat16
        vmem, dma = pltpu.VMEM, pltpu.SemaphoreType.DMA
        inside = pl.BlockSpec(memory_space=pltpu.VMEM)
        return pl.pallas_call(
            functools.partial(body_kernel, (xs, zs, ch, chp, nr)),
            out_shape=jax.ShapeDtypeStruct(state.shape, bf16),
            in_specs=[pl.BlockSpec(memory_space=pl.ANY)] * 8,
            out_specs=inside,
            scratch_shapes=[
                vmem(state.shape, bf16),
                vmem((9, ch, PEERS * ch), bf16),
                vmem((1, ch), f32),
                vmem((9, ch, PEERS * ch), bf16),
                vmem((1, ch), f32),
                vmem(wet.shape, jnp.int32),
                vmem(nb.shape, jnp.int32),
                vmem(fold.shape, jnp.int32),
                vmem((chp * nr, LANES), f32),
                vmem((2, PEERS, pairs, 2, ch, LANES), bf16),
                vmem((nr + 2, PEERS * SLOT, LANES), bf16),
                vmem((PEERS * SLOT, LANES), f32),
                vmem((3 * chp, 3 * PEERS * SLOT), f32),
                vmem((2, 3 * chp, 3 * PEERS * SLOT), bf16),
                vmem((nr, chp, LANES), f32),
                vmem((2 * zs, 3, ch, LANES), bf16),
                vmem((2 * zs, 3, ch, LANES), bf16),
                vmem((2, xs, 3, ch, LANES), bf16),
                vmem((xs, 3, ch, LANES), bf16),
                vmem((xs, 3, ch, LANES), bf16),
                vmem((2, PEERS, 3, ch, LANES), bf16),
                vmem((8, LANES), jnp.int32),
                vmem((xs, 8, LANES), jnp.int32),
                pltpu.SMEM((xs, 8, LANES), jnp.int32),
                dma((2, 4, CHUNKS)),
                dma((2, 4, CHUNKS)),
                dma((2, PEERS)),
                dma((2, PEERS)),
                dma((2, 8)),
                dma((2, 8)),
                dma((2, zs)),
                dma((2, zs)),
                dma((2, xs)),
                dma((2, xs)),
                dma((xs,)),
                dma((xs,)),
                dma((9,)),
            ],
            compiler_params=pltpu.CompilerParams(
                collective_id=0, has_side_effects=True, vmem_limit_bytes=63 * 1024 * 1024
            ),
        )(
            state,
            jnp.swapaxes(w1, 1, 2),
            b1.reshape(1, -1),
            jnp.swapaxes(w2, 1, 2),
            b2.reshape(1, -1),
            wet,
            nb,
            fold,
        )

    return jax.shard_map(
        body,
        mesh=mesh,
        in_specs=(
            P("tiles", "chan", None, None),
            P(None, None, "chan"),
            P("chan"),
            P(None, None, "chan"),
            P("chan"),
            P("tiles", None, None),
            P("tiles", None),
            P("tiles", None),
        ),
        out_specs=P("tiles", "chan", None, None),
        check_vma=False,
    )


def solution(mesh):
    return build(mesh, X_SIZE, Z_SIZE)
```

```python
import functools
import math

import jax
import jax.numpy as jnp
from jax import lax
from jax.experimental import pallas as pl
from jax.experimental.pallas import tpu as pltpu
from jax.sharding import PartitionSpec as P

MESH = pl.DeviceIdType.MESH
LANES = 128
SLOT = 64
PEERS = 4
X_SIZE = 4
Z_SIZE = 8
CHUNKS = 4


def body_kernel(
    geo,
    state_at,
    w1_at,
    b1_at,
    w2_at,
    b2_at,
    wet_at,
    nb_at,
    fold_at,
    out,
    state,
    w1,
    b1,
    w2,
    b2,
    wet,
    nb,
    fold,
    flat,
    share,
    grid,
    sides_k,
    taps_f,
    taps,
    sums,
    rows_0,
    rows_1,
    cols_0,
    cols_1,
    slots_rows,
    slots_cols,
    rows_x0,
    rows_x1,
    cols_x0,
    cols_x1,
    halo,
    table_own,
    table,
    table_s,
    y_send,
    y_recv,
    h_send,
    h_recv,
    z_send,
    z_recv,
    s_send,
    s_recv,
    u_send,
    u_recv,
    t_send,
    t_recv,
    local_sem,
):
    xs, zs, ch, chp, nr = geo
    ring = (rows_0, cols_0), (rows_1, cols_1)
    slots = slots_rows, slots_cols
    slots_x = (rows_x0, cols_x0), (rows_x1, cols_x1)
    halo_at = pl.ds(0, 2), pl.ds(2, 1)
    pairs = nr // 2
    part = pairs // CHUNKS
    rows_of = 2 * part
    depth = PEERS * SLOT
    f32, bf16 = jnp.float32, jnp.bfloat16

    t = lax.axis_index("tiles")
    c = lax.axis_index("chan")
    k = lax.rem(t, 2)
    z = lax.rem(t // 2, zs)
    x = t // (2 * zs)
    me = z * 2 + k
    up = lax.rem(c + 1, PEERS)
    down = lax.rem(c + PEERS - 1, PEERS)

    def along_z(o):
        return lax.rem(z + o + zs, zs) * 2 + k

    def z_peer(o):
        return x * zs * 2 + along_z(o)

    def x_peer(o):
        return lax.rem(x + o, xs) * zs * 2 + me

    sibling = t + 1 - 2 * k
    copies = [
        pltpu.make_async_copy(src, dst, local_sem.at[n])
        for n, (src, dst) in enumerate(
            (
                (state_at, state),
                (wet_at, wet),
                (nb_at, nb),
                (fold_at, fold),
                (w1_at, w1),
                (w2_at, w2),
                (b1_at, b1),
                (b2_at, b2),
            )
        )
    ]
    for copy in copies:
        copy.start()
    lane = lax.broadcasted_iota(jnp.int32, (chp, LANES), 1)

    barrier = pltpu.get_barrier_semaphore()
    for o in range(1, PEERS):
        pl.semaphore_signal(barrier, inc=1, device_id=(t, lax.rem(c + o, PEERS)), device_id_type=MESH)
    tiles = [z_peer(o) for o in (2, -2, 1, -1)] + [x_peer(o) for o in range(1, xs)] + [sibling]
    for tile in tiles:
        pl.semaphore_signal(barrier, inc=1, device_id=(tile, c), device_id_type=MESH)

    def remote(src, dst, send, recv, tile, chan):
        return pltpu.make_async_remote_copy(
            src_ref=src, dst_ref=dst, send_sem=send, recv_sem=recv, device_id=(tile, chan), device_id_type=MESH
        )

    def y_copy(layer, n, q):
        src, dst, chan = ((0, 3, up), (0, 1, down), (3, 2, up), (1, 2, down))[n]
        at = (pl.ds(q * part, part),) + (() if n < 2 else (n - 2,))
        return remote(
            share.at[(layer, src) + at],
            share.at[(layer, dst) + at],
            y_send.at[layer, n, q],
            y_recv.at[layer, n, q],
            t,
            chan,
        )

    def z_copy(layer, n, p):
        origin, target = ((0, 2), (0, -2), (0, 1), (0, -1), (-2, 1), (2, -1), (-2, 2), (2, -2))[n]
        at = (along_z(origin),) + ((pl.ds(n - 6, 1),) if n >= 6 and p == 0 else ())
        where = ring[layer][p].at[at]
        return remote(where, where, z_send.at[layer, p, n], z_recv.at[layer, p, n], z_peer(target), c)

    def far_copies(layer, p):
        return [z_copy(layer, n, p) for n in ((6, 7) if p == 0 else (7,))]

    def s_copy(layer, o, p, mine=True):
        where = ring[layer][p].at[along_z(o) if mine else along_z(o) + 1 - 2 * k]
        return remote(where, where, s_send.at[layer, p, o], s_recv.at[layer, p, o], sibling, c)

    def u_copy(layer, o, p):
        return remote(
            slots[p].at[layer, lax.rem(x + o, xs)],
            slots_x[layer][p].at[x],
            u_send.at[layer, p, o],
            u_recv.at[layer, p, o],
            x_peer(o),
            c,
        )

    def t_copy(o):
        return remote(table_own, table.at[x], t_send.at[o], t_recv.at[o], x_peer(o), c)

    def h_copy(layer, o, p):
        return remote(
            halo.at[layer, 0, halo_at[p]],
            halo.at[layer, PEERS - o, halo_at[p]],
            h_send.at[layer, p, o],
            h_recv.at[layer, p, o],
            t,
            lax.rem(c + o, PEERS),
        )

    grid[...] = jnp.zeros(grid.shape, bf16)
    sides_k[...] = jnp.zeros(sides_k.shape, f32)
    table_own[...] = jnp.zeros((8, LANES), jnp.int32)
    for n in range(4):
        copies[n].wait()
    table_own[0:1, 0:8] = nb[...] * 2 + fold[...]
    flat[0 : ch * nr] = state[0].astype(f32).reshape(ch * nr, LANES)
    flat[ch * nr : chp * nr] = jnp.zeros(((chp - ch) * nr, LANES), f32)

    def put_row(layer, i, h, row, sides):
        r = 2 * i + h
        row16 = row[0:ch].astype(bf16)
        share[layer, 0, i, h] = row16
        grid[r + 1, 0:ch, :] = row16
        sides = jnp.where(lane == 1 + r, pltpu.roll(row, r + 2, 1), sides)
        return jnp.where(lane == 65 + r, pltpu.roll(row, r + 65, 1), sides)

    def mask_row(r):
        return wet[0, pl.ds(r, 1), :].astype(f32)

    def load_chunk(q, sides):
        for i in range(part):
            for h in range(2):
                r = 2 * (q * part + i) + h
                row = flat[pl.ds(r, chp, stride=nr), :] * mask_row(r)
                sides = put_row(0, q * part + i, h, row, sides)
        return sides

    def send_own(layer, q):
        for n in range(2):
            y_copy(layer, n, q).start()

    def send_ring(layer, p):
        for n in range(4):
            z_copy(layer, n, p).start()
        s_copy(layer, 0, p).start()

    sides = lax.fori_loop(0, CHUNKS, load_chunk, jnp.zeros((chp, LANES), f32))
    rows_0[me, 0] = share[0, 0, 0, 0]
    rows_0[me, 1] = share[0, 0, pairs - 1, 1]
    cols_0[me, 0] = sides[0:ch].astype(bf16)

    pl.semaphore_wait(barrier, PEERS - 1 + len(tiles))
    for p in range(2):
        send_ring(0, p)
    for q in range(2):
        send_own(0, q)
    for o in range(1, xs):
        t_copy(o).start()

    k_in = lax.broadcasted_iota(jnp.int32, (PEERS * ch, depth), 0)
    k_at = lax.broadcasted_iota(jnp.int32, (PEERS * ch, depth), 1)
    place = jnp.zeros((PEERS * ch, depth), jnp.bool_)
    for j in range(PEERS):
        owner = lax.rem(c + j, PEERS)
        place = place | ((k_at - SLOT * j == k_in - ch * owner) & (k_at >= SLOT * j) & (k_at < SLOT * j + ch))
    place = jnp.where(place, 1.0, 0.0).astype(bf16)
    taps_f[...] = jnp.zeros(taps_f.shape, f32)
    for n in range(4, 8):
        copies[n].wait()
    for layer, w in enumerate((w1, w2)):
        for a in range(3):
            for b in range(3):
                taps_f[b * chp : b * chp + ch, a * depth : (a + 1) * depth] = jnp.dot(
                    w[3 * a + b], place, preferred_element_type=f32
                )
        taps[layer] = taps_f[...].astype(bf16)

    eye = lax.broadcasted_iota(jnp.int32, (chp, ch), 0) == lax.broadcasted_iota(jnp.int32, (chp, ch), 1)

    def bias_column(b):
        spread = jnp.broadcast_to(b[...], (chp, ch))
        return jnp.sum(jnp.where(eye, spread, 0.0), axis=1, keepdims=True)

    biases = bias_column(b1), bias_column(b2)
    flip = jnp.where(
        lax.broadcasted_iota(jnp.int32, (LANES, LANES), 0) + lax.broadcasted_iota(jnp.int32, (LANES, LANES), 1)
        == LANES - 1,
        1.0,
        0.0,
    ).astype(bf16)

    table[x] = table_own[...]
    for o in range(1, xs):
        t_copy(o).wait_recv()
    move = pltpu.make_async_copy(table, table_s, local_sem.at[8])
    move.start()
    move.wait()

    lane_ch = lax.broadcasted_iota(jnp.int32, (ch, LANES), 1)
    east = (lane_ch >= 65) & (lane_ch < 65 + nr)
    west = (lane_ch >= 1) & (lane_ch < 1 + nr)

    def read_table(v):
        codes = [table_s[v, 0, n] for n in range(8)]
        return [code >> 1 for code in codes], [code & 1 for code in codes]

    def build_rows(layer, v):
        ids, folds = read_table(v)
        north, south = [lax.rem(jnp.maximum(q, 0), 2 * zs) for q in ids[0:2]]
        edges = ring[layer][0]
        slots_rows[layer, v, 0] = edges[south, 1]
        slots_rows[layer, v, 1] = jnp.where(folds[0] == 1, edges[north, 1], edges[north, 0])

    def build_cols(layer, v):
        ids, folds = read_table(v)
        at = [lax.rem(jnp.maximum(q, 0), 2 * zs) for q in ids]

        def cols(n):
            return ring[layer][1][at[n], 0].astype(f32)

        def corner_top(n):
            v = cols(n)
            return jnp.where(folds[n] == 1, pltpu.roll(v, 65, 1), pltpu.roll(v, nr, 1))

        result = jnp.where(east, cols(2), cols(3))
        result = jnp.where(lane_ch == 65 + nr, corner_top(4), result)
        result = jnp.where(lane_ch == 1 + nr, corner_top(5), result)
        result = jnp.where(lane_ch == 64, pltpu.roll(cols(6), LANES - nr, 1), result)
        result = jnp.where(lane_ch == 0, pltpu.roll(cols(7), LANES - nr, 1), result)
        slots_cols[layer, v, 0] = result.astype(bf16)

    def usable(code, value):
        return jnp.where(code >= 0, value, jnp.zeros_like(value))

    def merge_rows(layer):
        ids, folds = read_table(x)
        at = [jnp.maximum(q, 0) // (2 * zs) for q in ids[0:2]]
        edges = slots_x[layer][0]
        halo[layer, 0, 0] = usable(ids[1], edges[at[1], 0])
        north = edges[at[0], 1]
        turned = jnp.dot(north, flip, preferred_element_type=f32).astype(bf16)
        halo[layer, 0, 1] = usable(ids[0], jnp.where(folds[0] == 1, turned, north))

    def merge_cols(layer):
        ids, _ = read_table(x)

        def cols(n):
            return usable(ids[n], slots_x[layer][1][jnp.maximum(ids[n], 0) // (2 * zs), 0].astype(f32))

        result = jnp.where(east, cols(2), 0.0)
        result = jnp.where(west, cols(3), result)
        result = jnp.where(lane_ch == 65 + nr, cols(4), result)
        result = jnp.where(lane_ch == 1 + nr, cols(5), result)
        result = jnp.where(lane_ch == 64, cols(6), result)
        result = jnp.where(lane_ch == 0, cols(7), result)
        halo[layer, 0, 2] = result.astype(bf16)

    def gather(layer, q):
        for n in range(2):
            y_copy(layer, n, q).wait_recv()
            y_copy(layer, n + 2, q).start()
        if q == 0:
            for later in range(2, CHUNKS):
                send_own(layer, later)

    def conv_rows(layer, columns):
        stacked = jnp.concatenate(
            [jnp.concatenate([column[a] for column in columns], axis=1) for a in range(3)], axis=0
        )
        return jnp.dot(taps[layer], stacked, preferred_element_type=f32)

    def add_columns(total):
        left = jnp.where(lane == 0, 0.0, pltpu.roll(total[0:chp], 1, 1))
        right = jnp.where(lane == LANES - 1, 0.0, pltpu.roll(total[2 * chp : 3 * chp], LANES - 1, 1))
        return total[chp : 2 * chp] + left + right

    def conv_chunk(layer, q, low, count):
        for n in range(2, 4):
            y_copy(layer, n, q).wait_recv()

        def pack(i, carry):
            for h in range(2):
                for j in range(1, PEERS):
                    grid[1 + 2 * i + h, j * SLOT : j * SLOT + ch, :] = share[layer, j, i, h]
            return carry

        lax.fori_loop(q * part, (q + 1) * part, pack, 0)
        total = conv_rows(layer, [[grid[low + n + a] for a in range(3)] for n in range(count)])
        for n in range(count):
            sums[low + n] = add_columns(total[:, n * LANES : (n + 1) * LANES])

    def layer_sums(layer):
        def near(p):
            z_copy(layer, 0, p).wait_recv()
            z_copy(layer, 4, p).start()
            if p == 0:
                z_copy(layer, 6, p).start()
            z_copy(layer, 1, p).wait_recv()
            z_copy(layer, 5, p).start()
            z_copy(layer, 7, p).start()
            s_copy(layer, zs - 2, p).start()
            s_copy(layer, 2, p).start()
            for n, o in ((2, zs - 1), (3, 1)):
                z_copy(layer, n, p).wait_recv()
                s_copy(layer, o, p).start()

        def far(p):
            for n, o in ((4, zs - 3), (5, 3)):
                z_copy(layer, n, p).wait_recv()
                s_copy(layer, o, p).start()
            for copy in far_copies(layer, p):
                copy.wait_recv()
            s_copy(layer, 4, p).start()

        def along_x(p):
            for o in range(zs):
                s_copy(layer, o, p, False).wait_recv()

            def one_slot(v, carry):
                (build_rows, build_cols)[p](layer, v)
                return carry

            lax.fori_loop(0, xs, one_slot, 0)
            for o in range(1, xs):
                u_copy(layer, o, p).start()
            slots_x[layer][p][x] = slots[p][layer, x]

        def along_y(p):
            for o in range(1, xs):
                u_copy(layer, o, p).wait_recv()
            (merge_rows, merge_cols)[p](layer)
            for o in range(1, PEERS):
                h_copy(layer, o, p).start()

        near(0)
        near(1)
        gather(layer, 0)
        far(0)
        far(1)
        gather(layer, 1)
        along_x(0)
        along_x(1)
        gather(layer, 2)
        along_y(0)
        along_y(1)
        conv_chunk(layer, 0, 1, rows_of - 2)
        gather(layer, 3)
        for q in range(1, CHUNKS):
            conv_chunk(layer, q, q * rows_of - 1, rows_of)
        for p in range(2):
            for o in range(1, PEERS):
                h_copy(layer, o, p).wait_recv()
        for j in range(PEERS):
            block = slice(j * SLOT, j * SLOT + ch)
            grid[0, block, :] = halo[layer, j, 0]
            grid[nr + 1, block, :] = halo[layer, j, 1]
            sides_k[block, :] = halo[layer, j, 2].astype(f32)
        column = [pltpu.roll(sides_k[...], shift, 1).astype(bf16) if shift else sides_k[...].astype(bf16) for shift in (1, 0, LANES - 1)]
        total = conv_rows(layer, [[grid[r + a] for a in range(3)] for r in (0, nr - 1)] + [column])
        sums[0] = add_columns(total[:, 0:LANES])
        sums[nr - 1] = add_columns(total[:, LANES : 2 * LANES])
        return total[0:chp, 2 * LANES :], total[2 * chp : 3 * chp, 2 * LANES :]

    def full_row(r, to_west, to_east):
        edge = jnp.where(lane == 0, pltpu.roll(to_west, LANES - 1 - r, 1), 0.0)
        edge = jnp.where(lane == LANES - 1, pltpu.roll(to_east, 62 - r, 1), edge)
        return sums[r] + edge

    to_west, to_east = layer_sums(0)

    def hidden_row(r):
        v = full_row(r, to_west, to_east) + biases[0]
        v = 0.5 * v * (1.0 + jnp.tanh(math.sqrt(2.0 / math.pi) * (v + 0.044715 * (v * v * v))))
        return v * mask_row(r)

    def hidden_chunk(q, sides):
        for i in range(part):
            for h in range(2):
                sides = put_row(1, q * part + i, h, hidden_row(2 * (q * part + i) + h), sides)
        return sides

    def hidden_and_send(q, sides):
        sides = hidden_chunk(q, sides)
        send_own(1, q)
        return sides

    rows_1[me, 0] = hidden_row(0)[0:ch].astype(bf16)
    rows_1[me, 1] = hidden_row(nr - 1)[0:ch].astype(bf16)
    send_ring(1, 0)
    sides = lax.fori_loop(0, 2, hidden_and_send, jnp.zeros((chp, LANES), f32))
    sides = lax.fori_loop(2, CHUNKS, hidden_chunk, sides)
    cols_1[me, 0] = sides[0:ch].astype(bf16)
    send_ring(1, 1)

    to_west, to_east = layer_sums(1)

    def final_chunk(q, carry):
        for i in range(part):
            for h in range(2):
                r = 2 * (q * part + i) + h
                own = share[0, 0, q * part + i, h].astype(f32)
                v = own + (full_row(r, to_west, to_east) + biases[1])[0:ch]
                flat[pl.ds(r, ch, stride=nr), :] = v * mask_row(r)
        return carry

    lax.fori_loop(0, CHUNKS, final_chunk, 0)
    out[0] = flat[0 : ch * nr].reshape(ch, nr, LANES).astype(bf16)

    for o in range(1, xs):
        t_copy(o).wait_send()
    for layer in range(2):
        for n in range(4):
            for q in range(CHUNKS):
                y_copy(layer, n, q).wait_send()
        for p in range(2):
            for n in range(6):
                z_copy(layer, n, p).wait_send()
            for copy in far_copies(layer, p):
                copy.wait_send()
            for o in range(zs):
                s_copy(layer, o, p).wait_send()
            for o in range(1, xs):
                u_copy(layer, o, p).wait_send()
            for o in range(1, PEERS):
                h_copy(layer, o, p).wait_send()


def build(mesh, xs, zs):
    def body(state, w1, b1, w2, b2, wet, nb, fold):
        ch, nr = state.shape[1], state.shape[2]
        chp = -(-ch // 8) * 8
        pairs = nr // 2
        f32, bf16 = jnp.float32, jnp.bfloat16
        vmem, dma = pltpu.VMEM, pltpu.SemaphoreType.DMA
        inside = pl.BlockSpec(memory_space=pltpu.VMEM)
        return pl.pallas_call(
            functools.partial(body_kernel, (xs, zs, ch, chp, nr)),
            out_shape=jax.ShapeDtypeStruct(state.shape, bf16),
            in_specs=[pl.BlockSpec(memory_space=pl.ANY)] * 8,
            out_specs=inside,
            scratch_shapes=[
                vmem(state.shape, bf16),
                vmem((9, ch, PEERS * ch), bf16),
                vmem((1, ch), f32),
                vmem((9, ch, PEERS * ch), bf16),
                vmem((1, ch), f32),
                vmem(wet.shape, jnp.int32),
                vmem(nb.shape, jnp.int32),
                vmem(fold.shape, jnp.int32),
                vmem((chp * nr, LANES), f32),
                vmem((2, PEERS, pairs, 2, ch, LANES), bf16),
                vmem((nr + 2, PEERS * SLOT, LANES), bf16),
                vmem((PEERS * SLOT, LANES), f32),
                vmem((3 * chp, 3 * PEERS * SLOT), f32),
                vmem((2, 3 * chp, 3 * PEERS * SLOT), bf16),
                vmem((nr, chp, LANES), f32),
                vmem((2 * zs, 2, ch, LANES), bf16),
                vmem((2 * zs, 2, ch, LANES), bf16),
                vmem((2 * zs, 1, ch, LANES), bf16),
                vmem((2 * zs, 1, ch, LANES), bf16),
                vmem((2, xs, 2, ch, LANES), bf16),
                vmem((2, xs, 1, ch, LANES), bf16),
                vmem((xs, 2, ch, LANES), bf16),
                vmem((xs, 2, ch, LANES), bf16),
                vmem((xs, 1, ch, LANES), bf16),
                vmem((xs, 1, ch, LANES), bf16),
                vmem((2, PEERS, 3, ch, LANES), bf16),
                vmem((8, LANES), jnp.int32),
                vmem((xs, 8, LANES), jnp.int32),
                pltpu.SMEM((xs, 8, LANES), jnp.int32),
                dma((2, 4, CHUNKS)),
                dma((2, 4, CHUNKS)),
                dma((2, 2, PEERS)),
                dma((2, 2, PEERS)),
                dma((2, 2, 8)),
                dma((2, 2, 8)),
                dma((2, 2, zs)),
                dma((2, 2, zs)),
                dma((2, 2, xs)),
                dma((2, 2, xs)),
                dma((xs,)),
                dma((xs,)),
                dma((9,)),
            ],
            compiler_params=pltpu.CompilerParams(
                collective_id=0, has_side_effects=True, vmem_limit_bytes=63 * 1024 * 1024
            ),
        )(
            state,
            jnp.swapaxes(w1, 1, 2),
            b1.reshape(1, -1),
            jnp.swapaxes(w2, 1, 2),
            b2.reshape(1, -1),
            wet,
            nb,
            fold,
        )

    return jax.shard_map(
        body,
        mesh=mesh,
        in_specs=(
            P("tiles", "chan", None, None),
            P(None, None, "chan"),
            P("chan"),
            P(None, None, "chan"),
            P("chan"),
            P("tiles", None, None),
            P("tiles", None),
            P("tiles", None),
        ),
        out_specs=P("tiles", "chan", None, None),
        check_vma=False,
    )


def solution(mesh):
    return build(mesh, X_SIZE, Z_SIZE)
```

```python
import functools
import math

import jax
import jax.numpy as jnp
from jax import lax
from jax.experimental import pallas as pl
from jax.experimental.pallas import tpu as pltpu
from jax.sharding import PartitionSpec as P

MESH = pl.DeviceIdType.MESH
LANES = 128
SLOT = 64
PEERS = 4
X_SIZE = 4
Z_SIZE = 8
CHUNKS = 4


def body_kernel(
    geo,
    state_at,
    w1_at,
    b1_at,
    w2_at,
    b2_at,
    wet_at,
    nb_at,
    fold_at,
    out,
    state,
    w1,
    b1,
    w2,
    b2,
    wet,
    nb,
    fold,
    flat,
    share,
    grid,
    sides_k,
    taps_f,
    taps,
    sums,
    rows_0,
    rows_1,
    cols_0,
    cols_1,
    slots_rows,
    slots_cols,
    rows_x0,
    rows_x1,
    cols_x0,
    cols_x1,
    halo,
    table_own,
    table,
    table_s,
    y_send,
    y_recv,
    h_send,
    h_recv,
    z_send,
    z_recv,
    s_send,
    s_recv,
    u_send,
    u_recv,
    t_send,
    t_recv,
    local_sem,
):
    xs, zs, ch, chp, nr = geo
    ring = (rows_0, cols_0), (rows_1, cols_1)
    slots = slots_rows, slots_cols
    slots_x = (rows_x0, cols_x0), (rows_x1, cols_x1)
    halo_at = pl.ds(0, 2), pl.ds(2, 1)
    pairs = nr // 2
    part = pairs // CHUNKS
    rows_of = 2 * part
    depth = PEERS * SLOT
    f32, bf16 = jnp.float32, jnp.bfloat16

    t = lax.axis_index("tiles")
    c = lax.axis_index("chan")
    k = lax.rem(t, 2)
    z = lax.rem(t // 2, zs)
    x = t // (2 * zs)
    me = z * 2 + k
    up = lax.rem(c + 1, PEERS)
    down = lax.rem(c + PEERS - 1, PEERS)

    def along_z(o):
        return lax.rem(z + o + zs, zs) * 2 + k

    def z_peer(o):
        return x * zs * 2 + along_z(o)

    def x_peer(o):
        return lax.rem(x + o, xs) * zs * 2 + me

    sibling = t + 1 - 2 * k
    copies = [
        pltpu.make_async_copy(src, dst, local_sem.at[n])
        for n, (src, dst) in enumerate(
            (
                (state_at, state),
                (wet_at, wet),
                (nb_at, nb),
                (fold_at, fold),
                (w1_at, w1),
                (w2_at, w2),
                (b1_at, b1),
                (b2_at, b2),
            )
        )
    ]
    for copy in copies:
        copy.start()
    lane = lax.broadcasted_iota(jnp.int32, (chp, LANES), 1)

    barrier = pltpu.get_barrier_semaphore()
    for o in range(1, PEERS):
        pl.semaphore_signal(barrier, inc=1, device_id=(t, lax.rem(c + o, PEERS)), device_id_type=MESH)
    tiles = [z_peer(o) for o in (2, -2, 1, -1)] + [x_peer(o) for o in range(1, xs)] + [sibling]
    for tile in tiles:
        pl.semaphore_signal(barrier, inc=1, device_id=(tile, c), device_id_type=MESH)

    def remote(src, dst, send, recv, tile, chan):
        return pltpu.make_async_remote_copy(
            src_ref=src, dst_ref=dst, send_sem=send, recv_sem=recv, device_id=(tile, chan), device_id_type=MESH
        )

    def y_copy(layer, n, q):
        src, dst, chan = ((0, 3, up), (0, 1, down), (3, 2, up), (1, 2, down))[n]
        at = (pl.ds(q * part, part),) + (() if n < 2 else (n - 2,))
        return remote(
            share.at[(layer, src) + at],
            share.at[(layer, dst) + at],
            y_send.at[layer, n, q],
            y_recv.at[layer, n, q],
            t,
            chan,
        )

    def z_copy(layer, n, p):
        origin, target = ((0, 2), (0, -2), (0, 1), (0, -1), (-2, 1), (2, -1), (-2, 2), (2, -2))[n]
        at = (along_z(origin),) + ((pl.ds(n - 6, 1),) if n >= 6 and p == 0 else ())
        where = ring[layer][p].at[at]
        return remote(where, where, z_send.at[layer, p, n], z_recv.at[layer, p, n], z_peer(target), c)

    def far_copies(layer, p):
        return [z_copy(layer, n, p) for n in ((6, 7) if p == 0 else (7,))]

    def s_copy(layer, o, p, mine=True):
        where = ring[layer][p].at[along_z(o) if mine else along_z(o) + 1 - 2 * k]
        return remote(where, where, s_send.at[layer, p, o], s_recv.at[layer, p, o], sibling, c)

    def u_copy(layer, o, p):
        return remote(
            slots[p].at[layer, lax.rem(x + o, xs)],
            slots_x[layer][p].at[x],
            u_send.at[layer, p, o],
            u_recv.at[layer, p, o],
            x_peer(o),
            c,
        )

    def t_copy(o):
        return remote(table_own, table.at[x], t_send.at[o], t_recv.at[o], x_peer(o), c)

    def h_copy(layer, o, p):
        return remote(
            halo.at[layer, 0, halo_at[p]],
            halo.at[layer, PEERS - o, halo_at[p]],
            h_send.at[layer, p, o],
            h_recv.at[layer, p, o],
            t,
            lax.rem(c + o, PEERS),
        )

    grid[...] = jnp.zeros(grid.shape, bf16)
    sides_k[...] = jnp.zeros(sides_k.shape, f32)
    table_own[...] = jnp.zeros((8, LANES), jnp.int32)
    for n in range(4):
        copies[n].wait()
    table_own[0:1, 0:8] = nb[...] * 2 + fold[...]
    flat[0 : ch * nr] = state[0].astype(f32).reshape(ch * nr, LANES)
    flat[ch * nr : chp * nr] = jnp.zeros(((chp - ch) * nr, LANES), f32)

    def put_row(layer, i, h, row, sides):
        r = 2 * i + h
        row16 = row[0:ch].astype(bf16)
        share[layer, 0, i, h] = row16
        grid[r + 1, 0:ch, :] = row16
        return jnp.where((lane == 2 * r + 3) | (lane == 2 * r + 4), pltpu.roll(row, 2 * r + 4, 1), sides)

    def mask_row(r):
        return wet[0, pl.ds(r, 1), :].astype(f32)

    def load_chunk(q, sides):
        for i in range(part):
            for h in range(2):
                r = 2 * (q * part + i) + h
                row = flat[pl.ds(r, chp, stride=nr), :] * mask_row(r)
                sides = put_row(0, q * part + i, h, row, sides)
        return sides

    def send_own(layer, q):
        for n in range(2):
            y_copy(layer, n, q).start()

    def send_ring(layer, p):
        for n in range(4):
            z_copy(layer, n, p).start()
        s_copy(layer, 0, p).start()

    sides = lax.fori_loop(0, CHUNKS, load_chunk, jnp.zeros((chp, LANES), f32))
    rows_0[me, 0] = share[0, 0, 0, 0]
    rows_0[me, 1] = share[0, 0, pairs - 1, 1]
    cols_0[me, 0] = sides[0:ch].astype(bf16)

    pl.semaphore_wait(barrier, PEERS - 1 + len(tiles))
    for p in range(2):
        send_ring(0, p)
    for q in range(CHUNKS):
        send_own(0, q)
    for o in range(1, xs):
        t_copy(o).start()

    k_in = lax.broadcasted_iota(jnp.int32, (PEERS * ch, depth), 0)
    k_at = lax.broadcasted_iota(jnp.int32, (PEERS * ch, depth), 1)
    place = jnp.zeros((PEERS * ch, depth), jnp.bool_)
    for j in range(PEERS):
        owner = lax.rem(c + j, PEERS)
        place = place | ((k_at - SLOT * j == k_in - ch * owner) & (k_at >= SLOT * j) & (k_at < SLOT * j + ch))
    place = jnp.where(place, 1.0, 0.0).astype(bf16)
    taps_f[...] = jnp.zeros(taps_f.shape, f32)
    for n in range(4, 8):
        copies[n].wait()
    for layer, w in enumerate((w1, w2)):
        for a in range(3):
            for b in range(3):
                taps_f[b * chp : b * chp + ch, a * depth : (a + 1) * depth] = jnp.dot(
                    w[3 * a + b], place, preferred_element_type=f32
                )
        taps[layer] = taps_f[...].astype(bf16)

    eye = lax.broadcasted_iota(jnp.int32, (chp, ch), 0) == lax.broadcasted_iota(jnp.int32, (chp, ch), 1)

    def bias_column(b):
        spread = jnp.broadcast_to(b[...], (chp, ch))
        return jnp.sum(jnp.where(eye, spread, 0.0), axis=1, keepdims=True)

    biases = bias_column(b1), bias_column(b2)
    flip = jnp.where(
        lax.broadcasted_iota(jnp.int32, (LANES, LANES), 0) + lax.broadcasted_iota(jnp.int32, (LANES, LANES), 1)
        == LANES - 1,
        1.0,
        0.0,
    ).astype(bf16)

    table[x] = table_own[...]
    for o in range(1, xs):
        t_copy(o).wait_recv()
    move = pltpu.make_async_copy(table, table_s, local_sem.at[8])
    move.start()
    move.wait()

    lane_ch = lax.broadcasted_iota(jnp.int32, (ch, LANES), 1)
    odd = (lane_ch & 1) == 1
    east = (~odd) & (lane_ch >= 4) & (lane_ch <= 2 * nr + 2)
    west = odd & (lane_ch >= 3) & (lane_ch <= 2 * nr + 1)

    def read_table(v):
        codes = [table_s[v, 0, n] for n in range(8)]
        return [code >> 1 for code in codes], [code & 1 for code in codes]

    def build_rows(layer, v):
        ids, folds = read_table(v)
        north, south = [lax.rem(jnp.maximum(q, 0), 2 * zs) for q in ids[0:2]]
        edges = ring[layer][0]
        slots_rows[layer, v, 0] = edges[south, 1]
        slots_rows[layer, v, 1] = jnp.where(folds[0] == 1, edges[north, 1], edges[north, 0])

    def build_cols(layer, v):
        ids, folds = read_table(v)
        at = [lax.rem(jnp.maximum(q, 0), 2 * zs) for q in ids]

        def cols(n):
            return ring[layer][1][at[n], 0].astype(f32)

        def corner_top(n, across):
            v = cols(n)
            return jnp.where(folds[n] == 1, pltpu.roll(v, across, 1), pltpu.roll(v, 2 * nr, 1))

        result = jnp.where(odd, cols(3), cols(2))
        result = jnp.where(lane_ch == 2 * nr + 4, corner_top(4, 3), result)
        result = jnp.where(lane_ch == 2 * nr + 3, corner_top(5, 1), result)
        result = jnp.where(lane_ch == 2, pltpu.roll(cols(6), LANES - 2 * nr, 1), result)
        result = jnp.where(lane_ch == 1, pltpu.roll(cols(7), LANES - 2 * nr, 1), result)
        slots_cols[layer, v, 0] = result.astype(bf16)

    def usable(code, value):
        return jnp.where(code >= 0, value, jnp.zeros_like(value))

    def merge_rows(layer):
        ids, folds = read_table(x)
        at = [jnp.maximum(q, 0) // (2 * zs) for q in ids[0:2]]
        edges = slots_x[layer][0]
        halo[layer, 0, 0] = usable(ids[1], edges[at[1], 0])
        north = edges[at[0], 1]
        turned = jnp.dot(north, flip, preferred_element_type=f32).astype(bf16)
        halo[layer, 0, 1] = usable(ids[0], jnp.where(folds[0] == 1, turned, north))

    def merge_cols(layer):
        ids, _ = read_table(x)

        def cols(n):
            return usable(ids[n], slots_x[layer][1][jnp.maximum(ids[n], 0) // (2 * zs), 0].astype(f32))

        result = jnp.where(east, cols(2), 0.0)
        result = jnp.where(west, cols(3), result)
        result = jnp.where(lane_ch == 2 * nr + 4, cols(4), result)
        result = jnp.where(lane_ch == 2 * nr + 3, cols(5), result)
        result = jnp.where(lane_ch == 2, cols(6), result)
        result = jnp.where(lane_ch == 1, cols(7), result)
        halo[layer, 0, 2] = result.astype(bf16)

    def gather(layer, q):
        for n in range(2):
            y_copy(layer, n, q).wait_recv()
            y_copy(layer, n + 2, q).start()

    def conv_rows(layer, columns):
        stacked = jnp.concatenate(
            [jnp.concatenate([column[a] for column in columns], axis=1) for a in range(3)], axis=0
        )
        return jnp.dot(taps[layer], stacked, preferred_element_type=f32)

    def add_columns(total):
        left = jnp.where(lane == 0, 0.0, pltpu.roll(total[0:chp], 1, 1))
        right = jnp.where(lane == LANES - 1, 0.0, pltpu.roll(total[2 * chp : 3 * chp], LANES - 1, 1))
        return total[chp : 2 * chp] + left + right

    def conv_chunk(layer, q, low, count):
        for n in range(2, 4):
            y_copy(layer, n, q).wait_recv()

        def pack(i, carry):
            for h in range(2):
                for j in range(1, PEERS):
                    grid[1 + 2 * i + h, j * SLOT : j * SLOT + ch, :] = share[layer, j, i, h]
            return carry

        lax.fori_loop(q * part, (q + 1) * part, pack, 0)
        total = conv_rows(layer, [[grid[low + n + a] for a in range(3)] for n in range(count)])
        for n in range(count):
            sums[low + n] = add_columns(total[:, n * LANES : (n + 1) * LANES])

    def layer_sums(layer):
        def near(p):
            z_copy(layer, 0, p).wait_recv()
            z_copy(layer, 4, p).start()
            if p == 0:
                z_copy(layer, 6, p).start()
            z_copy(layer, 1, p).wait_recv()
            z_copy(layer, 5, p).start()
            z_copy(layer, 7, p).start()
            s_copy(layer, zs - 2, p).start()
            s_copy(layer, 2, p).start()
            for n, o in ((2, zs - 1), (3, 1)):
                z_copy(layer, n, p).wait_recv()
                s_copy(layer, o, p).start()

        def far(p):
            for n, o in ((4, zs - 3), (5, 3)):
                z_copy(layer, n, p).wait_recv()
                s_copy(layer, o, p).start()
            for copy in far_copies(layer, p):
                copy.wait_recv()
            s_copy(layer, 4, p).start()

        def along_x(p):
            for o in range(zs):
                s_copy(layer, o, p, False).wait_recv()

            def one_slot(v, carry):
                (build_rows, build_cols)[p](layer, v)
                return carry

            lax.fori_loop(0, xs, one_slot, 0)
            for o in range(1, xs):
                u_copy(layer, o, p).start()
            slots_x[layer][p][x] = slots[p][layer, x]

        def along_y(p):
            for o in range(1, xs):
                u_copy(layer, o, p).wait_recv()
            (merge_rows, merge_cols)[p](layer)
            for o in range(1, PEERS):
                h_copy(layer, o, p).start()

        near(0)
        near(1)
        far(0)
        gather(layer, 0)
        far(1)
        along_x(0)
        gather(layer, 1)
        along_x(1)
        gather(layer, 2)
        along_y(0)
        gather(layer, 3)
        along_y(1)
        conv_chunk(layer, 0, 1, rows_of - 2)
        for q in range(1, CHUNKS):
            conv_chunk(layer, q, q * rows_of - 1, rows_of)
        for p in range(2):
            for o in range(1, PEERS):
                h_copy(layer, o, p).wait_recv()
        for j in range(PEERS):
            block = slice(j * SLOT, j * SLOT + ch)
            grid[0, block, :] = halo[layer, j, 0]
            grid[nr + 1, block, :] = halo[layer, j, 1]
            sides_k[block, :] = halo[layer, j, 2].astype(f32)
        frame = sides_k[...]
        column = [v.astype(bf16) for v in (pltpu.roll(frame, 2, 1), frame, pltpu.roll(frame, LANES - 2, 1))]
        total = conv_rows(layer, [[grid[r + a] for a in range(3)] for r in (0, nr - 1)] + [column])
        sums[0] = add_columns(total[:, 0:LANES])
        sums[nr - 1] = add_columns(total[:, LANES : 2 * LANES])
        return jnp.where((lane & 1) == 1, total[0:chp, 2 * LANES :], total[2 * chp : 3 * chp, 2 * LANES :])

    def turn(columns, r):
        return pltpu.roll(columns, 123 - 2 * r, 1)

    def full_row(r, below, this):
        return sums[r] + jnp.where(lane == 0, below, jnp.where(lane == LANES - 1, this, 0.0))

    columns_0 = layer_sums(0)

    def hidden_row(r, below, this):
        v = full_row(r, below, this) + biases[0]
        v = 0.5 * v * (1.0 + jnp.tanh(math.sqrt(2.0 / math.pi) * (v + 0.044715 * (v * v * v))))
        return v * mask_row(r)

    def hidden_chunk(q, sides):
        below = turn(columns_0, q * rows_of - 1)
        for i in range(part):
            for h in range(2):
                r = 2 * (q * part + i) + h
                this = turn(columns_0, r)
                sides = put_row(1, q * part + i, h, hidden_row(r, below, this), sides)
                below = this
        return sides

    def hidden_and_send(q, sides):
        sides = hidden_chunk(q, sides)
        send_own(1, q)
        return sides

    for n, r in enumerate((0, nr - 1)):
        rows_1[me, n] = hidden_row(r, turn(columns_0, r - 1), turn(columns_0, r))[0:ch].astype(bf16)
    send_ring(1, 0)
    sides = lax.fori_loop(0, CHUNKS, hidden_and_send, jnp.zeros((chp, LANES), f32))
    cols_1[me, 0] = sides[0:ch].astype(bf16)
    send_ring(1, 1)

    columns_1 = layer_sums(1)

    def final_chunk(q, carry):
        below = turn(columns_1, q * rows_of - 1)
        for i in range(part):
            for h in range(2):
                r = 2 * (q * part + i) + h
                this = turn(columns_1, r)
                own = share[0, 0, q * part + i, h].astype(f32)
                v = own + (full_row(r, below, this) + biases[1])[0:ch]
                flat[pl.ds(r, ch, stride=nr), :] = v * mask_row(r)
                below = this
        return carry

    lax.fori_loop(0, CHUNKS, final_chunk, 0)
    out[0] = flat[0 : ch * nr].reshape(ch, nr, LANES).astype(bf16)

    for o in range(1, xs):
        t_copy(o).wait_send()
    for layer in range(2):
        for n in range(4):
            for q in range(CHUNKS):
                y_copy(layer, n, q).wait_send()
        for p in range(2):
            for n in range(6):
                z_copy(layer, n, p).wait_send()
            for copy in far_copies(layer, p):
                copy.wait_send()
            for o in range(zs):
                s_copy(layer, o, p).wait_send()
            for o in range(1, xs):
                u_copy(layer, o, p).wait_send()
            for o in range(1, PEERS):
                h_copy(layer, o, p).wait_send()


def build(mesh, xs, zs):
    def body(state, w1, b1, w2, b2, wet, nb, fold):
        ch, nr = state.shape[1], state.shape[2]
        chp = -(-ch // 8) * 8
        pairs = nr // 2
        f32, bf16 = jnp.float32, jnp.bfloat16
        vmem, dma = pltpu.VMEM, pltpu.SemaphoreType.DMA
        inside = pl.BlockSpec(memory_space=pltpu.VMEM)
        return pl.pallas_call(
            functools.partial(body_kernel, (xs, zs, ch, chp, nr)),
            out_shape=jax.ShapeDtypeStruct(state.shape, bf16),
            in_specs=[pl.BlockSpec(memory_space=pl.ANY)] * 8,
            out_specs=inside,
            scratch_shapes=[
                vmem(state.shape, bf16),
                vmem((9, ch, PEERS * ch), bf16),
                vmem((1, ch), f32),
                vmem((9, ch, PEERS * ch), bf16),
                vmem((1, ch), f32),
                vmem(wet.shape, jnp.int32),
                vmem(nb.shape, jnp.int32),
                vmem(fold.shape, jnp.int32),
                vmem((chp * nr, LANES), f32),
                vmem((2, PEERS, pairs, 2, ch, LANES), bf16),
                vmem((nr + 2, PEERS * SLOT, LANES), bf16),
                vmem((PEERS * SLOT, LANES), f32),
                vmem((3 * chp, 3 * PEERS * SLOT), f32),
                vmem((2, 3 * chp, 3 * PEERS * SLOT), bf16),
                vmem((nr, chp, LANES), f32),
                vmem((2 * zs, 2, ch, LANES), bf16),
                vmem((2 * zs, 2, ch, LANES), bf16),
                vmem((2 * zs, 1, ch, LANES), bf16),
                vmem((2 * zs, 1, ch, LANES), bf16),
                vmem((2, xs, 2, ch, LANES), bf16),
                vmem((2, xs, 1, ch, LANES), bf16),
                vmem((xs, 2, ch, LANES), bf16),
                vmem((xs, 2, ch, LANES), bf16),
                vmem((xs, 1, ch, LANES), bf16),
                vmem((xs, 1, ch, LANES), bf16),
                vmem((2, PEERS, 3, ch, LANES), bf16),
                vmem((8, LANES), jnp.int32),
                vmem((xs, 8, LANES), jnp.int32),
                pltpu.SMEM((xs, 8, LANES), jnp.int32),
                dma((2, 4, CHUNKS)),
                dma((2, 4, CHUNKS)),
                dma((2, 2, PEERS)),
                dma((2, 2, PEERS)),
                dma((2, 2, 8)),
                dma((2, 2, 8)),
                dma((2, 2, zs)),
                dma((2, 2, zs)),
                dma((2, 2, xs)),
                dma((2, 2, xs)),
                dma((xs,)),
                dma((xs,)),
                dma((9,)),
            ],
            compiler_params=pltpu.CompilerParams(
                collective_id=0, has_side_effects=True, vmem_limit_bytes=63 * 1024 * 1024
            ),
        )(
            state,
            jnp.swapaxes(w1, 1, 2),
            b1.reshape(1, -1),
            jnp.swapaxes(w2, 1, 2),
            b2.reshape(1, -1),
            wet,
            nb,
            fold,
        )

    return jax.shard_map(
        body,
        mesh=mesh,
        in_specs=(
            P("tiles", "chan", None, None),
            P(None, None, "chan"),
            P("chan"),
            P(None, None, "chan"),
            P("chan"),
            P("tiles", None, None),
            P("tiles", None),
            P("tiles", None),
        ),
        out_specs=P("tiles", "chan", None, None),
        check_vma=False,
    )


def solution(mesh):
    return build(mesh, X_SIZE, Z_SIZE)
```

```python
import functools
import math

import jax
import jax.numpy as jnp
from jax import lax
from jax.experimental import pallas as pl
from jax.experimental.pallas import tpu as pltpu
from jax.sharding import PartitionSpec as P

MESH = pl.DeviceIdType.MESH
LANES = 128
SLOT = 64
PEERS = 4
X_SIZE = 4
Z_SIZE = 8
CHUNKS = 4


def body_kernel(
    geo,
    state_at,
    w1_at,
    b1_at,
    w2_at,
    b2_at,
    wet_at,
    nb_at,
    fold_at,
    out,
    state,
    w1,
    b1,
    w2,
    b2,
    wet,
    nb,
    fold,
    flat,
    share,
    grid,
    sides_k,
    taps_f,
    taps,
    sums,
    rows_0,
    rows_1,
    cols_0,
    cols_1,
    slots_rows,
    slots_cols,
    rows_x0,
    rows_x1,
    cols_x0,
    cols_x1,
    halo,
    fix,
    fix_f,
    mask_cols,
    sums_cols,
    table_own,
    table,
    table_s,
    y_send,
    y_recv,
    h_send,
    h_recv,
    f_send,
    f_recv,
    z_send,
    z_recv,
    s_send,
    s_recv,
    u_send,
    u_recv,
    t_send,
    t_recv,
    local_sem,
):
    xs, zs, ch, chp, nr = geo
    ring = (rows_0, cols_0), (rows_1, cols_1)
    slots = slots_rows, slots_cols
    slots_x = (rows_x0, cols_x0), (rows_x1, cols_x1)
    halo_at = pl.ds(0, 2), pl.ds(2, 1)
    pairs = nr // 2
    part = pairs // CHUNKS
    rows_of = 2 * part
    depth = PEERS * SLOT
    f32, bf16 = jnp.float32, jnp.bfloat16

    t = lax.axis_index("tiles")
    c = lax.axis_index("chan")
    k = lax.rem(t, 2)
    z = lax.rem(t // 2, zs)
    x = t // (2 * zs)
    me = z * 2 + k
    up = lax.rem(c + 1, PEERS)
    down = lax.rem(c + PEERS - 1, PEERS)

    def along_z(o):
        return lax.rem(z + o + zs, zs) * 2 + k

    def z_peer(o):
        return x * zs * 2 + along_z(o)

    def x_peer(o):
        return lax.rem(x + o, xs) * zs * 2 + me

    sibling = t + 1 - 2 * k
    copies = [
        pltpu.make_async_copy(src, dst, local_sem.at[n])
        for n, (src, dst) in enumerate(
            (
                (state_at, state),
                (wet_at, wet),
                (nb_at, nb),
                (fold_at, fold),
                (w1_at, w1),
                (w2_at, w2),
                (b1_at, b1),
                (b2_at, b2),
            )
        )
    ]
    for copy in copies:
        copy.start()
    lane = lax.broadcasted_iota(jnp.int32, (chp, LANES), 1)

    barrier = pltpu.get_barrier_semaphore()
    for o in range(1, PEERS):
        pl.semaphore_signal(barrier, inc=1, device_id=(t, lax.rem(c + o, PEERS)), device_id_type=MESH)
    tiles = [z_peer(o) for o in (2, -2, 1, -1)] + [x_peer(o) for o in range(1, xs)] + [sibling]
    for tile in tiles:
        pl.semaphore_signal(barrier, inc=1, device_id=(tile, c), device_id_type=MESH)

    def remote(src, dst, send, recv, tile, chan):
        return pltpu.make_async_remote_copy(
            src_ref=src, dst_ref=dst, send_sem=send, recv_sem=recv, device_id=(tile, chan), device_id_type=MESH
        )

    def y_copy(layer, n, q):
        src, dst, chan = ((0, 3, up), (0, 1, down), (3, 2, up), (1, 2, down))[n]
        at = (pl.ds(q * part, part),) + (() if n < 2 else (n - 2,))
        return remote(
            share.at[(layer, src) + at],
            share.at[(layer, dst) + at],
            y_send.at[layer, n, q],
            y_recv.at[layer, n, q],
            t,
            chan,
        )

    def z_copy(layer, n, p):
        origin, target = ((0, 2), (0, -2), (0, 1), (0, -1), (-2, 1), (2, -1), (-2, 2), (2, -2))[n]
        at = (along_z(origin),) + ((pl.ds(n - 6, 1),) if n >= 6 and p == 0 else ())
        where = ring[layer][p].at[at]
        return remote(where, where, z_send.at[layer, p, n], z_recv.at[layer, p, n], z_peer(target), c)

    def far_copies(layer, p):
        return [z_copy(layer, n, p) for n in ((6, 7) if p == 0 else (7,))]

    def s_copy(layer, o, p, mine=True):
        where = ring[layer][p].at[along_z(o) if mine else along_z(o) + 1 - 2 * k]
        return remote(where, where, s_send.at[layer, p, o], s_recv.at[layer, p, o], sibling, c)

    def u_copy(layer, o, p):
        return remote(
            slots[p].at[layer, lax.rem(x + o, xs)],
            slots_x[layer][p].at[x],
            u_send.at[layer, p, o],
            u_recv.at[layer, p, o],
            x_peer(o),
            c,
        )

    def t_copy(o):
        return remote(table_own, table.at[x], t_send.at[o], t_recv.at[o], x_peer(o), c)

    def h_copy(layer, o, p):
        return remote(
            halo.at[layer, 0, halo_at[p]],
            halo.at[layer, PEERS - o, halo_at[p]],
            h_send.at[layer, p, o],
            h_recv.at[layer, p, o],
            t,
            lax.rem(c + o, PEERS),
        )

    def f_copy(o, p):
        return remote(
            fix.at[0, halo_at[p]],
            fix.at[PEERS - o, halo_at[p]],
            f_send.at[p, o],
            f_recv.at[p, o],
            t,
            lax.rem(c + o, PEERS),
        )

    grid[...] = jnp.zeros(grid.shape, bf16)
    sides_k[...] = jnp.zeros(sides_k.shape, f32)
    table_own[...] = jnp.zeros((8, LANES), jnp.int32)
    for n in range(4):
        copies[n].wait()
    table_own[0:1, 0:8] = nb[...] * 2 + fold[...]
    flat[0 : ch * nr] = state[0].astype(f32).reshape(ch * nr, LANES)
    flat[ch * nr : chp * nr] = jnp.zeros(((chp - ch) * nr, LANES), f32)

    def put_cols(r, row, sides):
        at = lax.broadcasted_iota(jnp.int32, row.shape, 1)
        return jnp.where((at == 2 * r + 3) | (at == 2 * r + 4), pltpu.roll(row, 2 * r + 4, 1), sides)

    def mask_row(r):
        return wet[0, pl.ds(r, 1), :].astype(f32)

    def load_chunk(q, carry):
        sides, wet_sides = carry
        for i in range(part):
            for h in range(2):
                r = 2 * (q * part + i) + h
                row_mask = mask_row(r)
                row = flat[pl.ds(r, chp, stride=nr), :] * row_mask
                row16 = row[0:ch].astype(bf16)
                share[0, 0, q * part + i, h] = row16
                grid[r + 1, 0:ch, :] = row16
                sides = put_cols(r, row, sides)
                wet_sides = put_cols(r, jnp.broadcast_to(row_mask, (8, LANES)), wet_sides)
        return sides, wet_sides

    def send_own(layer, q):
        for n in range(2):
            y_copy(layer, n, q).start()

    def send_ring(layer, p):
        for n in range(4):
            z_copy(layer, n, p).start()
        s_copy(layer, 0, p).start()

    sides, wet_sides = lax.fori_loop(
        0, CHUNKS, load_chunk, (jnp.zeros((chp, LANES), f32), jnp.zeros((8, LANES), f32))
    )
    mask_cols[...] = wet_sides
    sums_cols[...] = jnp.zeros((chp, LANES), f32)
    sums[0] = jnp.zeros((chp, LANES), f32)
    sums[nr - 1] = jnp.zeros((chp, LANES), f32)
    rows_0[me, 0] = share[0, 0, 0, 0]
    rows_0[me, 1] = share[0, 0, pairs - 1, 1]
    cols_0[me, 0] = sides[0:ch].astype(bf16)

    pl.semaphore_wait(barrier, PEERS - 1 + len(tiles))
    for p in range(2):
        send_ring(0, p)
    for q in range(CHUNKS):
        send_own(0, q)
    for o in range(1, xs):
        t_copy(o).start()

    k_in = lax.broadcasted_iota(jnp.int32, (PEERS * ch, depth), 0)
    k_at = lax.broadcasted_iota(jnp.int32, (PEERS * ch, depth), 1)
    place = jnp.zeros((PEERS * ch, depth), jnp.bool_)
    for j in range(PEERS):
        owner = lax.rem(c + j, PEERS)
        place = place | ((k_at - SLOT * j == k_in - ch * owner) & (k_at >= SLOT * j) & (k_at < SLOT * j + ch))
    place = jnp.where(place, 1.0, 0.0).astype(bf16)
    taps_f[...] = jnp.zeros(taps_f.shape, f32)
    for n in range(4, 8):
        copies[n].wait()
    for layer, w in enumerate((w1, w2)):
        for a in range(3):
            for b in range(3):
                taps_f[b * chp : b * chp + ch, a * depth : (a + 1) * depth] = jnp.dot(
                    w[3 * a + b], place, preferred_element_type=f32
                )
        taps[layer] = taps_f[...].astype(bf16)

    eye = lax.broadcasted_iota(jnp.int32, (chp, ch), 0) == lax.broadcasted_iota(jnp.int32, (chp, ch), 1)

    def bias_column(b):
        spread = jnp.broadcast_to(b[...], (chp, ch))
        return jnp.sum(jnp.where(eye, spread, 0.0), axis=1, keepdims=True)

    biases = bias_column(b1), bias_column(b2)
    flip = jnp.where(
        lax.broadcasted_iota(jnp.int32, (LANES, LANES), 0) + lax.broadcasted_iota(jnp.int32, (LANES, LANES), 1)
        == LANES - 1,
        1.0,
        0.0,
    ).astype(bf16)

    table[x] = table_own[...]
    for o in range(1, xs):
        t_copy(o).wait_recv()
    move = pltpu.make_async_copy(table, table_s, local_sem.at[8])
    move.start()
    move.wait()

    lane_ch = lax.broadcasted_iota(jnp.int32, (ch, LANES), 1)
    odd = (lane_ch & 1) == 1
    east = (~odd) & (lane_ch >= 4) & (lane_ch <= 2 * nr + 2)
    west = odd & (lane_ch >= 3) & (lane_ch <= 2 * nr + 1)

    def read_table(v):
        codes = [table_s[v, 0, n] for n in range(8)]
        return [code >> 1 for code in codes], [code & 1 for code in codes]

    def build_rows(layer, v):
        ids, folds = read_table(v)
        north, south = [lax.rem(jnp.maximum(q, 0), 2 * zs) for q in ids[0:2]]
        edges = ring[layer][0]
        slots_rows[layer, v, 0] = edges[south, 1]
        slots_rows[layer, v, 1] = jnp.where(folds[0] == 1, edges[north, 1], edges[north, 0])

    def build_cols(layer, v):
        ids, folds = read_table(v)
        at = [lax.rem(jnp.maximum(q, 0), 2 * zs) for q in ids]

        def cols(n):
            return ring[layer][1][at[n], 0].astype(f32)

        def corner_top(n, across):
            v = cols(n)
            return jnp.where(folds[n] == 1, pltpu.roll(v, across, 1), pltpu.roll(v, 2 * nr, 1))

        result = jnp.where(odd, cols(3), cols(2))
        result = jnp.where(lane_ch == 2 * nr + 4, corner_top(4, 3), result)
        result = jnp.where(lane_ch == 2 * nr + 3, corner_top(5, 1), result)
        result = jnp.where(lane_ch == 2, pltpu.roll(cols(6), LANES - 2 * nr, 1), result)
        result = jnp.where(lane_ch == 1, pltpu.roll(cols(7), LANES - 2 * nr, 1), result)
        slots_cols[layer, v, 0] = result.astype(bf16)

    def usable(code, value):
        return jnp.where(code >= 0, value, jnp.zeros_like(value))

    def merge_rows(layer):
        ids, folds = read_table(x)
        at = [jnp.maximum(q, 0) // (2 * zs) for q in ids[0:2]]
        edges = slots_x[layer][0]
        halo[layer, 0, 0] = usable(ids[1], edges[at[1], 0])
        north = edges[at[0], 1]
        turned = jnp.dot(north, flip, preferred_element_type=f32).astype(bf16)
        halo[layer, 0, 1] = usable(ids[0], jnp.where(folds[0] == 1, turned, north))

    def merge_cols(layer):
        ids, _ = read_table(x)

        def cols(n):
            return usable(ids[n], slots_x[layer][1][jnp.maximum(ids[n], 0) // (2 * zs), 0].astype(f32))

        result = jnp.where(east, cols(2), 0.0)
        result = jnp.where(west, cols(3), result)
        result = jnp.where(lane_ch == 2 * nr + 4, cols(4), result)
        result = jnp.where(lane_ch == 2 * nr + 3, cols(5), result)
        result = jnp.where(lane_ch == 2, cols(6), result)
        result = jnp.where(lane_ch == 1, cols(7), result)
        halo[layer, 0, 2] = result.astype(bf16)

    def gather(layer, q):
        for n in range(2):
            y_copy(layer, n, q).wait_recv()
            y_copy(layer, n + 2, q).start()

    def conv_rows(layer, columns):
        stacked = jnp.concatenate(
            [jnp.concatenate([column[a] for column in columns], axis=1) for a in range(3)], axis=0
        )
        return jnp.dot(taps[layer], stacked, preferred_element_type=f32)

    def add_columns(total):
        left = jnp.where(lane == 0, 0.0, pltpu.roll(total[0:chp], 1, 1))
        right = jnp.where(lane == LANES - 1, 0.0, pltpu.roll(total[2 * chp : 3 * chp], LANES - 1, 1))
        return total[chp : 2 * chp] + left + right

    def conv_chunk(layer, q, low, count):
        for n in range(2, 4):
            y_copy(layer, n, q).wait_recv()

        def pack(i, carry):
            for h in range(2):
                for j in range(layer == 0, PEERS):
                    row = share[layer, j, i, h]
                    if layer == 1:
                        ends = pltpu.roll(fix_f[j], LANES - 4 - 2 * (2 * i + h), 1)[0:ch].astype(bf16)
                        row = jnp.where((lane_ch == 0) | (lane_ch == LANES - 1), ends, row)
                    grid[1 + 2 * i + h, j * SLOT : j * SLOT + ch, :] = row
            return carry

        lax.fori_loop(q * part, (q + 1) * part, pack, 0)
        if layer == 1 and q in (0, CHUNKS - 1):
            for j in range(PEERS):
                grid[nr if q else 1, j * SLOT : j * SLOT + ch, :] = fix[j, 1 if q else 0]
        total = conv_rows(layer, [[grid[low + n + a] for a in range(3)] for n in range(count)])
        for n in range(count):
            sums[low + n] = add_columns(total[:, n * LANES : (n + 1) * LANES])

    def gelu(v):
        v = v + biases[0]
        return 0.5 * v * (1.0 + jnp.tanh(math.sqrt(2.0 / math.pi) * (v + 0.044715 * (v * v * v))))

    def hidden_inside(q):
        def one_part(i, carry):
            cols = sums_cols[...]
            for n in range(2):
                for h in range(2):
                    r = 2 * (2 * i + n) + h
                    row = sums[r]
                    share[1, 0, 2 * i + n, h] = (gelu(row) * mask_row(r))[0:ch].astype(bf16)
                    cols = put_cols(r, row, cols)
            sums_cols[...] = cols
            return carry

        lax.fori_loop(q * part // 2, (q + 1) * part // 2, one_part, 0)
        send_own(1, q)

    def layer_sums(layer):
        def near(p):
            z_copy(layer, 0, p).wait_recv()
            z_copy(layer, 4, p).start()
            if p == 0:
                z_copy(layer, 6, p).start()
            z_copy(layer, 1, p).wait_recv()
            z_copy(layer, 5, p).start()
            z_copy(layer, 7, p).start()
            s_copy(layer, zs - 2, p).start()
            s_copy(layer, 2, p).start()
            for n, o in ((2, zs - 1), (3, 1)):
                z_copy(layer, n, p).wait_recv()
                s_copy(layer, o, p).start()

        def far(p):
            for n, o in ((4, zs - 3), (5, 3)):
                z_copy(layer, n, p).wait_recv()
                s_copy(layer, o, p).start()
            for copy in far_copies(layer, p):
                copy.wait_recv()
            s_copy(layer, 4, p).start()

        def along_x(p):
            for o in range(zs):
                s_copy(layer, o, p, False).wait_recv()

            def one_slot(v, carry):
                (build_rows, build_cols)[p](layer, v)
                return carry

            lax.fori_loop(0, xs, one_slot, 0)
            for o in range(1, xs):
                u_copy(layer, o, p).start()
            slots_x[layer][p][x] = slots[p][layer, x]

        def along_y(p):
            for o in range(1, xs):
                u_copy(layer, o, p).wait_recv()
            (merge_rows, merge_cols)[p](layer)
            for o in range(1, PEERS):
                h_copy(layer, o, p).start()

        near(0)
        near(1)
        far(0)
        gather(layer, 0)
        far(1)
        along_x(0)
        gather(layer, 1)
        along_x(1)
        gather(layer, 2)
        along_y(0)
        gather(layer, 3)
        along_y(1)
        if layer == 1:
            for p in range(2):
                for o in range(1, PEERS):
                    f_copy(o, p).wait_recv()
            for j in range(PEERS):
                fix_f[j, 0:ch, :] = fix[j, 2].astype(f32)
        conv_chunk(layer, 0, 1, rows_of - 2)
        for q in range(1, CHUNKS):
            conv_chunk(layer, q, q * rows_of - 1, rows_of)
            if layer == 0:
                hidden_inside(q - 1)
        if layer == 0:
            hidden_inside(CHUNKS - 1)
        for p in range(2):
            for o in range(1, PEERS):
                h_copy(layer, o, p).wait_recv()
        for j in range(PEERS):
            block = slice(j * SLOT, j * SLOT + ch)
            grid[0, block, :] = halo[layer, j, 0]
            grid[nr + 1, block, :] = halo[layer, j, 1]
            sides_k[block, :] = halo[layer, j, 2].astype(f32)
        frame = sides_k[...]
        column = [v.astype(bf16) for v in (pltpu.roll(frame, 2, 1), frame, pltpu.roll(frame, LANES - 2, 1))]
        total = conv_rows(layer, [[grid[r + a] for a in range(3)] for r in (0, nr - 1)] + [column])
        sums[0] = add_columns(total[:, 0:LANES])
        sums[nr - 1] = add_columns(total[:, LANES : 2 * LANES])
        return jnp.where((lane & 1) == 1, total[0:chp, 2 * LANES :], total[2 * chp : 3 * chp, 2 * LANES :])

    def turn(columns, r):
        return pltpu.roll(columns, 123 - 2 * r, 1)

    def full_row(r, below, this):
        return sums[r] + jnp.where(lane == 0, below, jnp.where(lane == LANES - 1, this, 0.0))

    columns_0 = layer_sums(0)

    cols = sums_cols[...]
    for n, r in enumerate((0, nr - 1)):
        row = full_row(r, turn(columns_0, r - 1), turn(columns_0, r))
        row16 = (gelu(row) * mask_row(r))[0:ch].astype(bf16)
        rows_1[me, n] = row16
        fix[0, n] = row16
        cols = put_cols(r, sums[r], cols)
    send_ring(1, 0)
    frame = jnp.where((lane & 1) == 1, pltpu.roll(columns_0, LANES - 1, 1), pltpu.roll(columns_0, 1, 1))
    cols16 = (gelu(cols + frame) * mask_cols[0:1, :])[0:ch].astype(bf16)
    cols_1[me, 0] = cols16
    fix[0, 2] = cols16
    send_ring(1, 1)
    for p in range(2):
        for o in range(1, PEERS):
            f_copy(o, p).start()

    columns_1 = layer_sums(1)

    def final_chunk(q, carry):
        below = turn(columns_1, q * rows_of - 1)
        for i in range(part):
            for h in range(2):
                r = 2 * (q * part + i) + h
                this = turn(columns_1, r)
                own = share[0, 0, q * part + i, h].astype(f32)
                v = own + (full_row(r, below, this) + biases[1])[0:ch]
                flat[pl.ds(r, ch, stride=nr), :] = v * mask_row(r)
                below = this
        return carry

    lax.fori_loop(0, CHUNKS, final_chunk, 0)
    out[0] = flat[0 : ch * nr].reshape(ch, nr, LANES).astype(bf16)

    for o in range(1, xs):
        t_copy(o).wait_send()
    for p in range(2):
        for o in range(1, PEERS):
            f_copy(o, p).wait_send()
    for layer in range(2):
        for n in range(4):
            for q in range(CHUNKS):
                y_copy(layer, n, q).wait_send()
        for p in range(2):
            for n in range(6):
                z_copy(layer, n, p).wait_send()
            for copy in far_copies(layer, p):
                copy.wait_send()
            for o in range(zs):
                s_copy(layer, o, p).wait_send()
            for o in range(1, xs):
                u_copy(layer, o, p).wait_send()
            for o in range(1, PEERS):
                h_copy(layer, o, p).wait_send()


def build(mesh, xs, zs):
    def body(state, w1, b1, w2, b2, wet, nb, fold):
        ch, nr = state.shape[1], state.shape[2]
        chp = -(-ch // 8) * 8
        pairs = nr // 2
        f32, bf16 = jnp.float32, jnp.bfloat16
        vmem, dma = pltpu.VMEM, pltpu.SemaphoreType.DMA
        inside = pl.BlockSpec(memory_space=pltpu.VMEM)
        return pl.pallas_call(
            functools.partial(body_kernel, (xs, zs, ch, chp, nr)),
            out_shape=jax.ShapeDtypeStruct(state.shape, bf16),
            in_specs=[pl.BlockSpec(memory_space=pl.ANY)] * 8,
            out_specs=inside,
            scratch_shapes=[
                vmem(state.shape, bf16),
                vmem((9, ch, PEERS * ch), bf16),
                vmem((1, ch), f32),
                vmem((9, ch, PEERS * ch), bf16),
                vmem((1, ch), f32),
                vmem(wet.shape, jnp.int32),
                vmem(nb.shape, jnp.int32),
                vmem(fold.shape, jnp.int32),
                vmem((chp * nr, LANES), f32),
                vmem((2, PEERS, pairs, 2, ch, LANES), bf16),
                vmem((nr + 2, PEERS * SLOT, LANES), bf16),
                vmem((PEERS * SLOT, LANES), f32),
                vmem((3 * chp, 3 * PEERS * SLOT), f32),
                vmem((2, 3 * chp, 3 * PEERS * SLOT), bf16),
                vmem((nr, chp, LANES), f32),
                vmem((2 * zs, 2, ch, LANES), bf16),
                vmem((2 * zs, 2, ch, LANES), bf16),
                vmem((2 * zs, 1, ch, LANES), bf16),
                vmem((2 * zs, 1, ch, LANES), bf16),
                vmem((2, xs, 2, ch, LANES), bf16),
                vmem((2, xs, 1, ch, LANES), bf16),
                vmem((xs, 2, ch, LANES), bf16),
                vmem((xs, 2, ch, LANES), bf16),
                vmem((xs, 1, ch, LANES), bf16),
                vmem((xs, 1, ch, LANES), bf16),
                vmem((2, PEERS, 3, ch, LANES), bf16),
                vmem((PEERS, 3, ch, LANES), bf16),
                vmem((PEERS, chp, LANES), f32),
                vmem((8, LANES), f32),
                vmem((chp, LANES), f32),
                vmem((8, LANES), jnp.int32),
                vmem((xs, 8, LANES), jnp.int32),
                pltpu.SMEM((xs, 8, LANES), jnp.int32),
                dma((2, 4, CHUNKS)),
                dma((2, 4, CHUNKS)),
                dma((2, 2, PEERS)),
                dma((2, 2, PEERS)),
                dma((2, PEERS)),
                dma((2, PEERS)),
                dma((2, 2, 8)),
                dma((2, 2, 8)),
                dma((2, 2, zs)),
                dma((2, 2, zs)),
                dma((2, 2, xs)),
                dma((2, 2, xs)),
                dma((xs,)),
                dma((xs,)),
                dma((9,)),
            ],
            compiler_params=pltpu.CompilerParams(
                collective_id=0, has_side_effects=True, vmem_limit_bytes=63 * 1024 * 1024
            ),
        )(
            state,
            jnp.swapaxes(w1, 1, 2),
            b1.reshape(1, -1),
            jnp.swapaxes(w2, 1, 2),
            b2.reshape(1, -1),
            wet,
            nb,
            fold,
        )

    return jax.shard_map(
        body,
        mesh=mesh,
        in_specs=(
            P("tiles", "chan", None, None),
            P(None, None, "chan"),
            P("chan"),
            P(None, None, "chan"),
            P("chan"),
            P("tiles", None, None),
            P("tiles", None),
            P("tiles", None),
        ),
        out_specs=P("tiles", "chan", None, None),
        check_vma=False,
    )


def solution(mesh):
    return build(mesh, X_SIZE, Z_SIZE)
```

```python
import functools
import math

import jax
import jax.numpy as jnp
from jax import lax
from jax.experimental import pallas as pl
from jax.experimental.pallas import tpu as pltpu
from jax.sharding import PartitionSpec as P

MESH = pl.DeviceIdType.MESH
LANES = 128
SLOT = 64
PEERS = 4
X_SIZE = 4
Z_SIZE = 8
CHUNKS = 4


def body_kernel(
    geo,
    state_at,
    w1_at,
    b1_at,
    w2_at,
    b2_at,
    wet_at,
    nb_at,
    fold_at,
    out,
    state,
    w1,
    b1,
    w2,
    b2,
    wet,
    nb,
    fold,
    flat,
    share,
    grid,
    sides_k,
    taps_f,
    taps,
    sums,
    rows_0,
    rows_1,
    cols_0,
    cols_1,
    slots_rows,
    slots_cols,
    rows_x0,
    rows_x1,
    cols_x0,
    cols_x1,
    halo,
    fix,
    fix_f,
    mask_cols,
    sums_cols,
    table_own,
    table,
    table_s,
    y_send,
    y_recv,
    h_send,
    h_recv,
    f_send,
    f_recv,
    z_send,
    z_recv,
    s_send,
    s_recv,
    u_send,
    u_recv,
    t_send,
    t_recv,
    local_sem,
):
    xs, zs, ch, chp, nr = geo
    ring = (rows_0, cols_0), (rows_1, cols_1)
    slots = slots_rows, slots_cols
    slots_x = (rows_x0, cols_x0), (rows_x1, cols_x1)
    halo_at = pl.ds(0, 2), pl.ds(2, 1)
    pairs = nr // 2
    part = pairs // CHUNKS
    rows_of = 2 * part
    depth = PEERS * SLOT
    f32, bf16 = jnp.float32, jnp.bfloat16

    t = lax.axis_index("tiles")
    c = lax.axis_index("chan")
    k = lax.rem(t, 2)
    z = lax.rem(t // 2, zs)
    x = t // (2 * zs)
    me = z * 2 + k
    up = lax.rem(c + 1, PEERS)
    down = lax.rem(c + PEERS - 1, PEERS)

    def along_z(o):
        return lax.rem(z + o + zs, zs) * 2 + k

    def z_peer(o):
        return x * zs * 2 + along_z(o)

    def x_peer(o):
        return lax.rem(x + o, xs) * zs * 2 + me

    sibling = t + 1 - 2 * k
    copies = [
        pltpu.make_async_copy(src, dst, local_sem.at[n])
        for n, (src, dst) in enumerate(
            (
                (state_at, state),
                (wet_at, wet),
                (nb_at, nb),
                (fold_at, fold),
                (w1_at, w1),
                (w2_at, w2),
                (b1_at, b1),
                (b2_at, b2),
            )
        )
    ]
    for copy in copies:
        copy.start()
    lane = lax.broadcasted_iota(jnp.int32, (chp, LANES), 1)

    barrier = pltpu.get_barrier_semaphore()
    for o in range(1, PEERS):
        pl.semaphore_signal(barrier, inc=1, device_id=(t, lax.rem(c + o, PEERS)), device_id_type=MESH)
    tiles = [z_peer(o) for o in (2, -2, 1, -1)] + [x_peer(o) for o in range(1, xs)] + [sibling]
    for tile in tiles:
        pl.semaphore_signal(barrier, inc=1, device_id=(tile, c), device_id_type=MESH)

    def remote(src, dst, send, recv, tile, chan):
        return pltpu.make_async_remote_copy(
            src_ref=src, dst_ref=dst, send_sem=send, recv_sem=recv, device_id=(tile, chan), device_id_type=MESH
        )

    def y_copy(layer, n, q):
        src, dst, chan = ((0, 3, up), (0, 1, down), (3, 2, up), (1, 2, down))[n]
        at = (pl.ds(q * part, part),) + (() if n < 2 else (n - 2,))
        return remote(
            share.at[(layer, src) + at],
            share.at[(layer, dst) + at],
            y_send.at[layer, n, q],
            y_recv.at[layer, n, q],
            t,
            chan,
        )

    def z_copy(layer, n, p):
        origin, target = ((0, 2), (0, -2), (0, 1), (0, -1), (-2, 1), (2, -1), (-2, 2), (2, -2))[n]
        at = (along_z(origin),) + ((pl.ds(n - 6, 1),) if n >= 6 and p == 0 else ())
        where = ring[layer][p].at[at]
        return remote(where, where, z_send.at[layer, p, n], z_recv.at[layer, p, n], z_peer(target), c)

    def far_copies(layer, p):
        return [z_copy(layer, n, p) for n in ((6, 7) if p == 0 else (7,))]

    def s_copy(layer, o, p, mine=True):
        where = ring[layer][p].at[along_z(o) if mine else along_z(o) + 1 - 2 * k]
        return remote(where, where, s_send.at[layer, p, o], s_recv.at[layer, p, o], sibling, c)

    def u_copy(layer, o, p):
        return remote(
            slots[p].at[layer, lax.rem(x + o, xs)],
            slots_x[layer][p].at[x],
            u_send.at[layer, p, o],
            u_recv.at[layer, p, o],
            x_peer(o),
            c,
        )

    def t_copy(o):
        return remote(table_own, table.at[x], t_send.at[o], t_recv.at[o], x_peer(o), c)

    def h_copy(layer, o, p):
        return remote(
            halo.at[layer, 0, halo_at[p]],
            halo.at[layer, PEERS - o, halo_at[p]],
            h_send.at[layer, p, o],
            h_recv.at[layer, p, o],
            t,
            lax.rem(c + o, PEERS),
        )

    def f_copy(o, p):
        return remote(
            fix.at[0, halo_at[p]],
            fix.at[PEERS - o, halo_at[p]],
            f_send.at[p, o],
            f_recv.at[p, o],
            t,
            lax.rem(c + o, PEERS),
        )

    grid[...] = jnp.zeros(grid.shape, bf16)
    sides_k[...] = jnp.zeros(sides_k.shape, f32)
    table_own[...] = jnp.zeros((8, LANES), jnp.int32)
    for n in range(4):
        copies[n].wait()
    table_own[0:1, 0:8] = nb[...] * 2 + fold[...]
    flat[0 : ch * nr] = state[0].astype(f32).reshape(ch * nr, LANES)
    flat[ch * nr : chp * nr] = jnp.zeros(((chp - ch) * nr, LANES), f32)

    def put_cols(r, row, sides):
        at = lax.broadcasted_iota(jnp.int32, row.shape, 1)
        return jnp.where((at == 2 * r + 3) | (at == 2 * r + 4), pltpu.roll(row, 2 * r + 4, 1), sides)

    def mask_row(r):
        return wet[0, pl.ds(r, 1), :].astype(f32)

    def load_chunk(q, carry):
        sides, wet_sides = carry
        for i in range(part):
            for h in range(2):
                r = 2 * (q * part + i) + h
                row_mask = mask_row(r)
                row = flat[pl.ds(r, chp, stride=nr), :] * row_mask
                row16 = row[0:ch].astype(bf16)
                share[0, 0, q * part + i, h] = row16
                grid[r + 1, 0:ch, :] = row16
                sides = put_cols(r, row, sides)
                wet_sides = put_cols(r, jnp.broadcast_to(row_mask, (8, LANES)), wet_sides)
        return sides, wet_sides

    def send_own(layer, q):
        for n in range(2):
            y_copy(layer, n, q).start()

    def send_ring(layer, p):
        for n in range(4):
            z_copy(layer, n, p).start()
        s_copy(layer, 0, p).start()

    sides, wet_sides = lax.fori_loop(
        0, CHUNKS, load_chunk, (jnp.zeros((chp, LANES), f32), jnp.zeros((8, LANES), f32))
    )
    mask_cols[...] = wet_sides
    sums_cols[...] = jnp.zeros((chp, LANES), f32)
    sums[0] = jnp.zeros((chp, LANES), f32)
    sums[nr - 1] = jnp.zeros((chp, LANES), f32)
    rows_0[me, 0] = share[0, 0, 0, 0]
    rows_0[me, 1] = share[0, 0, pairs - 1, 1]
    cols_0[me, 0] = sides[0:ch].astype(bf16)

    pl.semaphore_wait(barrier, PEERS - 1 + len(tiles))
    for p in range(2):
        send_ring(0, p)
    for q in range(CHUNKS):
        send_own(0, q)
    for o in range(1, xs):
        t_copy(o).start()

    k_in = lax.broadcasted_iota(jnp.int32, (PEERS * ch, depth), 0)
    k_at = lax.broadcasted_iota(jnp.int32, (PEERS * ch, depth), 1)
    place = jnp.zeros((PEERS * ch, depth), jnp.bool_)
    for j in range(PEERS):
        owner = lax.rem(c + j, PEERS)
        place = place | ((k_at - SLOT * j == k_in - ch * owner) & (k_at >= SLOT * j) & (k_at < SLOT * j + ch))
    place = jnp.where(place, 1.0, 0.0).astype(bf16)
    taps_f[...] = jnp.zeros(taps_f.shape, f32)
    for n in range(4, 8):
        copies[n].wait()
    for layer, w in enumerate((w1, w2)):
        for a in range(3):
            for b in range(3):
                taps_f[b * chp : b * chp + ch, a * depth : (a + 1) * depth] = jnp.dot(
                    w[3 * a + b], place, preferred_element_type=f32
                )
        taps[layer] = taps_f[...].astype(bf16)

    eye = lax.broadcasted_iota(jnp.int32, (chp, ch), 0) == lax.broadcasted_iota(jnp.int32, (chp, ch), 1)

    def bias_column(b):
        spread = jnp.broadcast_to(b[...], (chp, ch))
        return jnp.sum(jnp.where(eye, spread, 0.0), axis=1, keepdims=True)

    biases = bias_column(b1), bias_column(b2)
    flip = jnp.where(
        lax.broadcasted_iota(jnp.int32, (LANES, LANES), 0) + lax.broadcasted_iota(jnp.int32, (LANES, LANES), 1)
        == LANES - 1,
        1.0,
        0.0,
    ).astype(bf16)

    table[x] = table_own[...]
    for o in range(1, xs):
        t_copy(o).wait_recv()
    move = pltpu.make_async_copy(table, table_s, local_sem.at[8])
    move.start()
    move.wait()

    lane_ch = lax.broadcasted_iota(jnp.int32, (ch, LANES), 1)
    odd = (lane_ch & 1) == 1
    east = (~odd) & (lane_ch >= 4) & (lane_ch <= 2 * nr + 2)
    west = odd & (lane_ch >= 3) & (lane_ch <= 2 * nr + 1)

    def read_table(v):
        codes = [table_s[v, 0, n] for n in range(8)]
        return [code >> 1 for code in codes], [code & 1 for code in codes]

    def build_rows(layer, v):
        ids, folds = read_table(v)
        north, south = [lax.rem(jnp.maximum(q, 0), 2 * zs) for q in ids[0:2]]
        edges = ring[layer][0]
        slots_rows[layer, v, 0] = edges[south, 1]
        slots_rows[layer, v, 1] = jnp.where(folds[0] == 1, edges[north, 1], edges[north, 0])

    def build_cols(layer, v):
        ids, folds = read_table(v)
        at = [lax.rem(jnp.maximum(q, 0), 2 * zs) for q in ids]

        def cols(n):
            return ring[layer][1][at[n], 0].astype(f32)

        def corner_top(n, across):
            v = cols(n)
            return jnp.where(folds[n] == 1, pltpu.roll(v, across, 1), pltpu.roll(v, 2 * nr, 1))

        result = jnp.where(odd, cols(3), cols(2))
        result = jnp.where(lane_ch == 2 * nr + 4, corner_top(4, 3), result)
        result = jnp.where(lane_ch == 2 * nr + 3, corner_top(5, 1), result)
        result = jnp.where(lane_ch == 2, pltpu.roll(cols(6), LANES - 2 * nr, 1), result)
        result = jnp.where(lane_ch == 1, pltpu.roll(cols(7), LANES - 2 * nr, 1), result)
        slots_cols[layer, v, 0] = result.astype(bf16)

    def usable(code, value):
        return jnp.where(code >= 0, value, jnp.zeros_like(value))

    def merge_rows(layer):
        ids, folds = read_table(x)
        at = [jnp.maximum(q, 0) // (2 * zs) for q in ids[0:2]]
        edges = slots_x[layer][0]
        halo[layer, 0, 0] = usable(ids[1], edges[at[1], 0])
        north = edges[at[0], 1]
        turned = jnp.dot(north, flip, preferred_element_type=f32).astype(bf16)
        halo[layer, 0, 1] = usable(ids[0], jnp.where(folds[0] == 1, turned, north))

    def merge_cols(layer):
        ids, _ = read_table(x)

        def cols(n):
            return usable(ids[n], slots_x[layer][1][jnp.maximum(ids[n], 0) // (2 * zs), 0].astype(f32))

        result = jnp.where(east, cols(2), 0.0)
        result = jnp.where(west, cols(3), result)
        result = jnp.where(lane_ch == 2 * nr + 4, cols(4), result)
        result = jnp.where(lane_ch == 2 * nr + 3, cols(5), result)
        result = jnp.where(lane_ch == 2, cols(6), result)
        result = jnp.where(lane_ch == 1, cols(7), result)
        halo[layer, 0, 2] = result.astype(bf16)

    def gather(layer, q):
        for n in range(2):
            y_copy(layer, n, q).wait_recv()
            y_copy(layer, n + 2, q).start()

    def conv_rows(layer, columns):
        stacked = jnp.concatenate(
            [jnp.concatenate([column[a] for column in columns], axis=1) for a in range(3)], axis=0
        )
        return jnp.dot(taps[layer], stacked, preferred_element_type=f32)

    def add_columns(total):
        left = jnp.where(lane == 0, 0.0, pltpu.roll(total[0:chp], 1, 1))
        right = jnp.where(lane == LANES - 1, 0.0, pltpu.roll(total[2 * chp : 3 * chp], LANES - 1, 1))
        return total[chp : 2 * chp] + left + right

    def conv_chunk(layer, q, low, count):
        for n in range(2, 4):
            y_copy(layer, n, q).wait_recv()

        def pack(i, carry):
            for h in range(2):
                for j in range(layer == 0, PEERS):
                    row = share[layer, j, i, h]
                    if layer == 1:
                        ends = pltpu.roll(fix_f[j], LANES - 4 - 2 * (2 * i + h), 1)[0:ch].astype(bf16)
                        row = jnp.where((lane_ch == 0) | (lane_ch == LANES - 1), ends, row)
                    grid[1 + 2 * i + h, j * SLOT : j * SLOT + ch, :] = row
            return carry

        lax.fori_loop(q * part, (q + 1) * part, pack, 0)
        if layer == 1 and q in (0, CHUNKS - 1):
            for j in range(PEERS):
                grid[nr if q else 1, j * SLOT : j * SLOT + ch, :] = fix[j, 1 if q else 0]
        total = conv_rows(layer, [[grid[low + n + a] for a in range(3)] for n in range(count)])
        for n in range(count):
            sums[low + n] = add_columns(total[:, n * LANES : (n + 1) * LANES])

    def gelu(v):
        v = v + biases[0]
        return 0.5 * v * (1.0 + jnp.tanh(math.sqrt(2.0 / math.pi) * (v + 0.044715 * (v * v * v))))

    def hidden_inside(q):
        def one_part(i, carry):
            cols = sums_cols[...]
            for n in range(2):
                for h in range(2):
                    r = 2 * (2 * i + n) + h
                    row = sums[r]
                    share[1, 0, 2 * i + n, h] = (gelu(row) * mask_row(r))[0:ch].astype(bf16)
                    cols = put_cols(r, row, cols)
            sums_cols[...] = cols
            return carry

        lax.fori_loop(q * part // 2, (q + 1) * part // 2, one_part, 0)
        send_own(1, q)

    def layer_sums(layer):
        def near(p):
            z_copy(layer, 0, p).wait_recv()
            z_copy(layer, 4, p).start()
            if p == 0:
                z_copy(layer, 6, p).start()
            z_copy(layer, 1, p).wait_recv()
            z_copy(layer, 5, p).start()
            z_copy(layer, 7, p).start()
            s_copy(layer, zs - 2, p).start()
            s_copy(layer, 2, p).start()
            for n, o in ((2, zs - 1), (3, 1)):
                z_copy(layer, n, p).wait_recv()
                s_copy(layer, o, p).start()

        def far(p):
            for n, o in ((4, zs - 3), (5, 3)):
                z_copy(layer, n, p).wait_recv()
                s_copy(layer, o, p).start()
            for copy in far_copies(layer, p):
                copy.wait_recv()
            s_copy(layer, 4, p).start()

        def along_x(p):
            for o in range(zs):
                s_copy(layer, o, p, False).wait_recv()

            def one_slot(v, carry):
                (build_rows, build_cols)[p](layer, v)
                return carry

            lax.fori_loop(0, xs, one_slot, 0)
            for o in range(1, xs):
                u_copy(layer, o, p).start()
            slots_x[layer][p][x] = slots[p][layer, x]

        def along_y(p):
            for o in range(1, xs):
                u_copy(layer, o, p).wait_recv()
            (merge_rows, merge_cols)[p](layer)
            for o in range(1, PEERS):
                h_copy(layer, o, p).start()

        def fixes():
            for p in range(2):
                for o in range(1, PEERS):
                    f_copy(o, p).wait_recv()
            for j in range(PEERS):
                fix_f[j, 0:ch, :] = fix[j, 2].astype(f32)

        def conv(q):
            if q == 0:
                conv_chunk(layer, 0, 1, rows_of - 2)
            else:
                conv_chunk(layer, q, q * rows_of - 1, rows_of)

        if layer == 0:
            near(0)
            near(1)
            far(0)
            gather(layer, 0)
            far(1)
            along_x(0)
            gather(layer, 1)
            along_x(1)
            gather(layer, 2)
            along_y(0)
            gather(layer, 3)
            along_y(1)
            conv(0)
            for q in range(1, CHUNKS):
                conv(q)
                hidden_inside(q - 1)
            hidden_inside(CHUNKS - 1)
        else:
            gather(layer, 0)
            near(0)
            gather(layer, 1)
            near(1)
            far(0)
            gather(layer, 2)
            far(1)
            along_x(0)
            fixes()
            along_x(1)
            gather(layer, 3)
            conv(0)
            conv(1)
            along_y(0)
            along_y(1)
            conv(2)
            conv(3)
        for p in range(2):
            for o in range(1, PEERS):
                h_copy(layer, o, p).wait_recv()
        for j in range(PEERS):
            block = slice(j * SLOT, j * SLOT + ch)
            grid[0, block, :] = halo[layer, j, 0]
            grid[nr + 1, block, :] = halo[layer, j, 1]
            sides_k[block, :] = halo[layer, j, 2].astype(f32)
        frame = sides_k[...]
        column = [v.astype(bf16) for v in (pltpu.roll(frame, 2, 1), frame, pltpu.roll(frame, LANES - 2, 1))]
        total = conv_rows(layer, [[grid[r + a] for a in range(3)] for r in (0, nr - 1)] + [column])
        sums[0] = add_columns(total[:, 0:LANES])
        sums[nr - 1] = add_columns(total[:, LANES : 2 * LANES])
        return jnp.where((lane & 1) == 1, total[0:chp, 2 * LANES :], total[2 * chp : 3 * chp, 2 * LANES :])

    def turn(columns, r):
        return pltpu.roll(columns, 123 - 2 * r, 1)

    def full_row(r, below, this):
        return sums[r] + jnp.where(lane == 0, below, jnp.where(lane == LANES - 1, this, 0.0))

    columns_0 = layer_sums(0)

    cols = sums_cols[...]
    for n, r in enumerate((0, nr - 1)):
        row = full_row(r, turn(columns_0, r - 1), turn(columns_0, r))
        row16 = (gelu(row) * mask_row(r))[0:ch].astype(bf16)
        rows_1[me, n] = row16
        fix[0, n] = row16
        cols = put_cols(r, sums[r], cols)
    send_ring(1, 0)
    frame = jnp.where((lane & 1) == 1, pltpu.roll(columns_0, LANES - 1, 1), pltpu.roll(columns_0, 1, 1))
    cols16 = (gelu(cols + frame) * mask_cols[0:1, :])[0:ch].astype(bf16)
    cols_1[me, 0] = cols16
    fix[0, 2] = cols16
    send_ring(1, 1)
    for p in range(2):
        for o in range(1, PEERS):
            f_copy(o, p).start()

    columns_1 = layer_sums(1)

    def final_chunk(q, carry):
        below = turn(columns_1, q * rows_of - 1)
        for i in range(part):
            for h in range(2):
                r = 2 * (q * part + i) + h
                this = turn(columns_1, r)
                own = share[0, 0, q * part + i, h].astype(f32)
                v = own + (full_row(r, below, this) + biases[1])[0:ch]
                flat[pl.ds(r, ch, stride=nr), :] = v * mask_row(r)
                below = this
        return carry

    lax.fori_loop(0, CHUNKS, final_chunk, 0)
    out[0] = flat[0 : ch * nr].reshape(ch, nr, LANES).astype(bf16)

    for o in range(1, xs):
        t_copy(o).wait_send()
    for p in range(2):
        for o in range(1, PEERS):
            f_copy(o, p).wait_send()
    for layer in range(2):
        for n in range(4):
            for q in range(CHUNKS):
                y_copy(layer, n, q).wait_send()
        for p in range(2):
            for n in range(6):
                z_copy(layer, n, p).wait_send()
            for copy in far_copies(layer, p):
                copy.wait_send()
            for o in range(zs):
                s_copy(layer, o, p).wait_send()
            for o in range(1, xs):
                u_copy(layer, o, p).wait_send()
            for o in range(1, PEERS):
                h_copy(layer, o, p).wait_send()


def build(mesh, xs, zs):
    def body(state, w1, b1, w2, b2, wet, nb, fold):
        ch, nr = state.shape[1], state.shape[2]
        chp = -(-ch // 8) * 8
        pairs = nr // 2
        f32, bf16 = jnp.float32, jnp.bfloat16
        vmem, dma = pltpu.VMEM, pltpu.SemaphoreType.DMA
        inside = pl.BlockSpec(memory_space=pltpu.VMEM)
        return pl.pallas_call(
            functools.partial(body_kernel, (xs, zs, ch, chp, nr)),
            out_shape=jax.ShapeDtypeStruct(state.shape, bf16),
            in_specs=[pl.BlockSpec(memory_space=pl.ANY)] * 8,
            out_specs=inside,
            scratch_shapes=[
                vmem(state.shape, bf16),
                vmem((9, ch, PEERS * ch), bf16),
                vmem((1, ch), f32),
                vmem((9, ch, PEERS * ch), bf16),
                vmem((1, ch), f32),
                vmem(wet.shape, jnp.int32),
                vmem(nb.shape, jnp.int32),
                vmem(fold.shape, jnp.int32),
                vmem((chp * nr, LANES), f32),
                vmem((2, PEERS, pairs, 2, ch, LANES), bf16),
                vmem((nr + 2, PEERS * SLOT, LANES), bf16),
                vmem((PEERS * SLOT, LANES), f32),
                vmem((3 * chp, 3 * PEERS * SLOT), f32),
                vmem((2, 3 * chp, 3 * PEERS * SLOT), bf16),
                vmem((nr, chp, LANES), f32),
                vmem((2 * zs, 2, ch, LANES), bf16),
                vmem((2 * zs, 2, ch, LANES), bf16),
                vmem((2 * zs, 1, ch, LANES), bf16),
                vmem((2 * zs, 1, ch, LANES), bf16),
                vmem((2, xs, 2, ch, LANES), bf16),
                vmem((2, xs, 1, ch, LANES), bf16),
                vmem((xs, 2, ch, LANES), bf16),
                vmem((xs, 2, ch, LANES), bf16),
                vmem((xs, 1, ch, LANES), bf16),
                vmem((xs, 1, ch, LANES), bf16),
                vmem((2, PEERS, 3, ch, LANES), bf16),
                vmem((PEERS, 3, ch, LANES), bf16),
                vmem((PEERS, chp, LANES), f32),
                vmem((8, LANES), f32),
                vmem((chp, LANES), f32),
                vmem((8, LANES), jnp.int32),
                vmem((xs, 8, LANES), jnp.int32),
                pltpu.SMEM((xs, 8, LANES), jnp.int32),
                dma((2, 4, CHUNKS)),
                dma((2, 4, CHUNKS)),
                dma((2, 2, PEERS)),
                dma((2, 2, PEERS)),
                dma((2, PEERS)),
                dma((2, PEERS)),
                dma((2, 2, 8)),
                dma((2, 2, 8)),
                dma((2, 2, zs)),
                dma((2, 2, zs)),
                dma((2, 2, xs)),
                dma((2, 2, xs)),
                dma((xs,)),
                dma((xs,)),
                dma((9,)),
            ],
            compiler_params=pltpu.CompilerParams(
                collective_id=0, has_side_effects=True, vmem_limit_bytes=63 * 1024 * 1024
            ),
        )(
            state,
            jnp.swapaxes(w1, 1, 2),
            b1.reshape(1, -1),
            jnp.swapaxes(w2, 1, 2),
            b2.reshape(1, -1),
            wet,
            nb,
            fold,
        )

    return jax.shard_map(
        body,
        mesh=mesh,
        in_specs=(
            P("tiles", "chan", None, None),
            P(None, None, "chan"),
            P("chan"),
            P(None, None, "chan"),
            P("chan"),
            P("tiles", None, None),
            P("tiles", None),
            P("tiles", None),
        ),
        out_specs=P("tiles", "chan", None, None),
        check_vma=False,
    )


def solution(mesh):
    return build(mesh, X_SIZE, Z_SIZE)
```

```python
import functools
import math

import jax
import jax.numpy as jnp
from jax import lax
from jax.experimental import pallas as pl
from jax.experimental.pallas import tpu as pltpu
from jax.sharding import PartitionSpec as P

MESH = pl.DeviceIdType.MESH
LANES = 128
SLOT = 64
PEERS = 4
X_SIZE = 4
Z_SIZE = 8
CHUNKS = 4


def body_kernel(
    geo,
    state_at,
    w1_at,
    b1_at,
    w2_at,
    b2_at,
    wet_at,
    nb_at,
    fold_at,
    out,
    state,
    w1,
    b1,
    w2,
    b2,
    wet,
    nb,
    fold,
    flat,
    share,
    grid,
    sides_k,
    taps_f,
    taps,
    sums,
    rows_0,
    rows_1,
    cols_0,
    cols_1,
    slots_rows,
    slots_cols,
    rows_x0,
    rows_x1,
    cols_x0,
    cols_x1,
    halo,
    fix,
    fix_f,
    mask_cols,
    sums_cols,
    result,
    table_own,
    table,
    table_s,
    y_send,
    y_recv,
    h_send,
    h_recv,
    f_send,
    f_recv,
    z_send,
    z_recv,
    s_send,
    s_recv,
    u_send,
    u_recv,
    t_send,
    t_recv,
    local_sem,
):
    xs, zs, ch, chp, nr = geo
    ring = (rows_0, cols_0), (rows_1, cols_1)
    slots = slots_rows, slots_cols
    slots_x = (rows_x0, cols_x0), (rows_x1, cols_x1)
    halo_at = pl.ds(0, 2), pl.ds(2, 1)
    pairs = nr // 2
    part = pairs // CHUNKS
    rows_of = 2 * part
    depth = PEERS * SLOT
    f32, bf16 = jnp.float32, jnp.bfloat16

    t = lax.axis_index("tiles")
    c = lax.axis_index("chan")
    k = lax.rem(t, 2)
    z = lax.rem(t // 2, zs)
    x = t // (2 * zs)
    me = z * 2 + k
    up = lax.rem(c + 1, PEERS)
    down = lax.rem(c + PEERS - 1, PEERS)

    def along_z(o):
        return lax.rem(z + o + zs, zs) * 2 + k

    def z_peer(o):
        return x * zs * 2 + along_z(o)

    def x_peer(o):
        return lax.rem(x + o, xs) * zs * 2 + me

    sibling = t + 1 - 2 * k
    copies = [
        pltpu.make_async_copy(src, dst, local_sem.at[n])
        for n, (src, dst) in enumerate(
            (
                (state_at, state),
                (wet_at, wet),
                (nb_at, nb),
                (fold_at, fold),
                (w1_at, w1),
                (w2_at, w2),
                (b1_at, b1),
                (b2_at, b2),
            )
        )
    ]
    for copy in copies:
        copy.start()
    lane = lax.broadcasted_iota(jnp.int32, (chp, LANES), 1)

    barrier = pltpu.get_barrier_semaphore()
    for o in range(1, PEERS):
        pl.semaphore_signal(barrier, inc=1, device_id=(t, lax.rem(c + o, PEERS)), device_id_type=MESH)
    tiles = [z_peer(o) for o in (2, -2, 1, -1)] + [x_peer(o) for o in range(1, xs)] + [sibling]
    for tile in tiles:
        pl.semaphore_signal(barrier, inc=1, device_id=(tile, c), device_id_type=MESH)

    def remote(src, dst, send, recv, tile, chan):
        return pltpu.make_async_remote_copy(
            src_ref=src, dst_ref=dst, send_sem=send, recv_sem=recv, device_id=(tile, chan), device_id_type=MESH
        )

    def y_copy(layer, n, q):
        src, dst, chan = ((0, 3, up), (0, 1, down), (3, 2, up), (1, 2, down))[n]
        at = (pl.ds(q * part, part),) + (() if n < 2 else (n - 2,))
        return remote(
            share.at[(layer, src) + at],
            share.at[(layer, dst) + at],
            y_send.at[layer, n, q],
            y_recv.at[layer, n, q],
            t,
            chan,
        )

    def z_copy(layer, n, p):
        origin, target = ((0, 2), (0, -2), (0, 1), (0, -1), (-2, 1), (2, -1), (-2, 2), (2, -2))[n]
        at = (along_z(origin),) + ((pl.ds(n - 6, 1),) if n >= 6 and p == 0 else ())
        where = ring[layer][p].at[at]
        return remote(where, where, z_send.at[layer, p, n], z_recv.at[layer, p, n], z_peer(target), c)

    def far_copies(layer, p):
        return [z_copy(layer, n, p) for n in ((6, 7) if p == 0 else (7,))]

    def s_copy(layer, o, p, mine=True):
        where = ring[layer][p].at[along_z(o) if mine else along_z(o) + 1 - 2 * k]
        return remote(where, where, s_send.at[layer, p, o], s_recv.at[layer, p, o], sibling, c)

    def u_copy(layer, o, p):
        return remote(
            slots[p].at[layer, lax.rem(x + o, xs)],
            slots_x[layer][p].at[x],
            u_send.at[layer, p, o],
            u_recv.at[layer, p, o],
            x_peer(o),
            c,
        )

    def t_copy(o):
        return remote(table_own, table.at[x], t_send.at[o], t_recv.at[o], x_peer(o), c)

    def h_copy(layer, o, p):
        return remote(
            halo.at[layer, 0, halo_at[p]],
            halo.at[layer, PEERS - o, halo_at[p]],
            h_send.at[layer, p, o],
            h_recv.at[layer, p, o],
            t,
            lax.rem(c + o, PEERS),
        )

    def f_copy(o, p):
        return remote(
            fix.at[0, halo_at[p]],
            fix.at[PEERS - o, halo_at[p]],
            f_send.at[p, o],
            f_recv.at[p, o],
            t,
            lax.rem(c + o, PEERS),
        )

    grid[...] = jnp.zeros(grid.shape, bf16)
    sides_k[...] = jnp.zeros(sides_k.shape, f32)
    table_own[...] = jnp.zeros((8, LANES), jnp.int32)
    for n in range(4):
        copies[n].wait()
    table_own[0:1, 0:8] = nb[...] * 2 + fold[...]
    flat[0 : ch * nr] = state[0].astype(f32).reshape(ch * nr, LANES)
    flat[ch * nr : chp * nr] = jnp.zeros(((chp - ch) * nr, LANES), f32)

    def put_cols(r, row, sides):
        at = lax.broadcasted_iota(jnp.int32, row.shape, 1)
        return jnp.where((at == 2 * r + 3) | (at == 2 * r + 4), pltpu.roll(row, 2 * r + 4, 1), sides)

    def mask_row(r):
        return wet[0, pl.ds(r, 1), :].astype(f32)

    def load_chunk(q, carry):
        sides, wet_sides = carry
        for i in range(part):
            for h in range(2):
                r = 2 * (q * part + i) + h
                row_mask = mask_row(r)
                row = flat[pl.ds(r, chp, stride=nr), :] * row_mask
                row16 = row[0:ch].astype(bf16)
                share[0, 0, q * part + i, h] = row16
                grid[r + 1, 0:ch, :] = row16
                sides = put_cols(r, row, sides)
                wet_sides = put_cols(r, jnp.broadcast_to(row_mask, (8, LANES)), wet_sides)
        return sides, wet_sides

    def send_own(layer, q):
        for n in range(2):
            y_copy(layer, n, q).start()

    def send_ring(layer, p):
        for n in range(4):
            z_copy(layer, n, p).start()
        s_copy(layer, 0, p).start()

    sides, wet_sides = lax.fori_loop(
        0, CHUNKS, load_chunk, (jnp.zeros((chp, LANES), f32), jnp.zeros((8, LANES), f32))
    )
    mask_cols[...] = wet_sides
    sums_cols[...] = jnp.zeros((chp, LANES), f32)
    sums[0] = jnp.zeros((chp, LANES), f32)
    sums[nr - 1] = jnp.zeros((chp, LANES), f32)
    rows_0[me, 0] = share[0, 0, 0, 0]
    rows_0[me, 1] = share[0, 0, pairs - 1, 1]
    cols_0[me, 0] = sides[0:ch].astype(bf16)

    pl.semaphore_wait(barrier, PEERS - 1 + len(tiles))
    for p in range(2):
        send_ring(0, p)
    for q in range(CHUNKS):
        send_own(0, q)
    for o in range(1, xs):
        t_copy(o).start()

    k_in = lax.broadcasted_iota(jnp.int32, (PEERS * ch, depth), 0)
    k_at = lax.broadcasted_iota(jnp.int32, (PEERS * ch, depth), 1)
    place = jnp.zeros((PEERS * ch, depth), jnp.bool_)
    for j in range(PEERS):
        owner = lax.rem(c + j, PEERS)
        place = place | ((k_at - SLOT * j == k_in - ch * owner) & (k_at >= SLOT * j) & (k_at < SLOT * j + ch))
    place = jnp.where(place, 1.0, 0.0).astype(bf16)
    taps_f[...] = jnp.zeros(taps_f.shape, f32)
    for n in range(4, 8):
        copies[n].wait()
    for layer, w in enumerate((w1, w2)):
        for a in range(3):
            for b in range(3):
                taps_f[b * chp : b * chp + ch, a * depth : (a + 1) * depth] = jnp.dot(
                    w[3 * a + b], place, preferred_element_type=f32
                )
        taps[layer] = taps_f[...].astype(bf16)

    eye = lax.broadcasted_iota(jnp.int32, (chp, ch), 0) == lax.broadcasted_iota(jnp.int32, (chp, ch), 1)

    def bias_column(b):
        spread = jnp.broadcast_to(b[...], (chp, ch))
        return jnp.sum(jnp.where(eye, spread, 0.0), axis=1, keepdims=True)

    biases = bias_column(b1), bias_column(b2)
    flip = jnp.where(
        lax.broadcasted_iota(jnp.int32, (LANES, LANES), 0) + lax.broadcasted_iota(jnp.int32, (LANES, LANES), 1)
        == LANES - 1,
        1.0,
        0.0,
    ).astype(bf16)

    table[x] = table_own[...]
    for o in range(1, xs):
        t_copy(o).wait_recv()
    move = pltpu.make_async_copy(table, table_s, local_sem.at[8])
    move.start()
    move.wait()

    lane_ch = lax.broadcasted_iota(jnp.int32, (ch, LANES), 1)
    odd = (lane_ch & 1) == 1
    east = (~odd) & (lane_ch >= 4) & (lane_ch <= 2 * nr + 2)
    west = odd & (lane_ch >= 3) & (lane_ch <= 2 * nr + 1)

    def read_table(v):
        codes = [table_s[v, 0, n] for n in range(8)]
        return [code >> 1 for code in codes], [code & 1 for code in codes]

    def build_rows(layer, v):
        ids, folds = read_table(v)
        north, south = [lax.rem(jnp.maximum(q, 0), 2 * zs) for q in ids[0:2]]
        edges = ring[layer][0]
        slots_rows[layer, v, 0] = edges[south, 1]
        slots_rows[layer, v, 1] = jnp.where(folds[0] == 1, edges[north, 1], edges[north, 0])

    def build_cols(layer, v):
        ids, folds = read_table(v)
        at = [lax.rem(jnp.maximum(q, 0), 2 * zs) for q in ids]

        def cols(n):
            return ring[layer][1][at[n], 0].astype(f32)

        def corner_top(n, across):
            v = cols(n)
            return jnp.where(folds[n] == 1, pltpu.roll(v, across, 1), pltpu.roll(v, 2 * nr, 1))

        result = jnp.where(odd, cols(3), cols(2))
        result = jnp.where(lane_ch == 2 * nr + 4, corner_top(4, 3), result)
        result = jnp.where(lane_ch == 2 * nr + 3, corner_top(5, 1), result)
        result = jnp.where(lane_ch == 2, pltpu.roll(cols(6), LANES - 2 * nr, 1), result)
        result = jnp.where(lane_ch == 1, pltpu.roll(cols(7), LANES - 2 * nr, 1), result)
        slots_cols[layer, v, 0] = result.astype(bf16)

    def usable(code, value):
        return jnp.where(code >= 0, value, jnp.zeros_like(value))

    def merge_rows(layer):
        ids, folds = read_table(x)
        at = [jnp.maximum(q, 0) // (2 * zs) for q in ids[0:2]]
        edges = slots_x[layer][0]
        halo[layer, 0, 0] = usable(ids[1], edges[at[1], 0])
        north = edges[at[0], 1]
        turned = jnp.dot(north, flip, preferred_element_type=f32).astype(bf16)
        halo[layer, 0, 1] = usable(ids[0], jnp.where(folds[0] == 1, turned, north))

    def merge_cols(layer):
        ids, _ = read_table(x)

        def cols(n):
            return usable(ids[n], slots_x[layer][1][jnp.maximum(ids[n], 0) // (2 * zs), 0].astype(f32))

        result = jnp.where(east, cols(2), 0.0)
        result = jnp.where(west, cols(3), result)
        result = jnp.where(lane_ch == 2 * nr + 4, cols(4), result)
        result = jnp.where(lane_ch == 2 * nr + 3, cols(5), result)
        result = jnp.where(lane_ch == 2, cols(6), result)
        result = jnp.where(lane_ch == 1, cols(7), result)
        halo[layer, 0, 2] = result.astype(bf16)

    def gather(layer, q):
        for n in range(2):
            y_copy(layer, n, q).wait_recv()
            y_copy(layer, n + 2, q).start()

    def conv_rows(layer, columns):
        stacked = jnp.concatenate(
            [jnp.concatenate([column[a] for column in columns], axis=1) for a in range(3)], axis=0
        )
        return jnp.dot(taps[layer], stacked, preferred_element_type=f32)

    def add_columns(total):
        left = jnp.where(lane == 0, 0.0, pltpu.roll(total[0:chp], 1, 1))
        right = jnp.where(lane == LANES - 1, 0.0, pltpu.roll(total[2 * chp : 3 * chp], LANES - 1, 1))
        return total[chp : 2 * chp] + left + right

    def conv_chunk(layer, q, low, count):
        for n in range(2, 4):
            y_copy(layer, n, q).wait_recv()

        def pack(i, carry):
            for h in range(2):
                for j in range(layer == 0, PEERS):
                    row = share[layer, j, i, h]
                    if layer == 1:
                        ends = pltpu.roll(fix_f[j], LANES - 4 - 2 * (2 * i + h), 1)[0:ch].astype(bf16)
                        row = jnp.where((lane_ch == 0) | (lane_ch == LANES - 1), ends, row)
                    grid[1 + 2 * i + h, j * SLOT : j * SLOT + ch, :] = row
            return carry

        lax.fori_loop(q * part, (q + 1) * part, pack, 0)
        if layer == 1 and q in (0, CHUNKS - 1):
            for j in range(PEERS):
                grid[nr if q else 1, j * SLOT : j * SLOT + ch, :] = fix[j, 1 if q else 0]
        total = conv_rows(layer, [[grid[low + n + a] for a in range(3)] for n in range(count)])
        for n in range(count):
            sums[low + n] = add_columns(total[:, n * LANES : (n + 1) * LANES])

    def gelu(v):
        v = v + biases[0]
        return 0.5 * v * (1.0 + jnp.tanh(math.sqrt(2.0 / math.pi) * (v + 0.044715 * (v * v * v))))

    def hidden_inside(q):
        def one_part(i, carry):
            cols = sums_cols[...]
            for n in range(2):
                for h in range(2):
                    r = 2 * (2 * i + n) + h
                    row = sums[r]
                    share[1, 0, 2 * i + n, h] = (gelu(row) * mask_row(r))[0:ch].astype(bf16)
                    cols = put_cols(r, row, cols)
            sums_cols[...] = cols
            return carry

        lax.fori_loop(q * part // 2, (q + 1) * part // 2, one_part, 0)
        send_own(1, q)

    def layer_sums(layer):
        def near(p):
            z_copy(layer, 0, p).wait_recv()
            z_copy(layer, 4, p).start()
            if p == 0:
                z_copy(layer, 6, p).start()
            z_copy(layer, 1, p).wait_recv()
            z_copy(layer, 5, p).start()
            z_copy(layer, 7, p).start()
            s_copy(layer, zs - 2, p).start()
            s_copy(layer, 2, p).start()
            for n, o in ((2, zs - 1), (3, 1)):
                z_copy(layer, n, p).wait_recv()
                s_copy(layer, o, p).start()

        def far(p):
            for n, o in ((4, zs - 3), (5, 3)):
                z_copy(layer, n, p).wait_recv()
                s_copy(layer, o, p).start()
            for copy in far_copies(layer, p):
                copy.wait_recv()
            s_copy(layer, 4, p).start()

        def along_x(p):
            for o in range(zs):
                s_copy(layer, o, p, False).wait_recv()

            def one_slot(v, carry):
                (build_rows, build_cols)[p](layer, v)
                return carry

            lax.fori_loop(0, xs, one_slot, 0)
            for o in range(1, xs):
                u_copy(layer, o, p).start()
            slots_x[layer][p][x] = slots[p][layer, x]

        def along_y(p):
            for o in range(1, xs):
                u_copy(layer, o, p).wait_recv()
            (merge_rows, merge_cols)[p](layer)
            for o in range(1, PEERS):
                h_copy(layer, o, p).start()

        def fixes():
            for p in range(2):
                for o in range(1, PEERS):
                    f_copy(o, p).wait_recv()
            for j in range(PEERS):
                fix_f[j, 0:ch, :] = fix[j, 2].astype(f32)

        def conv(q):
            if q == 0:
                conv_chunk(layer, 0, 1, rows_of - 2)
            else:
                conv_chunk(layer, q, q * rows_of - 1, rows_of)

        if layer == 0:
            near(0)
            near(1)
            far(0)
            gather(layer, 0)
            far(1)
            along_x(0)
            gather(layer, 1)
            along_x(1)
            gather(layer, 2)
            along_y(0)
            gather(layer, 3)
            along_y(1)
            conv(0)
            for q in range(1, CHUNKS):
                conv(q)
                hidden_inside(q - 1)
            hidden_inside(CHUNKS - 1)
        else:
            gather(layer, 0)
            near(0)
            gather(layer, 1)
            near(1)
            far(0)
            gather(layer, 2)
            far(1)
            along_x(0)
            fixes()
            along_x(1)
            gather(layer, 3)
            conv(0)
            conv(1)
            along_y(0)
            along_y(1)
            conv(2)
            conv(3)
        for p in range(2):
            for o in range(1, PEERS):
                h_copy(layer, o, p).wait_recv()
        for j in range(PEERS):
            block = slice(j * SLOT, j * SLOT + ch)
            grid[0, block, :] = halo[layer, j, 0]
            grid[nr + 1, block, :] = halo[layer, j, 1]
            sides_k[block, :] = halo[layer, j, 2].astype(f32)
        frame = sides_k[...]
        column = [v.astype(bf16) for v in (pltpu.roll(frame, 2, 1), frame, pltpu.roll(frame, LANES - 2, 1))]
        total = conv_rows(layer, [[grid[r + a] for a in range(3)] for r in (0, nr - 1)] + [column])
        sums[0] = add_columns(total[:, 0:LANES])
        sums[nr - 1] = add_columns(total[:, LANES : 2 * LANES])
        return jnp.where((lane & 1) == 1, total[0:chp, 2 * LANES :], total[2 * chp : 3 * chp, 2 * LANES :])

    def turn(columns, r):
        return pltpu.roll(columns, 123 - 2 * r, 1)

    def full_row(r, below, this):
        return sums[r] + jnp.where(lane == 0, below, jnp.where(lane == LANES - 1, this, 0.0))

    columns_0 = layer_sums(0)

    cols = sums_cols[...]
    for n, r in enumerate((0, nr - 1)):
        row = full_row(r, turn(columns_0, r - 1), turn(columns_0, r))
        row16 = (gelu(row) * mask_row(r))[0:ch].astype(bf16)
        rows_1[me, n] = row16
        fix[0, n] = row16
        cols = put_cols(r, sums[r], cols)
    send_ring(1, 0)
    frame = jnp.where((lane & 1) == 1, pltpu.roll(columns_0, LANES - 1, 1), pltpu.roll(columns_0, 1, 1))
    cols16 = (gelu(cols + frame) * mask_cols[0:1, :])[0:ch].astype(bf16)
    cols_1[me, 0] = cols16
    fix[0, 2] = cols16
    send_ring(1, 1)
    for p in range(2):
        for o in range(1, PEERS):
            f_copy(o, p).start()

    columns_1 = layer_sums(1)

    def final_chunk(q, carry):
        below = turn(columns_1, q * rows_of - 1)
        for i in range(part):
            for h in range(2):
                r = 2 * (q * part + i) + h
                this = turn(columns_1, r)
                own = share[0, 0, q * part + i, h].astype(f32)
                v = own + (full_row(r, below, this) + biases[1])[0:ch]
                flat[pl.ds(r, ch, stride=nr), :] = v * mask_row(r)
                below = this
        return carry

    results = []
    for part_of in range(2):
        lax.fori_loop(part_of * CHUNKS // 2, (part_of + 1) * CHUNKS // 2, final_chunk, 0)
        low = part_of * nr // 2
        result[:, low : low + nr // 2, :] = flat[0 : ch * nr].reshape(ch, nr, LANES)[:, low : low + nr // 2].astype(bf16)
        rows = pl.ds(low, nr // 2)
        results.append(
            pltpu.make_async_copy(result.at[:, rows, :], out.at[0, :, rows, :], local_sem.at[9 + part_of])
        )
        results[-1].start()

    for copy in results:
        copy.wait()
    for o in range(1, xs):
        t_copy(o).wait_send()
    for p in range(2):
        for o in range(1, PEERS):
            f_copy(o, p).wait_send()
    for layer in range(2):
        for n in range(4):
            for q in range(CHUNKS):
                y_copy(layer, n, q).wait_send()
        for p in range(2):
            for n in range(6):
                z_copy(layer, n, p).wait_send()
            for copy in far_copies(layer, p):
                copy.wait_send()
            for o in range(zs):
                s_copy(layer, o, p).wait_send()
            for o in range(1, xs):
                u_copy(layer, o, p).wait_send()
            for o in range(1, PEERS):
                h_copy(layer, o, p).wait_send()


def build(mesh, xs, zs):
    def body(state, w1, b1, w2, b2, wet, nb, fold):
        ch, nr = state.shape[1], state.shape[2]
        chp = -(-ch // 8) * 8
        pairs = nr // 2
        f32, bf16 = jnp.float32, jnp.bfloat16
        vmem, dma = pltpu.VMEM, pltpu.SemaphoreType.DMA
        return pl.pallas_call(
            functools.partial(body_kernel, (xs, zs, ch, chp, nr)),
            out_shape=jax.ShapeDtypeStruct(state.shape, bf16),
            in_specs=[pl.BlockSpec(memory_space=pl.ANY)] * 8,
            out_specs=pl.BlockSpec(memory_space=pl.ANY),
            scratch_shapes=[
                vmem(state.shape, bf16),
                vmem((9, ch, PEERS * ch), bf16),
                vmem((1, ch), f32),
                vmem((9, ch, PEERS * ch), bf16),
                vmem((1, ch), f32),
                vmem(wet.shape, jnp.int32),
                vmem(nb.shape, jnp.int32),
                vmem(fold.shape, jnp.int32),
                vmem((chp * nr, LANES), f32),
                vmem((2, PEERS, pairs, 2, ch, LANES), bf16),
                vmem((nr + 2, PEERS * SLOT, LANES), bf16),
                vmem((PEERS * SLOT, LANES), f32),
                vmem((3 * chp, 3 * PEERS * SLOT), f32),
                vmem((2, 3 * chp, 3 * PEERS * SLOT), bf16),
                vmem((nr, chp, LANES), f32),
                vmem((2 * zs, 2, ch, LANES), bf16),
                vmem((2 * zs, 2, ch, LANES), bf16),
                vmem((2 * zs, 1, ch, LANES), bf16),
                vmem((2 * zs, 1, ch, LANES), bf16),
                vmem((2, xs, 2, ch, LANES), bf16),
                vmem((2, xs, 1, ch, LANES), bf16),
                vmem((xs, 2, ch, LANES), bf16),
                vmem((xs, 2, ch, LANES), bf16),
                vmem((xs, 1, ch, LANES), bf16),
                vmem((xs, 1, ch, LANES), bf16),
                vmem((2, PEERS, 3, ch, LANES), bf16),
                vmem((PEERS, 3, ch, LANES), bf16),
                vmem((PEERS, chp, LANES), f32),
                vmem((8, LANES), f32),
                vmem((chp, LANES), f32),
                vmem((ch, nr, LANES), bf16),
                vmem((8, LANES), jnp.int32),
                vmem((xs, 8, LANES), jnp.int32),
                pltpu.SMEM((xs, 8, LANES), jnp.int32),
                dma((2, 4, CHUNKS)),
                dma((2, 4, CHUNKS)),
                dma((2, 2, PEERS)),
                dma((2, 2, PEERS)),
                dma((2, PEERS)),
                dma((2, PEERS)),
                dma((2, 2, 8)),
                dma((2, 2, 8)),
                dma((2, 2, zs)),
                dma((2, 2, zs)),
                dma((2, 2, xs)),
                dma((2, 2, xs)),
                dma((xs,)),
                dma((xs,)),
                dma((11,)),
            ],
            compiler_params=pltpu.CompilerParams(
                collective_id=0, has_side_effects=True, vmem_limit_bytes=63 * 1024 * 1024
            ),
        )(
            state,
            jnp.swapaxes(w1, 1, 2),
            b1.reshape(1, -1),
            jnp.swapaxes(w2, 1, 2),
            b2.reshape(1, -1),
            wet,
            nb,
            fold,
        )

    return jax.shard_map(
        body,
        mesh=mesh,
        in_specs=(
            P("tiles", "chan", None, None),
            P(None, None, "chan"),
            P("chan"),
            P(None, None, "chan"),
            P("chan"),
            P("tiles", None, None),
            P("tiles", None),
            P("tiles", None),
        ),
        out_specs=P("tiles", "chan", None, None),
        check_vma=False,
    )


def solution(mesh):
    return build(mesh, X_SIZE, Z_SIZE)
```

```python
import functools
import math

import jax
import jax.numpy as jnp
from jax import lax
from jax.experimental import pallas as pl
from jax.experimental.pallas import tpu as pltpu
from jax.sharding import PartitionSpec as P

MESH = pl.DeviceIdType.MESH
LANES = 128
SLOT = 64
PEERS = 4
X_SIZE = 4
Z_SIZE = 8
CHUNKS = 4


def body_kernel(
    geo,
    state_at,
    w1_at,
    b1_at,
    w2_at,
    b2_at,
    wet_at,
    nb_at,
    fold_at,
    out,
    state,
    w1,
    b1,
    w2,
    b2,
    wet,
    nb,
    fold,
    flat,
    share,
    grid,
    sides_k,
    taps_f,
    taps,
    sums,
    rows_0,
    rows_1,
    cols_0,
    cols_1,
    slots_rows,
    slots_cols,
    rows_x0,
    rows_x1,
    cols_x0,
    cols_x1,
    halo,
    fix,
    fix_f,
    mask_cols,
    sums_cols,
    result,
    table_own,
    table,
    table_s,
    y_send,
    y_recv,
    h_send,
    h_recv,
    f_send,
    f_recv,
    z_send,
    z_recv,
    s_send,
    s_recv,
    u_send,
    u_recv,
    t_send,
    t_recv,
    local_sem,
):
    xs, zs, ch, chp, nr = geo
    ring = (rows_0, cols_0), (rows_1, cols_1)
    slots = slots_rows, slots_cols
    slots_x = (rows_x0, cols_x0), (rows_x1, cols_x1)
    halo_at = pl.ds(0, 2), pl.ds(2, 1)
    pairs = nr // 2
    part = pairs // CHUNKS
    rows_of = 2 * part
    depth = PEERS * SLOT
    f32, bf16 = jnp.float32, jnp.bfloat16

    t = lax.axis_index("tiles")
    c = lax.axis_index("chan")
    k = lax.rem(t, 2)
    z = lax.rem(t // 2, zs)
    x = t // (2 * zs)
    me = z * 2 + k
    up = lax.rem(c + 1, PEERS)
    down = lax.rem(c + PEERS - 1, PEERS)

    def along_z(o):
        return lax.rem(z + o + zs, zs) * 2 + k

    def z_peer(o):
        return x * zs * 2 + along_z(o)

    def x_peer(o):
        return lax.rem(x + o, xs) * zs * 2 + me

    sibling = t + 1 - 2 * k
    copies = [
        pltpu.make_async_copy(src, dst, local_sem.at[n])
        for n, (src, dst) in enumerate(
            (
                (state_at, state),
                (wet_at, wet),
                (nb_at, nb),
                (fold_at, fold),
                (w1_at, w1),
                (w2_at, w2),
                (b1_at, b1),
                (b2_at, b2),
            )
        )
    ]
    for copy in copies:
        copy.start()
    lane = lax.broadcasted_iota(jnp.int32, (chp, LANES), 1)

    barrier = pltpu.get_barrier_semaphore()
    for o in range(1, PEERS):
        pl.semaphore_signal(barrier, inc=1, device_id=(t, lax.rem(c + o, PEERS)), device_id_type=MESH)
    tiles = [z_peer(o) for o in (2, -2, 1, -1)] + [x_peer(o) for o in range(1, xs)] + [sibling]
    for tile in tiles:
        pl.semaphore_signal(barrier, inc=1, device_id=(tile, c), device_id_type=MESH)

    def remote(src, dst, send, recv, tile, chan):
        return pltpu.make_async_remote_copy(
            src_ref=src, dst_ref=dst, send_sem=send, recv_sem=recv, device_id=(tile, chan), device_id_type=MESH
        )

    def y_copy(layer, n, q):
        src, dst, chan = ((0, 3, up), (0, 1, down), (3, 2, up), (1, 2, down))[n]
        at = (pl.ds(q * part, part),) + (() if n < 2 else (n - 2,))
        return remote(
            share.at[(layer, src) + at],
            share.at[(layer, dst) + at],
            y_send.at[layer, n, q],
            y_recv.at[layer, n, q],
            t,
            chan,
        )

    def z_copy(layer, n, p):
        origin, target = ((0, 2), (0, -2), (0, 1), (0, -1), (-2, 1), (2, -1), (-2, 2), (2, -2))[n]
        at = (along_z(origin),) + ((pl.ds(n - 6, 1),) if n >= 6 and p == 0 else ())
        where = ring[layer][p].at[at]
        return remote(where, where, z_send.at[layer, p, n], z_recv.at[layer, p, n], z_peer(target), c)

    def far_copies(layer, p):
        return [z_copy(layer, n, p) for n in ((6, 7) if p == 0 else (7,))]

    def s_copy(layer, o, p, mine=True):
        where = ring[layer][p].at[along_z(o) if mine else along_z(o) + 1 - 2 * k]
        return remote(where, where, s_send.at[layer, p, o], s_recv.at[layer, p, o], sibling, c)

    def u_copy(layer, o, p):
        return remote(
            slots[p].at[layer, lax.rem(x + o, xs)],
            slots_x[layer][p].at[x],
            u_send.at[layer, p, o],
            u_recv.at[layer, p, o],
            x_peer(o),
            c,
        )

    def t_copy(o):
        return remote(table_own, table.at[x], t_send.at[o], t_recv.at[o], x_peer(o), c)

    def h_copy(layer, o, p):
        return remote(
            halo.at[layer, 0, halo_at[p]],
            halo.at[layer, PEERS - o, halo_at[p]],
            h_send.at[layer, p, o],
            h_recv.at[layer, p, o],
            t,
            lax.rem(c + o, PEERS),
        )

    def f_copy(o, p):
        return remote(
            fix.at[0, halo_at[p]],
            fix.at[PEERS - o, halo_at[p]],
            f_send.at[p, o],
            f_recv.at[p, o],
            t,
            lax.rem(c + o, PEERS),
        )

    grid[...] = jnp.zeros(grid.shape, bf16)
    sides_k[...] = jnp.zeros(sides_k.shape, f32)
    table_own[...] = jnp.zeros((8, LANES), jnp.int32)
    for n in range(4):
        copies[n].wait()
    table_own[0:1, 0:8] = nb[...] * 2 + fold[...]
    flat[0 : ch * nr] = state[0].astype(f32).reshape(ch * nr, LANES)
    flat[ch * nr : chp * nr] = jnp.zeros(((chp - ch) * nr, LANES), f32)

    def put_cols(r, row, sides):
        at = lax.broadcasted_iota(jnp.int32, row.shape, 1)
        return jnp.where((at == 2 * r + 3) | (at == 2 * r + 4), pltpu.roll(row, 2 * r + 4, 1), sides)

    def mask_row(r):
        return wet[0, pl.ds(r, 1), :].astype(f32)

    def load_chunk(q, carry):
        sides, wet_sides = carry
        for i in range(part):
            for h in range(2):
                r = 2 * (q * part + i) + h
                row_mask = mask_row(r)
                row = flat[pl.ds(r, chp, stride=nr), :] * row_mask
                row16 = row[0:ch].astype(bf16)
                share[0, 0, q * part + i, h] = row16
                grid[r + 1, 0:ch, :] = row16
                sides = put_cols(r, row, sides)
                wet_sides = put_cols(r, jnp.broadcast_to(row_mask, (8, LANES)), wet_sides)
        return sides, wet_sides

    def send_own(layer, q):
        for n in range(2):
            y_copy(layer, n, q).start()

    def send_ring(layer, p):
        for n in range(4):
            z_copy(layer, n, p).start()
        s_copy(layer, 0, p).start()

    sides, wet_sides = lax.fori_loop(
        0, CHUNKS, load_chunk, (jnp.zeros((chp, LANES), f32), jnp.zeros((8, LANES), f32))
    )
    mask_cols[...] = wet_sides
    sums_cols[...] = jnp.zeros((chp, LANES), f32)
    sums[0] = jnp.zeros((chp, LANES), f32)
    sums[nr - 1] = jnp.zeros((chp, LANES), f32)
    rows_0[me, 0] = share[0, 0, 0, 0]
    rows_0[me, 1] = share[0, 0, pairs - 1, 1]
    cols_0[me, 0] = sides[0:ch].astype(bf16)

    pl.semaphore_wait(barrier, PEERS - 1 + len(tiles))
    for p in range(2):
        send_ring(0, p)
    for q in range(CHUNKS):
        send_own(0, q)
    for o in range(1, xs):
        t_copy(o).start()

    k_in = lax.broadcasted_iota(jnp.int32, (PEERS * ch, depth), 0)
    k_at = lax.broadcasted_iota(jnp.int32, (PEERS * ch, depth), 1)
    place = jnp.zeros((PEERS * ch, depth), jnp.bool_)
    for j in range(PEERS):
        owner = lax.rem(c + j, PEERS)
        place = place | ((k_at - SLOT * j == k_in - ch * owner) & (k_at >= SLOT * j) & (k_at < SLOT * j + ch))
    place = jnp.where(place, 1.0, 0.0).astype(bf16)
    taps_f[...] = jnp.zeros(taps_f.shape, f32)
    for n in range(4, 8):
        copies[n].wait()
    for layer, w in enumerate((w1, w2)):
        for a in range(3):
            for b in range(3):
                taps_f[b * chp : b * chp + ch, a * depth : (a + 1) * depth] = jnp.dot(
                    w[3 * a + b], place, preferred_element_type=f32
                )
        taps[layer] = taps_f[...].astype(bf16)

    eye = lax.broadcasted_iota(jnp.int32, (chp, ch), 0) == lax.broadcasted_iota(jnp.int32, (chp, ch), 1)

    def bias_column(b):
        spread = jnp.broadcast_to(b[...], (chp, ch))
        return jnp.sum(jnp.where(eye, spread, 0.0), axis=1, keepdims=True)

    biases = bias_column(b1), bias_column(b2)
    flip = jnp.where(
        lax.broadcasted_iota(jnp.int32, (LANES, LANES), 0) + lax.broadcasted_iota(jnp.int32, (LANES, LANES), 1)
        == LANES - 1,
        1.0,
        0.0,
    ).astype(bf16)

    table[x] = table_own[...]
    for o in range(1, xs):
        t_copy(o).wait_recv()
    move = pltpu.make_async_copy(table, table_s, local_sem.at[8])
    move.start()
    move.wait()

    lane_ch = lax.broadcasted_iota(jnp.int32, (ch, LANES), 1)
    odd = (lane_ch & 1) == 1
    east = (~odd) & (lane_ch >= 4) & (lane_ch <= 2 * nr + 2)
    west = odd & (lane_ch >= 3) & (lane_ch <= 2 * nr + 1)

    def read_table(v):
        codes = [table_s[v, 0, n] for n in range(8)]
        return [code >> 1 for code in codes], [code & 1 for code in codes]

    def build_rows(layer, v):
        ids, folds = read_table(v)
        north, south = [lax.rem(jnp.maximum(q, 0), 2 * zs) for q in ids[0:2]]
        edges = ring[layer][0]
        slots_rows[layer, v, 0] = edges[south, 1]
        slots_rows[layer, v, 1] = jnp.where(folds[0] == 1, edges[north, 1], edges[north, 0])

    def build_cols(layer, v):
        ids, folds = read_table(v)
        at = [lax.rem(jnp.maximum(q, 0), 2 * zs) for q in ids]

        def cols(n):
            return ring[layer][1][at[n], 0].astype(f32)

        def corner_top(n, across):
            v = cols(n)
            return jnp.where(folds[n] == 1, pltpu.roll(v, across, 1), pltpu.roll(v, 2 * nr, 1))

        result = jnp.where(odd, cols(3), cols(2))
        result = jnp.where(lane_ch == 2 * nr + 4, corner_top(4, 3), result)
        result = jnp.where(lane_ch == 2 * nr + 3, corner_top(5, 1), result)
        result = jnp.where(lane_ch == 2, pltpu.roll(cols(6), LANES - 2 * nr, 1), result)
        result = jnp.where(lane_ch == 1, pltpu.roll(cols(7), LANES - 2 * nr, 1), result)
        slots_cols[layer, v, 0] = result.astype(bf16)

    def usable(code, value):
        return jnp.where(code >= 0, value, jnp.zeros_like(value))

    def merge_rows(layer):
        ids, folds = read_table(x)
        at = [jnp.maximum(q, 0) // (2 * zs) for q in ids[0:2]]
        edges = slots_x[layer][0]
        halo[layer, 0, 0] = usable(ids[1], edges[at[1], 0])
        north = edges[at[0], 1]
        turned = jnp.dot(north, flip, preferred_element_type=f32).astype(bf16)
        halo[layer, 0, 1] = usable(ids[0], jnp.where(folds[0] == 1, turned, north))

    def merge_cols(layer):
        ids, _ = read_table(x)

        def cols(n):
            return usable(ids[n], slots_x[layer][1][jnp.maximum(ids[n], 0) // (2 * zs), 0].astype(f32))

        result = jnp.where(east, cols(2), 0.0)
        result = jnp.where(west, cols(3), result)
        result = jnp.where(lane_ch == 2 * nr + 4, cols(4), result)
        result = jnp.where(lane_ch == 2 * nr + 3, cols(5), result)
        result = jnp.where(lane_ch == 2, cols(6), result)
        result = jnp.where(lane_ch == 1, cols(7), result)
        halo[layer, 0, 2] = result.astype(bf16)

    def gather(layer, q):
        for n in range(2):
            y_copy(layer, n, q).wait_recv()
            y_copy(layer, n + 2, q).start()

    def conv_rows(layer, columns):
        stacked = jnp.concatenate(
            [jnp.concatenate([column[a] for column in columns], axis=1) for a in range(3)], axis=0
        )
        return jnp.dot(taps[layer], stacked, preferred_element_type=f32)

    def add_columns(total):
        left = jnp.where(lane == 0, 0.0, pltpu.roll(total[0:chp], 1, 1))
        right = jnp.where(lane == LANES - 1, 0.0, pltpu.roll(total[2 * chp : 3 * chp], LANES - 1, 1))
        return total[chp : 2 * chp] + left + right

    def conv_chunk(layer, q, low, count):
        for n in range(2, 4):
            y_copy(layer, n, q).wait_recv()

        def pack(i, carry):
            for h in range(2):
                for j in range(layer == 0, PEERS):
                    row = share[layer, j, i, h]
                    if layer == 1:
                        ends = pltpu.roll(fix_f[j], LANES - 4 - 2 * (2 * i + h), 1)[0:ch].astype(bf16)
                        row = jnp.where((lane_ch == 0) | (lane_ch == LANES - 1), ends, row)
                    grid[1 + 2 * i + h, j * SLOT : j * SLOT + ch, :] = row
            return carry

        lax.fori_loop(q * part, (q + 1) * part, pack, 0)
        if layer == 1 and q in (0, CHUNKS - 1):
            for j in range(PEERS):
                grid[nr if q else 1, j * SLOT : j * SLOT + ch, :] = fix[j, 1 if q else 0]
        total = conv_rows(layer, [[grid[low + n + a] for a in range(3)] for n in range(count)])
        for n in range(count):
            sums[low + n] = add_columns(total[:, n * LANES : (n + 1) * LANES])

    def gelu(v):
        v = v + biases[0]
        return 0.5 * v * (1.0 + jnp.tanh(math.sqrt(2.0 / math.pi) * (v + 0.044715 * (v * v * v))))

    def hidden_inside(q):
        def one_part(i, carry):
            cols = sums_cols[...]
            for n in range(2):
                for h in range(2):
                    r = 2 * (2 * i + n) + h
                    row = sums[r]
                    share[1, 0, 2 * i + n, h] = (gelu(row) * mask_row(r))[0:ch].astype(bf16)
                    cols = put_cols(r, row, cols)
            sums_cols[...] = cols
            return carry

        lax.fori_loop(q * part // 2, (q + 1) * part // 2, one_part, 0)
        send_own(1, q)

    def layer_sums(layer):
        def near(p):
            z_copy(layer, 0, p).wait_recv()
            z_copy(layer, 4, p).start()
            if p == 0:
                z_copy(layer, 6, p).start()
            z_copy(layer, 1, p).wait_recv()
            z_copy(layer, 5, p).start()
            z_copy(layer, 7, p).start()
            s_copy(layer, zs - 2, p).start()
            s_copy(layer, 2, p).start()
            for n, o in ((2, zs - 1), (3, 1)):
                z_copy(layer, n, p).wait_recv()
                s_copy(layer, o, p).start()

        def far(p):
            for n, o in ((4, zs - 3), (5, 3)):
                z_copy(layer, n, p).wait_recv()
                s_copy(layer, o, p).start()
            for copy in far_copies(layer, p):
                copy.wait_recv()
            s_copy(layer, 4, p).start()

        def along_x(p):
            for o in range(zs):
                s_copy(layer, o, p, False).wait_recv()

            def one_slot(v, carry):
                (build_rows, build_cols)[p](layer, v)
                return carry

            lax.fori_loop(0, xs, one_slot, 0)
            for o in (2, 1, 3):
                u_copy(layer, o, p).start()
            slots_x[layer][p][x] = slots[p][layer, x]

        def along_y(p):
            for o in range(1, xs):
                u_copy(layer, o, p).wait_recv()
            (merge_rows, merge_cols)[p](layer)
            for o in (2, 1, 3):
                h_copy(layer, o, p).start()

        def fixes():
            for p in range(2):
                for o in range(1, PEERS):
                    f_copy(o, p).wait_recv()
            for j in range(PEERS):
                fix_f[j, 0:ch, :] = fix[j, 2].astype(f32)

        def conv(q):
            if q == 0:
                conv_chunk(layer, 0, 1, rows_of - 2)
            else:
                conv_chunk(layer, q, q * rows_of - 1, rows_of)

        if layer == 0:
            near(0)
            near(1)
            far(0)
            gather(layer, 0)
            far(1)
            along_x(0)
            gather(layer, 1)
            along_x(1)
            gather(layer, 2)
            along_y(0)
            gather(layer, 3)
            along_y(1)
            conv(0)
            for q in range(1, CHUNKS):
                conv(q)
                hidden_inside(q - 1)
            hidden_inside(CHUNKS - 1)
        else:
            gather(layer, 0)
            near(0)
            gather(layer, 1)
            near(1)
            far(0)
            gather(layer, 2)
            far(1)
            along_x(0)
            fixes()
            along_x(1)
            gather(layer, 3)
            conv(0)
            conv(1)
            along_y(0)
            along_y(1)
            conv(2)
            conv(3)
        for p in range(2):
            for o in range(1, PEERS):
                h_copy(layer, o, p).wait_recv()
        for j in range(PEERS):
            block = slice(j * SLOT, j * SLOT + ch)
            grid[0, block, :] = halo[layer, j, 0]
            grid[nr + 1, block, :] = halo[layer, j, 1]
            sides_k[block, :] = halo[layer, j, 2].astype(f32)
        frame = sides_k[...]
        column = [v.astype(bf16) for v in (pltpu.roll(frame, 2, 1), frame, pltpu.roll(frame, LANES - 2, 1))]
        total = conv_rows(layer, [[grid[r + a] for a in range(3)] for r in (0, nr - 1)] + [column])
        sums[0] = add_columns(total[:, 0:LANES])
        sums[nr - 1] = add_columns(total[:, LANES : 2 * LANES])
        return jnp.where((lane & 1) == 1, total[0:chp, 2 * LANES :], total[2 * chp : 3 * chp, 2 * LANES :])

    def turn(columns, r):
        return pltpu.roll(columns, 123 - 2 * r, 1)

    def full_row(r, below, this):
        return sums[r] + jnp.where(lane == 0, below, jnp.where(lane == LANES - 1, this, 0.0))

    columns_0 = layer_sums(0)

    cols = sums_cols[...]
    for n, r in enumerate((0, nr - 1)):
        row = full_row(r, turn(columns_0, r - 1), turn(columns_0, r))
        row16 = (gelu(row) * mask_row(r))[0:ch].astype(bf16)
        rows_1[me, n] = row16
        fix[0, n] = row16
        cols = put_cols(r, sums[r], cols)
    send_ring(1, 0)
    frame = jnp.where((lane & 1) == 1, pltpu.roll(columns_0, LANES - 1, 1), pltpu.roll(columns_0, 1, 1))
    cols16 = (gelu(cols + frame) * mask_cols[0:1, :])[0:ch].astype(bf16)
    cols_1[me, 0] = cols16
    fix[0, 2] = cols16
    send_ring(1, 1)
    for p in range(2):
        for o in range(1, PEERS):
            f_copy(o, p).start()

    columns_1 = layer_sums(1)

    def final_chunk(q, carry):
        below = turn(columns_1, q * rows_of - 1)
        for i in range(part):
            for h in range(2):
                r = 2 * (q * part + i) + h
                this = turn(columns_1, r)
                own = share[0, 0, q * part + i, h].astype(f32)
                v = own + (full_row(r, below, this) + biases[1])[0:ch]
                flat[pl.ds(r, ch, stride=nr), :] = v * mask_row(r)
                below = this
        return carry

    results = []
    for part_of in range(2):
        lax.fori_loop(part_of * CHUNKS // 2, (part_of + 1) * CHUNKS // 2, final_chunk, 0)
        low = part_of * nr // 2
        result[:, low : low + nr // 2, :] = flat[0 : ch * nr].reshape(ch, nr, LANES)[:, low : low + nr // 2].astype(bf16)
        rows = pl.ds(low, nr // 2)
        results.append(
            pltpu.make_async_copy(result.at[:, rows, :], out.at[0, :, rows, :], local_sem.at[9 + part_of])
        )
        results[-1].start()

    for copy in results:
        copy.wait()
    for o in range(1, xs):
        t_copy(o).wait_send()
    for p in range(2):
        for o in range(1, PEERS):
            f_copy(o, p).wait_send()
    for layer in range(2):
        for n in range(4):
            for q in range(CHUNKS):
                y_copy(layer, n, q).wait_send()
        for p in range(2):
            for n in range(6):
                z_copy(layer, n, p).wait_send()
            for copy in far_copies(layer, p):
                copy.wait_send()
            for o in range(zs):
                s_copy(layer, o, p).wait_send()
            for o in range(1, xs):
                u_copy(layer, o, p).wait_send()
            for o in range(1, PEERS):
                h_copy(layer, o, p).wait_send()


def build(mesh, xs, zs):
    def body(state, w1, b1, w2, b2, wet, nb, fold):
        ch, nr = state.shape[1], state.shape[2]
        chp = -(-ch // 8) * 8
        pairs = nr // 2
        f32, bf16 = jnp.float32, jnp.bfloat16
        vmem, dma = pltpu.VMEM, pltpu.SemaphoreType.DMA
        return pl.pallas_call(
            functools.partial(body_kernel, (xs, zs, ch, chp, nr)),
            out_shape=jax.ShapeDtypeStruct(state.shape, bf16),
            in_specs=[pl.BlockSpec(memory_space=pl.ANY)] * 8,
            out_specs=pl.BlockSpec(memory_space=pl.ANY),
            scratch_shapes=[
                vmem(state.shape, bf16),
                vmem((9, ch, PEERS * ch), bf16),
                vmem((1, ch), f32),
                vmem((9, ch, PEERS * ch), bf16),
                vmem((1, ch), f32),
                vmem(wet.shape, jnp.int32),
                vmem(nb.shape, jnp.int32),
                vmem(fold.shape, jnp.int32),
                vmem((chp * nr, LANES), f32),
                vmem((2, PEERS, pairs, 2, ch, LANES), bf16),
                vmem((nr + 2, PEERS * SLOT, LANES), bf16),
                vmem((PEERS * SLOT, LANES), f32),
                vmem((3 * chp, 3 * PEERS * SLOT), f32),
                vmem((2, 3 * chp, 3 * PEERS * SLOT), bf16),
                vmem((nr, chp, LANES), f32),
                vmem((2 * zs, 2, ch, LANES), bf16),
                vmem((2 * zs, 2, ch, LANES), bf16),
                vmem((2 * zs, 1, ch, LANES), bf16),
                vmem((2 * zs, 1, ch, LANES), bf16),
                vmem((2, xs, 2, ch, LANES), bf16),
                vmem((2, xs, 1, ch, LANES), bf16),
                vmem((xs, 2, ch, LANES), bf16),
                vmem((xs, 2, ch, LANES), bf16),
                vmem((xs, 1, ch, LANES), bf16),
                vmem((xs, 1, ch, LANES), bf16),
                vmem((2, PEERS, 3, ch, LANES), bf16),
                vmem((PEERS, 3, ch, LANES), bf16),
                vmem((PEERS, chp, LANES), f32),
                vmem((8, LANES), f32),
                vmem((chp, LANES), f32),
                vmem((ch, nr, LANES), bf16),
                vmem((8, LANES), jnp.int32),
                vmem((xs, 8, LANES), jnp.int32),
                pltpu.SMEM((xs, 8, LANES), jnp.int32),
                dma((2, 4, CHUNKS)),
                dma((2, 4, CHUNKS)),
                dma((2, 2, PEERS)),
                dma((2, 2, PEERS)),
                dma((2, PEERS)),
                dma((2, PEERS)),
                dma((2, 2, 8)),
                dma((2, 2, 8)),
                dma((2, 2, zs)),
                dma((2, 2, zs)),
                dma((2, 2, xs)),
                dma((2, 2, xs)),
                dma((xs,)),
                dma((xs,)),
                dma((11,)),
            ],
            compiler_params=pltpu.CompilerParams(
                collective_id=0, has_side_effects=True, vmem_limit_bytes=63 * 1024 * 1024
            ),
        )(
            state,
            jnp.swapaxes(w1, 1, 2),
            b1.reshape(1, -1),
            jnp.swapaxes(w2, 1, 2),
            b2.reshape(1, -1),
            wet,
            nb,
            fold,
        )

    return jax.shard_map(
        body,
        mesh=mesh,
        in_specs=(
            P("tiles", "chan", None, None),
            P(None, None, "chan"),
            P("chan"),
            P(None, None, "chan"),
            P("chan"),
            P("tiles", None, None),
            P("tiles", None),
            P("tiles", None),
        ),
        out_specs=P("tiles", "chan", None, None),
        check_vma=False,
    )


def solution(mesh):
    return build(mesh, X_SIZE, Z_SIZE)
```
